32 devices in a mesh: fsdp: 8 (over y, x, core), dp: 4 (over z).
Axes of the slice: x: 2, y: 2, z: 4, core: 2. Of those that a mesh axis runs over, the one named last changes fastest.
Arguments:
- candidate_layer_inputs: bfloat16 [128, 32, 8192], P(('dp', 'fsdp')), parts along dimension 0, may hold values from -8 to 8
- candidate_loss_cotangent: bfloat16 [128, 32, 1024], P(('dp', 'fsdp')), parts along dimension 0, may hold values from -8 to 8
- candidate_live_lengths: int32 [128], P(('dp', 'fsdp')), parts along dimension 0, may hold values from 4 to 32, as said below
- probe_layer_inputs: bfloat16 [128, 32, 8192], P(('dp', 'fsdp')), parts along dimension 0, may hold values from -8 to 8
- probe_loss_cotangent: bfloat16 [128, 32, 1024], P(('dp', 'fsdp')), parts along dimension 0, may hold values from -8 to 8
- probe_live_lengths: int32 [128], P(('dp', 'fsdp')), parts along dimension 0, may hold values from 4 to 32, as said below
- adapter_down_matrix: bfloat16 [8192, 128], P('fsdp'), may hold values from -0.0625 to 0.0625
- adapter_up_matrix: bfloat16 [1024, 128], P('fsdp'), may hold values from -0.5 to 0.5
- input_side_sketch: bfloat16 [8192, 256], P('fsdp'), may hold values from -0.0625 to 0.0625
- output_side_sketch: bfloat16 [1024, 256], P('fsdp'), may hold values from -0.1875 to 0.1875
- rank_sketch_down: bfloat16 [128, 16], replicated, may hold values from -0.5 to 0.5
- rank_sketch_up: bfloat16 [128, 16], replicated, may hold values from -0.5 to 0.5
Outputs:
- scores: float32 [128, 32], P(('dp', 'fsdp')), parts along dimension 0
- features: bfloat16 [128, 8192], P(('dp', 'fsdp')), parts along dimension 0
The draws below stay inside these ranges and needn't reach their ends.
There are 4 independent parts, one for each index of `dp`. The reference program is written for one: setup_inputs(seed, part) draws one part's arguments, and reference() takes and returns one part's arrays. A program takes and returns all parts, laid end to end along the dimension named above; an argument that names none is the same for every part. Nothing has to cross between parts.
Inputs may be any that keep to these rules, and one draw needn't show every extreme that they name: `candidate_live_lengths`: the live positions of an example are its first that many; some example has exactly 32 live positions and some exactly 4. `probe_live_lengths`: the live positions of an example are its first that many; some example has exactly 32 live positions and some exactly 4.
All inputs are finite; a program needn't handle non-finite values.
Results may differ from the reference program's by a relative error of at most 0.0056.
Values may be sent and summed in bfloat16 or wider, within the bound.
No kernel may reach another device: no remote copies, remote signals or barrier semaphores. Data moves between devices by JAX's collectives and lax.ppermute only.
A program may use at most 64 MiB of HBM per device.

```python
import jax
import jax.numpy as jnp
from jax import lax

MODEL_DIM = 8192
VALUE_WIDTH = 1024
ADAPTER_RANK = 128
KP = 256
KS = 16
SEQ = 32
TRAIN = 32
PROBES = 32


def activation_draw(key, salt, shared_salt, count, seq_len, model_width):
    shared_key = jax.random.fold_in(key, shared_salt)
    noise_key = jax.random.fold_in(key, salt)
    shared_row = 0.5 * jax.random.normal(shared_key, (model_width,), jnp.float32)
    noise = jax.random.normal(noise_key, (count, seq_len, model_width), jnp.float32)
    values = shared_row + noise
    return jnp.clip(values, -8.0, 8.0)


def length_draw(key, salt, count):
    base = jax.random.randint(jax.random.fold_in(key, salt), (count,), SEQ // 8, SEQ + 1)
    order = jax.random.permutation(jax.random.fold_in(key, salt + 1), count)
    base = base.at[order[0]].set(SEQ)
    base = base.at[order[1]].set(SEQ // 8)
    return base.astype(jnp.int32)


def draw_candidate_layer_inputs(key, part):
    return activation_draw(key, 11, 501, TRAIN, SEQ, MODEL_DIM).astype(jnp.bfloat16)


def draw_probe_layer_inputs(key, part):
    return activation_draw(key, 21, 501, PROBES, SEQ, MODEL_DIM).astype(jnp.bfloat16)


def draw_candidate_loss_cotangent(key, part):
    return activation_draw(key, 31, 502, TRAIN, SEQ, VALUE_WIDTH).astype(jnp.bfloat16)


def draw_probe_loss_cotangent(key, part):
    return activation_draw(key, 41, 502, PROBES, SEQ, VALUE_WIDTH).astype(jnp.bfloat16)


def draw_candidate_live_lengths(key, part):
    return length_draw(key, 61, TRAIN)


def draw_probe_live_lengths(key, part):
    return length_draw(key, 71, PROBES)


def level_of(key, extent, shards, smallest, high):
    def one(position, blocks):
        steps = jax.random.uniform(jax.random.fold_in(jax.random.fold_in(key, 6), position), (blocks,), jnp.float32, smallest / len(shards), high / len(shards))
        return jnp.repeat(jnp.exp(steps), extent[position] // blocks).reshape((-1,) + (1,) * (len(extent) - position - 1))

    gain = one(*shards[0])
    for cut in shards[1:]:
        gain = gain * one(*cut)
    return gain


def scatter_about(rng, shape, width, bound, shards=(), kind=jnp.bfloat16):
    gain = level_of(rng, shape, shards, -0.22, 0.18) if shards else 1.0
    values = jax.random.normal(rng, shape, jnp.float32) * width * gain
    return jnp.minimum(jnp.maximum(values, -bound), bound).astype(kind)


def setup_inputs(seed: int = 0, part: int = 0) -> dict:
    seeds = jax.random.split(jax.random.key(seed), 13)
    part_splits = jax.random.split(jax.random.fold_in(seeds[12], part), 13)
    candidate_layer_inputs = draw_candidate_layer_inputs(jax.random.fold_in(jax.random.fold_in(seeds[12], part), 71), part)
    candidate_loss_cotangent = draw_candidate_loss_cotangent(jax.random.fold_in(jax.random.fold_in(seeds[12], part), 71), part)
    candidate_live_lengths = draw_candidate_live_lengths(jax.random.fold_in(jax.random.fold_in(seeds[12], part), 71), part)
    probe_layer_inputs = draw_probe_layer_inputs(jax.random.fold_in(jax.random.fold_in(seeds[12], part), 71), part)
    probe_loss_cotangent = draw_probe_loss_cotangent(jax.random.fold_in(jax.random.fold_in(seeds[12], part), 71), part)
    probe_live_lengths = draw_probe_live_lengths(jax.random.fold_in(jax.random.fold_in(seeds[12], part), 71), part)
    adapter_down_matrix = scatter_about(seeds[6], (MODEL_DIM, ADAPTER_RANK), MODEL_DIM ** -0.5, 0.0625, ((0, 8),))
    adapter_up_matrix = scatter_about(seeds[7], (VALUE_WIDTH, ADAPTER_RANK), ADAPTER_RANK ** -0.5, 0.5, ((0, 8),))
    input_side_sketch = scatter_about(seeds[8], (MODEL_DIM, KP), MODEL_DIM ** -0.5, 0.0625, ((0, 8),))
    output_side_sketch = scatter_about(seeds[9], (VALUE_WIDTH, KP), VALUE_WIDTH ** -0.5, 0.1875, ((0, 8),))
    rank_sketch_down = scatter_about(seeds[10], (ADAPTER_RANK, KS), ADAPTER_RANK ** -0.5, 0.5)
    rank_sketch_up = scatter_about(seeds[11], (ADAPTER_RANK, KS), ADAPTER_RANK ** -0.5, 0.5)
    return {"candidate_layer_inputs": candidate_layer_inputs, "candidate_loss_cotangent": candidate_loss_cotangent, "candidate_live_lengths": candidate_live_lengths, "probe_layer_inputs": probe_layer_inputs, "probe_loss_cotangent": probe_loss_cotangent, "probe_live_lengths": probe_live_lengths, "adapter_down_matrix": adapter_down_matrix, "adapter_up_matrix": adapter_up_matrix, "input_side_sketch": input_side_sketch, "output_side_sketch": output_side_sketch, "rank_sketch_down": rank_sketch_down, "rank_sketch_up": rank_sketch_up}


eps_mean = 1e-06

def live_cotangent(loss_cotangent, example_lengths):
    positions = lax.broadcasted_iota(jnp.int32, loss_cotangent.shape[:2], 1)
    live_mask = (positions < example_lengths[:, None]).astype(loss_cotangent.dtype)
    return loss_cotangent * live_mask[:, :, None]

def compute_sketch_features(down_total_acc, inward_total_acc, loss_cotangent, example_lengths, adapter_up_matrix, output_side_sketch, rank_sketch_down, rank_sketch_up):
    examples = loss_cotangent.shape[0]
    seq_len = loss_cotangent.shape[1]
    kv_width = loss_cotangent.shape[2]
    masked_values = live_cotangent(loss_cotangent, example_lengths).reshape(examples * seq_len, kv_width)
    gradient_rowset = jnp.dot(masked_values, adapter_up_matrix, preferred_element_type=jnp.float32).astype(jnp.bfloat16)
    outward = jnp.dot(masked_values, output_side_sketch, preferred_element_type=jnp.float32).astype(jnp.bfloat16)
    down_round = down_total_acc.astype(jnp.bfloat16)
    inward_round = inward_total_acc.astype(jnp.bfloat16)
    left_small = jnp.dot(gradient_rowset, rank_sketch_down, preferred_element_type=jnp.float32).astype(jnp.bfloat16)
    right_small = jnp.dot(down_round, rank_sketch_up, preferred_element_type=jnp.float32).astype(jnp.bfloat16)
    small_cols = rank_sketch_down.shape[1]
    large_cols = inward_round.shape[1]
    grad_left = jnp.einsum('esk,esp->ekp', left_small.reshape(examples, seq_len, small_cols).astype(jnp.float32), inward_round.reshape(examples, seq_len, large_cols).astype(jnp.float32), precision=lax.Precision.HIGHEST)
    grad_right = jnp.einsum('esk,esp->ekp', right_small.reshape(examples, seq_len, small_cols).astype(jnp.float32), outward.reshape(examples, seq_len, large_cols).astype(jnp.float32), precision=lax.Precision.HIGHEST)
    joined = jnp.concatenate([grad_left, grad_right], axis=1).reshape(examples, 2 * small_cols * large_cols)
    inv_rms = lax.rsqrt(lax.optimization_barrier(jnp.mean(joined * joined, axis=1, keepdims=True)) + eps_mean)
    return (joined * inv_rms).astype(jnp.bfloat16)

def reference(candidate_layer_inputs, candidate_loss_cotangent, candidate_live_lengths, probe_layer_inputs, probe_loss_cotangent, probe_live_lengths, adapter_down_matrix, adapter_up_matrix, input_side_sketch, output_side_sketch, rank_sketch_down, rank_sketch_up):

    def one_side(inputs, loss_cotangent, example_lengths):
        model_width = inputs.shape[2]
        flattened_rowset = inputs.reshape(-1, model_width)
        down_total_acc = jnp.dot(flattened_rowset, adapter_down_matrix, preferred_element_type=jnp.float32)
        inward_total_acc = jnp.dot(flattened_rowset, input_side_sketch, preferred_element_type=jnp.float32)
        return compute_sketch_features(down_total_acc, inward_total_acc, loss_cotangent, example_lengths, adapter_up_matrix, output_side_sketch, rank_sketch_down, rank_sketch_up)
    features = one_side(candidate_layer_inputs, candidate_loss_cotangent, candidate_live_lengths)
    probe_features = one_side(probe_layer_inputs, probe_loss_cotangent, probe_live_lengths)
    scores = jnp.dot(features, probe_features.T, preferred_element_type=jnp.float32) / features.shape[1]
    return (scores, features)
```

```python
import functools

import jax
import jax.numpy as jnp
from jax import lax
from jax.experimental import pallas as pl
from jax.experimental.pallas import tpu as pltpu
from jax.sharding import PartitionSpec as P

eps_mean = 1e-06
LAST = (((1,), (1,)), ((), ()))
VMEM = pl.BlockSpec(memory_space=pltpu.VMEM)
SMEM = pl.BlockSpec(memory_space=pltpu.SMEM)
MIB = 1 << 20


def dot(a, b):
    return jnp.dot(a, b, preferred_element_type=jnp.float32)


def dot_last(a, b):
    return lax.dot_general(a, b, LAST, preferred_element_type=jnp.float32)


def split_two(x):
    high = x.astype(jnp.bfloat16)
    return high, (x - high.astype(jnp.float32)).astype(jnp.bfloat16)


def fold_kernel(down_ref, up_ref, rank_down_ref, rank_up_ref, out_ref):
    first = (((0,), (1,)), ((), ()))
    rows = down_ref.shape[0]
    out_ref[:, :rows] = lax.dot_general(
        rank_up_ref[...], down_ref[...], first, preferred_element_type=jnp.float32
    ).astype(jnp.bfloat16)
    out_ref[:, rows:] = lax.dot_general(
        rank_down_ref[...], up_ref[...], first, preferred_element_type=jnp.float32
    ).astype(jnp.bfloat16)


def spread(small, lengths_ref, seq):
    ks, width = small.shape
    count = width // seq
    rows = lax.broadcasted_iota(jnp.int32, (count * ks, width), 0)
    cols = lax.broadcasted_iota(jnp.int32, (count * ks, width), 1)
    live = jnp.zeros((count * ks, width), jnp.bool_)
    for e in range(count):
        start = e * seq
        live = live | (
            (rows >= e * ks)
            & (rows < (e + 1) * ks)
            & (cols >= start)
            & (cols < start + lengths_ref[e])
        )
    tiled = jnp.concatenate([small] * count, axis=0)
    return jnp.where(live, tiled, 0.0).astype(jnp.bfloat16)


def rows_kernel(
    order, seq, halves,
    c_x, c_m, c_len, p_x, p_m, p_len, t_same, t_other,
    left_ref, right_ref,
):
    me = lax.axis_index("fsdp")
    ks = t_same.shape[0] * 2 // len(order)
    n = len(order)
    model, value = c_x.shape[1], c_m.shape[1]
    kd, ku = model // n, value // n
    sides = ((c_x, c_m, c_len), (p_x, p_m, p_len))
    tables = [
        (t_same if g < n // 2 else t_other)[(g % (n // 2)) * ks : (g % (n // 2) + 1) * ks, :]
        for g in range(n)
    ]
    part = ku // halves
    total = 2 * left_ref.shape[0] // 4
    for side, (x, m, lengths) in enumerate(sides):
        left_small = 0.0
        right_small = 0.0
        for g, k in enumerate(order):
            j = me ^ k
            left_small += dot_last(tables[g][:, kd:], m[:, pl.ds(pl.multiple_of(j * ku, ku), ku)])
        for g, k in enumerate(order):
            j = me ^ k
            right_small += dot_last(tables[g][:, :kd], x[:, pl.ds(pl.multiple_of(j * kd, kd), kd)])
        left_wide = spread(left_small.astype(jnp.bfloat16).astype(jnp.float32), lengths, seq)
        right_wide = spread(right_small.astype(jnp.bfloat16).astype(jnp.float32), lengths, seq)
        rows = left_wide.shape[0]
        at = side * rows
        for b in range(n):
            high, low = split_two(dot(left_wide, x[:, b * kd : (b + 1) * kd]))
            left_ref[at : at + rows, b * kd : (b + 1) * kd] = high
            left_ref[total + at : total + at + rows, b * kd : (b + 1) * kd] = low
        high, low = split_two(dot(right_wide, m[...]))
        for b in range(n * halves):
            right_ref[b, at : at + rows, :] = high[:, b * part : (b + 1) * part]
            right_ref[b, total + at : total + at + rows, :] = low[:, b * part : (b + 1) * part]


def join_kernel(keys, ks, s_rows, left_ref, right_ref, *refs):
    pieces, (c_out, p_out, left_scratch, right_scratch) = refs[: len(keys)], refs[len(keys) :]
    me = lax.axis_index("fsdp")
    halves = 1 + max(h for _, h in keys)
    left = 0.0
    right = 0.0
    for (k, h), piece in zip(keys, pieces):
        at = (me ^ k) * halves + h
        left += dot(left_ref[:, pl.ds(pl.multiple_of(at * s_rows, s_rows), s_rows)], piece[:s_rows, :])
        right += dot(right_ref[at], piece[s_rows:, :])
    total = left.shape[0] // 2
    left = left[:total] + left[total:]
    right = right[:total] + right[total:]
    count, cols = total // ks, left.shape[1]
    left = left.reshape(count, ks, cols)
    right = right.reshape(count, ks, cols)
    mean = jnp.sum(left * left + right * right, axis=(1, 2), keepdims=True) / (2 * ks * cols)
    scale = lax.rsqrt(mean + eps_mean)
    lanes = left_scratch.shape[2]
    for scratch, value in ((left_scratch, left), (right_scratch, right)):
        scaled = (value * scale).reshape(total, cols)
        for b in range(cols // lanes):
            scratch[b] = scaled[:, b * lanes : (b + 1) * lanes]
    half = count // 2
    for side, out in enumerate((c_out, p_out)):
        for t, scratch in enumerate((left_scratch, right_scratch)):
            for r in range(ks):
                for b in range(cols // lanes):
                    at = (t * ks + r) * cols + b * lanes
                    rows = pl.ds(side * half * ks + r, half, stride=ks)
                    out[:, at : at + lanes] = scratch[b, rows, :].astype(jnp.bfloat16)


def score_kernel(order, c_ref, same_ref, other_ref, out_ref):
    me = lax.axis_index("fsdp")
    feats = c_ref[...]
    mixed = jnp.concatenate([dot_last(feats, same_ref[...]), dot_last(feats, other_ref[...])], axis=1)
    width = mixed.shape[1]
    per = width // len(order)
    rows = lax.broadcasted_iota(jnp.int32, (width, width), 0)
    cols = lax.broadcasted_iota(jnp.int32, (width, width), 1)
    target = jnp.zeros((width, width), jnp.int32)
    for g, k in enumerate(order):
        target = jnp.where(rows // per == g, (me ^ k) * per + rows % per, target)
    place = (target == cols).astype(jnp.float32)
    out = lax.dot_general(
        mixed, place, (((1,), (0,)), ((), ())),
        preferred_element_type=jnp.float32, precision=lax.Precision.HIGHEST,
    )
    out_ref[...] = out / feats.shape[1]


def swap(x, k, axis, size):
    return lax.ppermute(x, axis, [(i, i ^ k) for i in range(size)])


def fast_body(n, c_x, c_m, c_len, p_x, p_m, p_len, down, up, sketch_in, sketch_out, rank_down, rank_up):
    examples, seq, model = c_x.shape
    value = c_m.shape[2]
    ks, kp = rank_down.shape[1], sketch_in.shape[1]
    s_shard, o_shard = sketch_in.shape[0], sketch_out.shape[0]
    sw = functools.partial(swap, axis="fsdp", size=n)
    order = (0, 2, 4, 6, 1, 3, 5, 7)
    halves = 2
    s_rows, o_rows = s_shard // halves, o_shard // halves

    h0, h1 = (
        jnp.concatenate(
            [sketch_in[h * s_rows : (h + 1) * s_rows], sketch_out[h * o_rows : (h + 1) * o_rows]]
        )
        for h in range(halves)
    )
    x0, y1 = sw(h0, 2), sw(h1, 4)

    table = pl.pallas_call(
        fold_kernel,
        out_shape=jax.ShapeDtypeStruct((ks, down.shape[0] + up.shape[0]), jnp.bfloat16),
        in_specs=[VMEM] * 4,
        out_specs=VMEM,
        compiler_params=pltpu.CompilerParams(vmem_limit_bytes=4 * MIB),
        name="fold_ranks",
    )(down, up, rank_down, rank_up)
    t_same = jnp.concatenate([table, sw(table, 2), sw(table, 4), sw(table, 6)])
    t_other = sw(t_same, 1)

    x1, y0 = sw(h1, 2), sw(h0, 4)
    d0, d1 = sw(x0, 4), sw(y1, 2)
    pieces = {(0, 0): h0, (0, 1): h1, (2, 0): x0, (2, 1): x1, (4, 0): y0, (4, 1): y1, (6, 0): d0, (6, 1): d1}
    for (k, h), piece in list(pieces.items()):
        pieces[(k ^ 1, h)] = sw(piece, 1)

    flat = (examples * seq, model)
    flat_m = (examples * seq, value)
    total = 2 * examples * ks
    left, right = pl.pallas_call(
        functools.partial(rows_kernel, order, seq, halves),
        out_shape=(
            jax.ShapeDtypeStruct((2 * total, model), jnp.bfloat16),
            jax.ShapeDtypeStruct((n * halves, 2 * total, o_rows), jnp.bfloat16),
        ),
        in_specs=[VMEM, VMEM, SMEM, VMEM, VMEM, SMEM, VMEM, VMEM],
        out_specs=(VMEM, VMEM),
        compiler_params=pltpu.CompilerParams(vmem_limit_bytes=24 * MIB),
        name="example_rows",
    )(
        c_x.reshape(flat), c_m.reshape(flat_m), c_len, p_x.reshape(flat), p_m.reshape(flat_m), p_len, t_same, t_other
    )

    keys = tuple(sorted(pieces))
    feats = jax.ShapeDtypeStruct((examples, 2 * ks * kp), jnp.bfloat16)
    c_feat, p_feat = pl.pallas_call(
        functools.partial(join_kernel, keys, ks, s_rows),
        out_shape=(feats, feats),
        in_specs=[VMEM] * (2 + len(keys)),
        out_specs=(VMEM, VMEM),
        scratch_shapes=[pltpu.VMEM((kp // 128, total, 128), jnp.float32)] * 2,
        compiler_params=pltpu.CompilerParams(vmem_limit_bytes=24 * MIB),
        name="join_features",
    )(left, right, *(pieces[key] for key in keys))

    same = jnp.concatenate([p_feat, sw(p_feat, 2), sw(p_feat, 4), sw(p_feat, 6)])
    other = sw(same, 1)
    scores = pl.pallas_call(
        functools.partial(score_kernel, order),
        out_shape=jax.ShapeDtypeStruct((examples, n * examples), jnp.float32),
        in_specs=[VMEM] * 3,
        out_specs=VMEM,
        compiler_params=pltpu.CompilerParams(vmem_limit_bytes=8 * MIB),
        name="score_rows",
    )(c_feat, same, other)
    return scores, c_feat


def plain_features(x, m, lengths, down, up, sketch_in, sketch_out, rank_down, rank_up):
    examples, seq, model = x.shape
    ks, kp = rank_down.shape[1], sketch_in.shape[1]
    live = (lax.broadcasted_iota(jnp.int32, (examples, seq), 1) < lengths[:, None]).astype(m.dtype)
    masked = (m * live[:, :, None]).reshape(examples * seq, -1)
    rows = x.reshape(examples * seq, model)
    grad_rows = dot(masked, up).astype(jnp.bfloat16)
    outward = dot(masked, sketch_out).astype(jnp.bfloat16)
    down_round = dot(rows, down).astype(jnp.bfloat16)
    inward = dot(rows, sketch_in).astype(jnp.bfloat16)
    left_small = dot(grad_rows, rank_down).astype(jnp.bfloat16)
    right_small = dot(down_round, rank_up).astype(jnp.bfloat16)

    def outer(small, wide):
        return jnp.einsum(
            "esk,esp->ekp",
            small.reshape(examples, seq, ks),
            wide.reshape(examples, seq, kp),
            preferred_element_type=jnp.float32,
        )

    joined = jnp.concatenate([outer(left_small, inward), outer(right_small, outward)], axis=1)
    joined = joined.reshape(examples, 2 * ks * kp)
    scale = lax.rsqrt(jnp.mean(joined * joined, axis=1, keepdims=True) + eps_mean)
    return (joined * scale).astype(jnp.bfloat16)


def plain_body(c_x, c_m, c_len, p_x, p_m, p_len, down, up, sketch_in, sketch_out, rank_down, rank_up):
    weights = [
        lax.all_gather(w, "fsdp", axis=0, tiled=True) for w in (down, up, sketch_in, sketch_out)
    ]
    p_feat = plain_features(p_x, p_m, p_len, *weights, rank_down, rank_up)
    c_feat = plain_features(c_x, c_m, c_len, *weights, rank_down, rank_up)
    every = lax.all_gather(p_feat, "fsdp", axis=0, tiled=True)
    return dot(c_feat, every.T) / c_feat.shape[1], c_feat


def solution(mesh):
    n = mesh.shape["fsdp"]
    rows = P(("dp", "fsdp"), None)
    cube = P(("dp", "fsdp"), None, None)
    line = P(("dp", "fsdp"))
    shard = P("fsdp", None)
    in_specs = (cube, cube, line, cube, cube, line, shard, shard, shard, shard, P(), P())

    def body(*args):
        if n == 1 << 3:
            return fast_body(n, *args)
        return plain_body(*args)

    return jax.shard_map(body, mesh=mesh, in_specs=in_specs, out_specs=(rows, rows), check_vma=False)
```

```python
import functools

import jax
import jax.numpy as jnp
from jax import lax
from jax.experimental import pallas as pl
from jax.experimental.pallas import tpu as pltpu
from jax.sharding import PartitionSpec as P

eps_mean = 1e-06
LAST = (((1,), (1,)), ((), ()))
VMEM = pl.BlockSpec(memory_space=pltpu.VMEM)
SMEM = pl.BlockSpec(memory_space=pltpu.SMEM)
HBM = pl.BlockSpec(memory_space=pltpu.HBM)
MIB = 1 << 20


def in_hbm(*arrays):
    return tuple(pltpu.with_memory_space_constraint(a, pltpu.HBM) for a in arrays)


def dot(a, b):
    return jnp.dot(a, b, preferred_element_type=jnp.float32)


def dot_last(a, b):
    return lax.dot_general(a, b, LAST, preferred_element_type=jnp.float32)


def split_two(x):
    high = x.astype(jnp.bfloat16)
    return high, (x - high.astype(jnp.float32)).astype(jnp.bfloat16)


def partner(me, kind, other):
    odd = (me % 2) ^ other
    return me ^ other ^ (0, 2 + 2 * odd, 4 - 2 * odd, 6)[kind]


def pack_kernel(
    halves, down_hbm, up_hbm, rank_down_hbm, rank_up_hbm, in_hbm, out_hbm, *refs
):
    packed, own_ref, (down_ref, up_ref, rank_down_ref, rank_up_ref, sems) = (
        refs[:halves], refs[halves], refs[halves + 1 :],
    )
    s_rows, o_rows = in_hbm.shape[0] // halves, out_hbm.shape[0] // halves
    moves = [
        (down_hbm, down_ref),
        (up_hbm, up_ref),
        (rank_down_hbm, rank_down_ref),
        (rank_up_hbm, rank_up_ref),
    ]
    for h, piece in enumerate(packed):
        for to, at in ((piece, 0), (own_ref, h * (s_rows + o_rows))):
            moves.append((in_hbm.at[pl.ds(h * s_rows, s_rows)], to.at[pl.ds(at, s_rows)]))
            moves.append((out_hbm.at[pl.ds(h * o_rows, o_rows)], to.at[pl.ds(at + s_rows, o_rows)]))
    copies = [pltpu.make_async_copy(a, b, sems.at[i]) for i, (a, b) in enumerate(moves)]
    for copy in copies:
        copy.start()
    for copy in copies[:4]:
        copy.wait()
    down_table = dot_last(rank_up_ref[...], down_ref[...]).astype(jnp.bfloat16)
    up_table = dot_last(rank_down_ref[...], up_ref[...]).astype(jnp.bfloat16)
    ks, width = up_table.shape
    lanes = own_ref.shape[1]
    blocks = down_table.shape[1] // lanes
    at = s_rows + o_rows
    for piece in packed:
        for b in range(blocks):
            piece[at + b * ks : at + (b + 1) * ks, :] = down_table[:, b * lanes : (b + 1) * lanes]
        piece[at + blocks * ks : at + (blocks + 1) * ks, :] = jnp.zeros((ks, lanes), jnp.bfloat16)
        piece[at + blocks * ks : at + (blocks + 1) * ks, :width] = up_table
    for copy in copies[4:]:
        copy.wait()


def load_kernel(
    seq, ks, c_x_hbm, c_m_hbm, c_len_hbm, p_x_hbm, p_m_hbm, p_len_hbm,
    x_ref, m_ref, live_ref, c_len, p_len, sems,
):
    rows = c_x_hbm.shape[0]
    moves = (
        (c_len_hbm, c_len), (p_len_hbm, p_len),
        (c_m_hbm, m_ref.at[pl.ds(0, rows)]), (p_m_hbm, m_ref.at[pl.ds(rows, rows)]),
        (c_x_hbm, x_ref.at[pl.ds(0, rows)]), (p_x_hbm, x_ref.at[pl.ds(rows, rows)]),
    )
    copies = [pltpu.make_async_copy(a, b, sems.at[i]) for i, (a, b) in enumerate(moves)]
    for copy in copies:
        copy.start()
    for copy in copies[:2]:
        copy.wait()
    height, width = live_ref.shape
    rows = lax.broadcasted_iota(jnp.int32, (height, width), 0)
    cols = lax.broadcasted_iota(jnp.int32, (height, width), 1)
    live = jnp.zeros((height, width), jnp.bool_)
    count = width // ks
    for e in range(count):
        length = c_len[e] if e < count // 2 else p_len[e - count // 2]
        live = live | (
            (cols >= e * ks)
            & (cols < (e + 1) * ks)
            & (rows >= e * seq)
            & (rows < e * seq + length)
        )
    live_ref[...] = live.astype(jnp.float32)
    for copy in copies[2:]:
        copy.wait()


def rows_kernel(n, halves, x, m, live_ref, t_same, t_other, left_ref, right_ref):
    me = lax.axis_index("fsdp")
    model, value = x.shape[1], m.shape[1]
    kd, ku = model // n, value // n
    lanes = t_same.shape[1]
    blocks = kd // lanes
    ks = t_same.shape[0] // (n // 2) // (blocks + 1)
    held = [
        (partner(me, kind, other), (t_same, t_other)[other], kind * (blocks + 1) * ks)
        for other in range(2)
        for kind in range(n // 2)
    ]
    part = ku // halves
    total = left_ref.shape[0] // 2

    def spread(small):
        small = small.astype(jnp.bfloat16).astype(jnp.float32)
        wide = jnp.concatenate([small] * (live_ref.shape[1] // ks), axis=1)
        return jnp.where(live_ref[...] > 0, wide, 0.0).T.astype(jnp.bfloat16)

    left_small = 0.0
    right_small = 0.0
    for j, table, at in held:
        up = table[at + blocks * ks : at + (blocks + 1) * ks, :ku]
        left_small += dot_last(m[:, pl.ds(pl.multiple_of(j * ku, ku), ku)], up)
    left_wide = spread(left_small)
    for j, table, at in held:
        for b in range(blocks):
            cols = pl.ds(pl.multiple_of(j * kd + b * lanes, lanes), lanes)
            right_small += dot_last(x[:, cols], table[at + b * ks : at + (b + 1) * ks, :])
    for b in range(n):
        high, low = split_two(dot(left_wide, x[:, b * kd : (b + 1) * kd]))
        left_ref[:total, b * kd : (b + 1) * kd] = high
        left_ref[total:, b * kd : (b + 1) * kd] = low
    high, low = split_two(dot(spread(right_small), m[...]))
    for b in range(n * halves):
        right_ref[b, :total, :] = high[:, b * part : (b + 1) * part]
        right_ref[b, total:, :] = low[:, b * part : (b + 1) * part]


def products(places, s_rows, halves, left_ref, right_ref, refs):
    me = lax.axis_index("fsdp")
    o_rows = right_ref.shape[2]
    left = 0.0
    right = 0.0
    for ref, row, kind, other, half in places:
        at = partner(me, kind, other) * halves + half
        cols = pl.ds(pl.multiple_of(at * s_rows, s_rows), s_rows)
        left += dot(left_ref[:, cols], refs[ref][row : row + s_rows, :])
        right += dot(right_ref[at], refs[ref][row + s_rows : row + s_rows + o_rows, :])
    total = left.shape[0] // 2
    return left[:total] + left[total:], right[:total] + right[total:]


def early_kernel(places, s_rows, halves, left_ref, right_ref, *refs):
    left, right = products(places, s_rows, halves, left_ref, right_ref, refs[:-1])
    refs[-1][0] = left
    refs[-1][1] = right


def join_kernel(places, ks, s_rows, halves, left_ref, right_ref, sums_ref, *refs):
    refs, (c_out, c_keep, p_out, left_scratch, right_scratch) = refs[:-5], refs[-5:]
    left, right = products(places, s_rows, halves, left_ref, right_ref, refs)
    left += sums_ref[0]
    right += sums_ref[1]
    total = left.shape[0]
    count, cols = total // ks, left.shape[1]
    left = left.reshape(count, ks, cols)
    right = right.reshape(count, ks, cols)
    mean = jnp.sum(left * left + right * right, axis=(1, 2), keepdims=True) / (2 * ks * cols)
    scale = lax.rsqrt(mean + eps_mean)
    lanes = left_scratch.shape[2]
    for scratch, value in ((left_scratch, left), (right_scratch, right)):
        scaled = (value * scale).reshape(total, cols)
        for b in range(cols // lanes):
            scratch[b] = scaled[:, b * lanes : (b + 1) * lanes]
    half = count // 2
    for side, outs in enumerate(((c_out, c_keep), (p_out,))):
        for t, scratch in enumerate((left_scratch, right_scratch)):
            for r in range(ks):
                for b in range(cols // lanes):
                    at = (t * ks + r) * cols + b * lanes
                    rows = pl.ds(side * half * ks + r, half, stride=ks)
                    value = scratch[b, rows, :].astype(jnp.bfloat16)
                    for out in outs:
                        out[:, at : at + lanes] = value


def score_kernel(order, c_ref, same_ref, other_ref, out_ref):
    me = lax.axis_index("fsdp")
    feats = c_ref[...]
    mixed = jnp.concatenate([dot_last(feats, same_ref[...]), dot_last(feats, other_ref[...])], axis=1)
    width = mixed.shape[1]
    per = width // len(order)
    rows = lax.broadcasted_iota(jnp.int32, (width, width), 0)
    cols = lax.broadcasted_iota(jnp.int32, (width, width), 1)
    target = jnp.zeros((width, width), jnp.int32)
    for g, k in enumerate(order):
        target = jnp.where(rows // per == g, (me ^ k) * per + rows % per, target)
    place = (target == cols).astype(jnp.float32)
    out = lax.dot_general(
        mixed, place, (((1,), (0,)), ((), ())),
        preferred_element_type=jnp.float32, precision=lax.Precision.HIGHEST,
    )
    out_ref[...] = out / feats.shape[1]


def swap(x, k, axis, size):
    return lax.ppermute(x, axis, [(i, i ^ k) for i in range(size)])


def fast_body(n, c_x, c_m, c_len, p_x, p_m, p_len, down, up, sketch_in, sketch_out, rank_down, rank_up):
    examples, seq, model = c_x.shape
    value = c_m.shape[2]
    ks, kp = rank_down.shape[1], sketch_in.shape[1]
    s_shard, o_shard = sketch_in.shape[0], sketch_out.shape[0]
    sw = functools.partial(swap, axis="fsdp", size=n)
    order = (0, 2, 4, 6, 1, 3, 5, 7)
    halves = 2
    s_rows, o_rows = s_shard // halves, o_shard // halves

    def along(x, first, second):
        return lax.ppermute(x, "fsdp", [(i, i ^ (second if i % 2 else first)) for i in range(n)])

    along_u = functools.partial(along, first=2, second=4)
    along_v = functools.partial(along, first=4, second=2)
    half = s_rows + o_rows
    t_rows = (s_shard // kp + 1) * ks

    def array(rows, like=sketch_in):
        return jax.ShapeDtypeStruct((rows, like.shape[1]), like.dtype)

    h0, h1, own = pl.pallas_call(
        functools.partial(pack_kernel, halves),
        out_shape=(array(half + t_rows), array(half + t_rows), array(2 * half)),
        in_specs=[HBM] * 6,
        out_specs=(VMEM,) * 3,
        scratch_shapes=[
            pltpu.VMEM(down.shape, down.dtype),
            pltpu.VMEM(up.shape, up.dtype),
            pltpu.VMEM(rank_down.shape[::-1], rank_down.dtype),
            pltpu.VMEM(rank_up.shape[::-1], rank_up.dtype),
            pltpu.SemaphoreType.DMA((4 + 4 * halves,)),
        ],
        compiler_params=pltpu.CompilerParams(vmem_limit_bytes=8 * MIB),
        name="pack_weights",
    )(*in_hbm(down, up, rank_down.T, rank_up.T, sketch_in, sketch_out))

    flat = (examples * seq, model)
    flat_m = (examples * seq, value)
    total = 2 * examples * ks
    rows = pl.pallas_call(
        functools.partial(load_kernel, seq, ks),
        out_shape=(
            jax.ShapeDtypeStruct((2 * examples * seq, model), c_x.dtype),
            jax.ShapeDtypeStruct((2 * examples * seq, value), c_m.dtype),
            jax.ShapeDtypeStruct((2 * examples * seq, total), jnp.float32),
        ),
        in_specs=[HBM] * 6,
        out_specs=(VMEM,) * 3,
        scratch_shapes=[
            pltpu.SMEM(c_len.shape, c_len.dtype),
            pltpu.SMEM(p_len.shape, p_len.dtype),
            pltpu.SemaphoreType.DMA((6,)),
        ],
        compiler_params=pltpu.CompilerParams(vmem_limit_bytes=8 * MIB),
        name="load_rows",
    )(*in_hbm(c_x.reshape(flat), c_m.reshape(flat_m), c_len, p_x.reshape(flat), p_m.reshape(flat_m), p_len))

    u0, v1 = along_u(h0), along_v(h1)
    c_own = sw(own, 1)
    u1, v0 = along_u(h1[:half]), along_v(h0[:half])
    u0, v1, c_own, rows = lax.optimization_barrier((u0, v1, c_own, rows))
    t_d = along_v(u0[half:])
    d0, d1 = along_v(u0[:half]), along_u(v1[:half])
    t_same = jnp.concatenate([h0[half:], u0[half:], v1[half:], t_d])
    t_other = sw(t_same, 1)
    u0, v1 = u0[:half], v1[:half]
    t_same, u1, v0 = lax.optimization_barrier((t_same, u1, v0))
    c_uv = sw(jnp.concatenate([u0, u1, v0, v1]), 1)

    left, right = pl.pallas_call(
        functools.partial(rows_kernel, n, halves),
        out_shape=(
            jax.ShapeDtypeStruct((2 * total, model), jnp.bfloat16),
            jax.ShapeDtypeStruct((n * halves, 2 * total, o_rows), jnp.bfloat16),
        ),
        in_specs=[VMEM] * 5,
        out_specs=(VMEM, VMEM),
        compiler_params=pltpu.CompilerParams(vmem_limit_bytes=16 * MIB),
        name="example_rows",
    )(*rows, t_same, t_other)

    early = (
        (0, 0, 0, 0, 0), (1, 0, 0, 0, 1), (2, 0, 0, 1, 0), (2, half, 0, 1, 1),
        (3, 0, 1, 0, 0), (4, 0, 1, 0, 1), (5, 0, 2, 0, 0), (6, 0, 2, 0, 1),
        (7, 0, 1, 1, 0), (7, half, 1, 1, 1), (7, 2 * half, 2, 1, 0), (7, 3 * half, 2, 1, 1),
    )
    sums = pl.pallas_call(
        functools.partial(early_kernel, early, s_rows, halves),
        out_shape=jax.ShapeDtypeStruct((2, total, kp), jnp.float32),
        in_specs=[VMEM] * 10,
        out_specs=VMEM,
        compiler_params=pltpu.CompilerParams(vmem_limit_bytes=16 * MIB),
        name="early_products",
    )(left, right, h0, h1, c_own, u0, u1, v0, v1, c_uv)

    sums, d0, d1 = lax.optimization_barrier((sums, d0, d1))
    late = ((0, 0, 3, 0, 0), (1, 0, 3, 0, 1), (2, 0, 3, 1, 0), (3, 0, 3, 1, 1))
    feats = jax.ShapeDtypeStruct((examples, 2 * ks * kp), jnp.bfloat16)
    c_feat, c_keep, p_feat = pl.pallas_call(
        functools.partial(join_kernel, late, ks, s_rows, halves),
        out_shape=(feats, feats, feats),
        in_specs=[VMEM] * 7,
        out_specs=(VMEM, VMEM, VMEM),
        scratch_shapes=[pltpu.VMEM((kp // 128, total, 128), jnp.float32)] * 2,
        compiler_params=pltpu.CompilerParams(vmem_limit_bytes=16 * MIB),
        name="join_features",
    )(left, right, sums, d0, d1, sw(d0, 1), sw(d1, 1))

    same = jnp.concatenate([p_feat, sw(p_feat, 2), sw(p_feat, 4), sw(p_feat, 6)])
    other = sw(same, 1)
    scores = pl.pallas_call(
        functools.partial(score_kernel, order),
        out_shape=jax.ShapeDtypeStruct((examples, n * examples), jnp.float32),
        in_specs=[VMEM] * 3,
        out_specs=VMEM,
        compiler_params=pltpu.CompilerParams(vmem_limit_bytes=8 * MIB),
        name="score_rows",
    )(c_keep, same, other)
    return scores, c_feat


def plain_features(x, m, lengths, down, up, sketch_in, sketch_out, rank_down, rank_up):
    examples, seq, model = x.shape
    ks, kp = rank_down.shape[1], sketch_in.shape[1]
    live = (lax.broadcasted_iota(jnp.int32, (examples, seq), 1) < lengths[:, None]).astype(m.dtype)
    masked = (m * live[:, :, None]).reshape(examples * seq, -1)
    rows = x.reshape(examples * seq, model)
    grad_rows = dot(masked, up).astype(jnp.bfloat16)
    outward = dot(masked, sketch_out).astype(jnp.bfloat16)
    down_round = dot(rows, down).astype(jnp.bfloat16)
    inward = dot(rows, sketch_in).astype(jnp.bfloat16)
    left_small = dot(grad_rows, rank_down).astype(jnp.bfloat16)
    right_small = dot(down_round, rank_up).astype(jnp.bfloat16)

    def outer(small, wide):
        return jnp.einsum(
            "esk,esp->ekp",
            small.reshape(examples, seq, ks),
            wide.reshape(examples, seq, kp),
            preferred_element_type=jnp.float32,
        )

    joined = jnp.concatenate([outer(left_small, inward), outer(right_small, outward)], axis=1)
    joined = joined.reshape(examples, 2 * ks * kp)
    scale = lax.rsqrt(jnp.mean(joined * joined, axis=1, keepdims=True) + eps_mean)
    return (joined * scale).astype(jnp.bfloat16)


def plain_body(c_x, c_m, c_len, p_x, p_m, p_len, down, up, sketch_in, sketch_out, rank_down, rank_up):
    weights = [
        lax.all_gather(w, "fsdp", axis=0, tiled=True) for w in (down, up, sketch_in, sketch_out)
    ]
    p_feat = plain_features(p_x, p_m, p_len, *weights, rank_down, rank_up)
    c_feat = plain_features(c_x, c_m, c_len, *weights, rank_down, rank_up)
    every = lax.all_gather(p_feat, "fsdp", axis=0, tiled=True)
    return dot(c_feat, every.T) / c_feat.shape[1], c_feat


def solution(mesh):
    n = mesh.shape["fsdp"]
    rows = P(("dp", "fsdp"), None)
    cube = P(("dp", "fsdp"), None, None)
    line = P(("dp", "fsdp"))
    shard = P("fsdp", None)
    in_specs = (cube, cube, line, cube, cube, line, shard, shard, shard, shard, P(), P())

    def body(*args):
        if n == 1 << 3:
            return fast_body(n, *args)
        return plain_body(*args)

    return jax.shard_map(body, mesh=mesh, in_specs=in_specs, out_specs=(rows, rows), check_vma=False)
```

```python
import functools

import jax
import jax.numpy as jnp
from jax import lax
from jax.experimental import pallas as pl
from jax.experimental.pallas import tpu as pltpu
from jax.sharding import PartitionSpec as P

eps_mean = 1e-06
LAST = (((1,), (1,)), ((), ()))
VMEM = pl.BlockSpec(memory_space=pltpu.VMEM)
SMEM = pl.BlockSpec(memory_space=pltpu.SMEM)
HBM = pl.BlockSpec(memory_space=pltpu.HBM)
MIB = 1 << 20
SHORT = pl.CostEstimate(flops=1, bytes_accessed=1, transcendentals=0)


def in_hbm(*arrays):
    return tuple(pltpu.with_memory_space_constraint(a, pltpu.HBM) for a in arrays)


def dot(a, b):
    return jnp.dot(a, b, preferred_element_type=jnp.float32)


def dot_last(a, b):
    return lax.dot_general(a, b, LAST, preferred_element_type=jnp.float32)


def first_way(core, plane):
    return 2 + 2 * ((core + plane) % 2)


def partner(me, kind, plane):
    first = first_way(me % 2, plane)
    return me ^ (0, first, 6 - first, 6)[kind]


def pack_kernel(
    down_hbm, up_hbm, rank_down_hbm, rank_up_hbm, in_hbm, out_hbm,
    extra_ref, own_ref, tail_ref, down_ref, up_ref, rank_down_ref, rank_up_ref, sems,
):
    s_rows, o_rows = in_hbm.shape[0], out_hbm.shape[0]
    tail = tail_ref.shape[0] - o_rows
    moves = (
        (down_hbm, down_ref),
        (up_hbm, up_ref),
        (rank_down_hbm, rank_down_ref),
        (rank_up_hbm, rank_up_ref),
        (out_hbm, extra_ref.at[pl.ds(0, o_rows)]),
        (out_hbm, tail_ref.at[pl.ds(tail, o_rows)]),
        (in_hbm.at[pl.ds(s_rows - tail, tail)], tail_ref.at[pl.ds(0, tail)]),
        (in_hbm, own_ref),
    )
    copies = [pltpu.make_async_copy(a, b, sems.at[i]) for i, (a, b) in enumerate(moves)]
    for copy in copies:
        copy.start()
    for copy in copies[:4]:
        copy.wait()
    down_table = dot_last(rank_up_ref[...], down_ref[...]).astype(jnp.bfloat16)
    up_table = dot_last(rank_down_ref[...], up_ref[...]).astype(jnp.bfloat16)
    ks, width = up_table.shape
    lanes = extra_ref.shape[1]
    blocks = down_table.shape[1] // lanes
    for b in range(blocks):
        at = o_rows + b * ks
        extra_ref[at : at + ks, :] = down_table[:, b * lanes : (b + 1) * lanes]
    at = o_rows + blocks * ks
    extra_ref[at:, :] = jnp.zeros((ks, lanes), jnp.bfloat16)
    extra_ref[at:, :width] = up_table
    for copy in copies[4:]:
        copy.wait()


def load_kernel(
    n, seq, ks, c_x_hbm, c_m_hbm, c_len_hbm, p_x_hbm, p_m_hbm, p_len_hbm,
    x_ref, m_ref, live_ref, send_ref, c_len, p_len, sems,
):
    half = c_x_hbm.shape[0]
    moves = (
        (c_len_hbm, c_len), (p_len_hbm, p_len),
        (c_m_hbm, m_ref.at[pl.ds(0, half)]), (p_m_hbm, m_ref.at[pl.ds(half, half)]),
        (c_x_hbm, x_ref.at[pl.ds(0, half)]), (p_x_hbm, x_ref.at[pl.ds(half, half)]),
    )
    copies = [pltpu.make_async_copy(a, b, sems.at[i]) for i, (a, b) in enumerate(moves)]
    for copy in copies:
        copy.start()
    for copy in copies[:2]:
        copy.wait()
    _, height, width = live_ref.shape
    rows = lax.broadcasted_iota(jnp.int32, (height, width), 0)
    cols = lax.broadcasted_iota(jnp.int32, (height, width), 1)
    for side, lengths in enumerate((c_len, p_len)):
        live = jnp.zeros((height, width), jnp.bool_)
        for e in range(width // ks):
            live = live | (
                (cols >= e * ks)
                & (cols < (e + 1) * ks)
                & (rows >= e * seq)
                & (rows < e * seq + lengths[e])
            )
        live_ref[side] = live.astype(jnp.float32)
    for copy in copies[2:]:
        copy.wait()
    other = 1 - lax.axis_index("fsdp") % 2
    at = 0
    for ref in (x_ref, m_ref):
        wide = ref.shape[1] // n
        for b in range(n // 2):
            first = pl.multiple_of((2 * b + other) * wide, wide)
            send_ref[:, at : at + wide] = ref[:, pl.ds(first, wide)]
            at += wide


def small_sums(n, ks, x, m, tables):
    kd, ku = x.shape[1] // n, m.shape[1] // n
    left = 0.0
    right = 0.0
    for j, ref, at in tables:
        lanes = ref.shape[1]
        blocks = kd // lanes
        up = ref[at + blocks * ks : at + (blocks + 1) * ks, :ku]
        left += dot_last(m[:, pl.ds(pl.multiple_of(j * ku, ku), ku)], up)
        for b in range(blocks):
            cols = pl.ds(pl.multiple_of(j * kd + b * lanes, lanes), lanes)
            right += dot_last(x[:, cols], ref[at + b * ks : at + (b + 1) * ks, :])
    return left, right


def small_kernel(n, ks, places, x, m, *refs):
    me, plane = lax.axis_index("fsdp"), lax.axis_index("dp")
    tables = [(partner(me ^ other, kind, plane), refs[r], at) for r, at, kind, other in places]
    refs[-1][0], refs[-1][1] = small_sums(n, ks, x, m, tables)


def products(n, places, x, m, xo, refs):
    me, plane = lax.axis_index("fsdp"), lax.axis_index("dp")
    kd, ku = x.shape[1] // n, m.shape[1] // n
    sums = [[0.0, 0.0], [0.0, 0.0]]
    for ref, row, kind, sketch, first, count in places:
        j = partner(me, kind, plane)
        piece = refs[ref][row : row + count, :]
        source, wide, base = ((x, kd, 0), (m, ku, (n // 2) * kd))[sketch]
        here = source[:, pl.ds(pl.multiple_of(j * wide + first, 128), count)]
        there = xo[:, pl.ds(pl.multiple_of(base + (j // 2) * wide + first, 128), count)]
        sums[0][sketch] += dot(here, piece)
        sums[1][sketch] += dot(there, piece)
    return sums


def early_kernel(n, places, x, m, xo, *refs):
    sums = products(n, places, x, m, xo, refs[:-1])
    for i in range(2):
        for t in range(2):
            refs[-1][i, t] = sums[i][t]


def late_kernel(n, places, side, table_places, x, m, xo, early, *refs):
    refs, (own_ref, send_ref) = refs[:-2], refs[-2:]
    half = x.shape[0] // 2
    rows = pl.ds(side * half, half)
    sums = products(n, places, x.at[rows], m.at[rows], xo.at[rows], refs)
    for t in range(2):
        own_ref[t] = sums[0][t] + early[0, t, rows, :]
        send_ref[t * half : (t + 1) * half, :] = (sums[1][t] + early[1, t, rows, :]).astype(jnp.bfloat16)
    at = 2 * half
    for ref, row, count in table_places:
        send_ref[at : at + count, :] = refs[ref][row : row + count, :]
        at += count


def join_kernel(n, ks, side, places, x, m, live, own, got, got_tables, first_small, more_small, *refs):
    outs, (left_scratch, right_scratch) = refs[:-2], refs[-2:]
    me, plane = lax.axis_index("fsdp"), lax.axis_index("dp")
    half = x.shape[0] // 2
    rows = pl.ds(side * half, half)
    tables = [(partner(me ^ other, kind, plane), got_tables, at) for at, kind, other in places]
    parts = small_sums(n, ks, x.at[rows], m.at[rows], tables)
    joined = []
    for t in range(2):
        small = parts[t] + first_small[t, rows, :] + more_small[t, rows, :]
        small = small.astype(jnp.bfloat16).astype(jnp.float32)
        wide = jnp.concatenate([small] * (live.shape[2] // ks), axis=1)
        factor = jnp.where(live[side] > 0, wide, 0.0).T.astype(jnp.bfloat16)
        total = own[t] + got[t * half : (t + 1) * half, :].astype(jnp.float32)
        joined.append(dot(factor, total.astype(jnp.bfloat16)))
    left, right = joined
    total = left.shape[0]
    count, cols = total // ks, left.shape[1]
    left = left.reshape(count, ks, cols)
    right = right.reshape(count, ks, cols)
    mean = jnp.sum(left * left + right * right, axis=(1, 2), keepdims=True) / (2 * ks * cols)
    scale = lax.rsqrt(mean + eps_mean)
    lanes = left_scratch.shape[2]
    for scratch, value in ((left_scratch, left), (right_scratch, right)):
        scaled = (value * scale).reshape(total, cols)
        for b in range(cols // lanes):
            scratch[b] = scaled[:, b * lanes : (b + 1) * lanes]
    for t, scratch in enumerate((left_scratch, right_scratch)):
        for r in range(ks):
            for b in range(cols // lanes):
                at = (t * ks + r) * cols + b * lanes
                value = scratch[b, pl.ds(r, count, stride=ks), :].astype(jnp.bfloat16)
                for out in outs:
                    out[:, at : at + lanes] = value


def same_kernel(c_ref, same_ref, out_ref):
    out_ref[...] = dot_last(c_ref[...], same_ref[...])


def score_kernel(order, c_ref, same_scores, other_ref, out_ref):
    me = lax.axis_index("fsdp")
    feats = c_ref[...]
    mixed = jnp.concatenate([same_scores[...], dot_last(feats, other_ref[...])], axis=1)
    width = mixed.shape[1]
    per = width // len(order)
    rows = lax.broadcasted_iota(jnp.int32, (width, width), 0)
    cols = lax.broadcasted_iota(jnp.int32, (width, width), 1)
    target = jnp.zeros((width, width), jnp.int32)
    for g, k in enumerate(order):
        target = jnp.where(rows // per == g, (me ^ k) * per + rows % per, target)
    place = (target == cols).astype(jnp.float32)
    out = lax.dot_general(
        mixed, place, (((1,), (0,)), ((), ())),
        preferred_element_type=jnp.float32, precision=lax.Precision.HIGHEST,
    )
    out_ref[...] = out / feats.shape[1]


def swap(x, k, axis, size):
    return lax.ppermute(x, axis, [(i, i ^ k) for i in range(size)])


def fast_body(n, planes, c_x, c_m, c_len, p_x, p_m, p_len, down, up, sketch_in, sketch_out, rank_down, rank_up):
    examples, seq, model = c_x.shape
    value = c_m.shape[2]
    ks, kp = rank_down.shape[1], sketch_in.shape[1]
    s_rows, o_rows = sketch_in.shape[0], sketch_out.shape[0]
    t_rows = (s_rows // kp + 1) * ks
    sw = functools.partial(swap, axis="fsdp", size=n)
    order = (0, 2, 4, 6, 1, 3, 5, 7)

    def along(x, second):
        pairs = []
        for i in range(n):
            for z in range(planes):
                way = first_way(i % 2, z)
                pairs.append((i * planes + z, (i ^ (6 - way if second else way)) * planes + z))
        return lax.ppermute(x, ("fsdp", "dp"), pairs)

    def array(*shape, dtype=jnp.bfloat16):
        return jax.ShapeDtypeStruct(shape, dtype)

    def kernel(f, name, outs, operands, in_specs=None, scratch=(), limit=8):
        return pl.pallas_call(
            f,
            out_shape=outs,
            in_specs=in_specs or [VMEM] * len(operands),
            out_specs=(VMEM,) * len(outs) if isinstance(outs, tuple) else VMEM,
            scratch_shapes=scratch,
            compiler_params=pltpu.CompilerParams(vmem_limit_bytes=limit * MIB),
            cost_estimate=SHORT,
            name=name,
        )(*operands)

    beside = s_rows * 5 // 8 // 128 * 128
    extra, own, tail = kernel(
        pack_kernel,
        "pack_weights",
        (array(o_rows + t_rows, kp), array(s_rows, kp), array(s_rows - beside + o_rows, kp)),
        in_hbm(down, up, rank_down.T, rank_up.T, sketch_in, sketch_out),
        in_specs=[HBM] * 6,
        scratch=[
            pltpu.VMEM(down.shape, down.dtype),
            pltpu.VMEM(up.shape, up.dtype),
            pltpu.VMEM(rank_down.shape[::-1], rank_down.dtype),
            pltpu.VMEM(rank_up.shape[::-1], rank_up.dtype),
            pltpu.SemaphoreType.DMA((8,)),
        ],
    )
    flat = (examples * seq, model)
    flat_m = (examples * seq, value)
    rows, total = 2 * examples * seq, 2 * examples * ks
    x, m, live, send = kernel(
        functools.partial(load_kernel, n, seq, ks),
        "load_rows",
        (
            array(rows, model),
            array(rows, value),
            array(2, rows // 2, total // 2, dtype=jnp.float32),
            array(rows, (model + value) // 2),
        ),
        in_hbm(c_x.reshape(flat), c_m.reshape(flat_m), c_len, p_x.reshape(flat), p_m.reshape(flat_m), p_len),
        in_specs=[HBM] * 6,
        scratch=[
            pltpu.SMEM(c_len.shape, c_len.dtype),
            pltpu.SMEM(p_len.shape, p_len.dtype),
            pltpu.SemaphoreType.DMA((6,)),
        ],
    )

    first, first_extra = along(sketch_in, False), along(extra, False)
    first, first_extra, x, m, live, send = lax.optimization_barrier((first, first_extra, x, m, live, send))

    more = along(jnp.concatenate([first, first_extra, tail]), True)
    rest = swap(jnp.concatenate([first[:beside], first_extra[o_rows:]]), 1, "dp", planes)
    xo = sw(send, 1)
    t_first = jnp.concatenate([extra[o_rows:], first_extra[o_rows:]])
    t_other = sw(t_first, 1)

    first_small = kernel(
        functools.partial(small_kernel, n, ks, ((0, 0, 0, 0), (0, t_rows, 1, 0), (1, 0, 0, 1), (1, t_rows, 1, 1))),
        "first_factors",
        array(2, rows, ks, dtype=jnp.float32),
        (x, m, t_first, t_other),
    )
    early = kernel(
        functools.partial(
            early_kernel, n,
            ((0, 0, 0, 0, 0, s_rows), (1, 0, 0, 1, 0, o_rows), (2, 0, 1, 0, 0, s_rows), (3, 0, 1, 1, 0, o_rows)),
        ),
        "early_products",
        array(2, 2, rows, kp, dtype=jnp.float32),
        (x, m, xo, own, extra, first, first_extra),
    )
    early, first_small = lax.optimization_barrier((early, first_small))

    t_at = s_rows + o_rows
    tail_at = t_at + t_rows
    left_rows = s_rows - beside
    late_places = (
        (0, 0, 3, 0, 0, s_rows), (0, s_rows, 3, 1, 0, o_rows),
        (0, tail_at, 2, 0, beside, left_rows), (0, tail_at + left_rows, 2, 1, 0, o_rows),
        (1, 0, 2, 0, 0, beside),
    )
    tables = ((0, t_at, t_rows), (1, beside, t_rows))

    def late(side, name, tables):
        return kernel(
            functools.partial(late_kernel, n, late_places, side, tables),
            name,
            (
                array(2, rows // 2, kp, dtype=jnp.float32),
                array(rows + sum(count for _, _, count in tables), kp),
            ),
            (x, m, xo, early, more, rest),
        )

    p_own, p_send = late(1, "probe_products", tables)
    p_got = sw(p_send, 1)
    more_small = kernel(
        functools.partial(small_kernel, n, ks, ((0, t_at, 3, 0), (1, beside, 2, 0))),
        "more_factors",
        array(2, rows, ks, dtype=jnp.float32),
        (x, m, more, rest),
    )
    got_places = ((rows, 3, 1), (rows + t_rows, 2, 1))
    feats = array(examples, 2 * ks * kp)
    scratch = [pltpu.VMEM((kp // 128, total // 2, 128), jnp.float32)] * 2

    def join(side, name, outs, own, got):
        return kernel(
            functools.partial(join_kernel, n, ks, side, got_places),
            name,
            outs,
            (x, m, live, own, got, p_got, first_small, more_small),
            scratch=scratch,
        )

    p_feat = join(1, "probe_features", feats, p_own, p_got)
    c_own, c_send = late(0, "candidate_products", ())
    c_feat, c_keep = join(0, "candidate_features", (feats, feats), c_own, sw(c_send, 1))

    got = [sw(p_feat, k) for k in (2, 4, 6)]
    c_keep, *got = lax.optimization_barrier((c_keep, *got))
    same = jnp.concatenate([p_feat, *got])
    other = sw(same, 1)
    same_scores = kernel(
        same_kernel, "same_scores", array(examples, n // 2 * examples, dtype=jnp.float32), (c_keep, same)
    )
    scores = kernel(
        functools.partial(score_kernel, order),
        "score_rows",
        array(examples, n * examples, dtype=jnp.float32),
        (c_keep, same_scores, other),
    )
    return scores, c_feat


def plain_features(x, m, lengths, down, up, sketch_in, sketch_out, rank_down, rank_up):
    examples, seq, model = x.shape
    ks, kp = rank_down.shape[1], sketch_in.shape[1]
    live = (lax.broadcasted_iota(jnp.int32, (examples, seq), 1) < lengths[:, None]).astype(m.dtype)
    masked = (m * live[:, :, None]).reshape(examples * seq, -1)
    rows = x.reshape(examples * seq, model)
    grad_rows = dot(masked, up).astype(jnp.bfloat16)
    outward = dot(masked, sketch_out).astype(jnp.bfloat16)
    down_round = dot(rows, down).astype(jnp.bfloat16)
    inward = dot(rows, sketch_in).astype(jnp.bfloat16)
    left_small = dot(grad_rows, rank_down).astype(jnp.bfloat16)
    right_small = dot(down_round, rank_up).astype(jnp.bfloat16)

    def outer(small, wide):
        return jnp.einsum(
            "esk,esp->ekp",
            small.reshape(examples, seq, ks),
            wide.reshape(examples, seq, kp),
            preferred_element_type=jnp.float32,
        )

    joined = jnp.concatenate([outer(left_small, inward), outer(right_small, outward)], axis=1)
    joined = joined.reshape(examples, 2 * ks * kp)
    scale = lax.rsqrt(jnp.mean(joined * joined, axis=1, keepdims=True) + eps_mean)
    return (joined * scale).astype(jnp.bfloat16)


def plain_body(c_x, c_m, c_len, p_x, p_m, p_len, down, up, sketch_in, sketch_out, rank_down, rank_up):
    weights = [
        lax.all_gather(w, "fsdp", axis=0, tiled=True) for w in (down, up, sketch_in, sketch_out)
    ]
    p_feat = plain_features(p_x, p_m, p_len, *weights, rank_down, rank_up)
    c_feat = plain_features(c_x, c_m, c_len, *weights, rank_down, rank_up)
    every = lax.all_gather(p_feat, "fsdp", axis=0, tiled=True)
    return dot(c_feat, every.T) / c_feat.shape[1], c_feat


def solution(mesh):
    n, planes = mesh.shape["fsdp"], mesh.shape["dp"]
    rows = P(("dp", "fsdp"), None)
    cube = P(("dp", "fsdp"), None, None)
    line = P(("dp", "fsdp"))
    shard = P("fsdp", None)
    in_specs = (cube, cube, line, cube, cube, line, shard, shard, shard, shard, P(), P())

    def body(*args):
        if n == 1 << 3 and planes % 2 == 0:
            return fast_body(n, planes, *args)
        return plain_body(*args)

    return jax.shard_map(body, mesh=mesh, in_specs=in_specs, out_specs=(rows, rows), check_vma=False)
```

```python
import functools

import jax
import jax.numpy as jnp
from jax import lax
from jax.experimental import pallas as pl
from jax.experimental.pallas import tpu as pltpu
from jax.sharding import PartitionSpec as P

eps_mean = 1e-06
LAST = (((1,), (1,)), ((), ()))
VMEM = pl.BlockSpec(memory_space=pltpu.VMEM)
SMEM = pl.BlockSpec(memory_space=pltpu.SMEM)
HBM = pl.BlockSpec(memory_space=pltpu.HBM)
MIB = 1 << 20
SHORT = pl.CostEstimate(flops=1, bytes_accessed=1, transcendentals=0)


def in_hbm(*arrays):
    return tuple(pltpu.with_memory_space_constraint(a, pltpu.HBM) for a in arrays)


def dot(a, b):
    return jnp.dot(a, b, preferred_element_type=jnp.float32)


def dot_last(a, b):
    return lax.dot_general(a, b, LAST, preferred_element_type=jnp.float32)


def split_two(x):
    high = x.astype(jnp.bfloat16)
    return high, (x - high.astype(jnp.float32)).astype(jnp.bfloat16)


def first_way(core, plane):
    return 2 + 2 * ((core + plane) % 2)


def partner(me, kind, plane):
    first = first_way(me % 2, plane)
    return me ^ (0, first, 6 - first, 6)[kind]


def pack_kernel(
    down_hbm, up_hbm, rank_down_hbm, rank_up_hbm, in_hbm, out_hbm,
    extra_ref, own_ref, tail_ref, down_ref, up_ref, rank_down_ref, rank_up_ref, sems,
):
    s_rows, o_rows = in_hbm.shape[0], out_hbm.shape[0]
    tail = tail_ref.shape[0] - o_rows
    moves = (
        (down_hbm, down_ref),
        (up_hbm, up_ref),
        (rank_down_hbm, rank_down_ref),
        (rank_up_hbm, rank_up_ref),
        (out_hbm, extra_ref.at[pl.ds(0, o_rows)]),
        (out_hbm, tail_ref.at[pl.ds(tail, o_rows)]),
        (in_hbm.at[pl.ds(s_rows - tail, tail)], tail_ref.at[pl.ds(0, tail)]),
        (in_hbm, own_ref),
    )
    copies = [pltpu.make_async_copy(a, b, sems.at[i]) for i, (a, b) in enumerate(moves)]
    for copy in copies:
        copy.start()
    for copy in copies[:4]:
        copy.wait()
    down_table = dot_last(rank_up_ref[...], down_ref[...]).astype(jnp.bfloat16)
    up_table = dot_last(rank_down_ref[...], up_ref[...]).astype(jnp.bfloat16)
    ks, width = up_table.shape
    lanes = extra_ref.shape[1]
    blocks = down_table.shape[1] // lanes
    for b in range(blocks):
        at = o_rows + b * ks
        extra_ref[at : at + ks, :] = down_table[:, b * lanes : (b + 1) * lanes]
    at = o_rows + blocks * ks
    extra_ref[at:, :] = jnp.zeros((ks, lanes), jnp.bfloat16)
    extra_ref[at:, :width] = up_table
    for copy in copies[4:]:
        copy.wait()


def load_kernel(
    n, seq, c_x_hbm, c_m_hbm, c_len_hbm, p_x_hbm, p_m_hbm, p_len_hbm,
    x_ref, m_ref, send_ref, c_len, p_len, sems,
):
    half = c_x_hbm.shape[0]
    moves = (
        (c_len_hbm, c_len), (p_len_hbm, p_len),
        (c_m_hbm, m_ref.at[pl.ds(0, half)]), (p_m_hbm, m_ref.at[pl.ds(half, half)]),
        (c_x_hbm, x_ref.at[pl.ds(0, half)]), (p_x_hbm, x_ref.at[pl.ds(half, half)]),
    )
    copies = [pltpu.make_async_copy(a, b, sems.at[i]) for i, (a, b) in enumerate(moves)]
    for copy in copies:
        copy.start()
    for copy in copies:
        copy.wait()
    for side, lengths in enumerate((c_len, p_len)):
        for e in range(half // seq):
            rows = pl.ds(side * half + e * seq, seq)
            for ref in (x_ref, m_ref):
                dead = lax.broadcasted_iota(jnp.int32, (seq, ref.shape[1]), 0) >= lengths[e]
                ref[rows, :] = jnp.where(dead, jnp.zeros((), ref.dtype), ref[rows, :])
    other = 1 - lax.axis_index("fsdp") % 2
    at = 0
    for ref in (x_ref, m_ref):
        wide = ref.shape[1] // n
        for b in range(n // 2):
            first = pl.multiple_of((2 * b + other) * wide, wide)
            send_ref[:, at : at + wide] = ref[:, pl.ds(first, wide)]
            at += wide


def spans(n, x, m, xo, j, sketch, first, count):
    source, wide, base = ((x, x.shape[1] // n, 0), (m, m.shape[1] // n, (n // 2) * (x.shape[1] // n)))[sketch]
    here = pl.ds(pl.multiple_of(j * wide + first, 128), count)
    there = pl.ds(pl.multiple_of(base + (j // 2) * wide + first, 128), count)
    return source[:, here], xo[:, there]


def small_sums(n, ks, places, x, m, xo, refs):
    me, plane = lax.axis_index("fsdp"), lax.axis_index("dp")
    ku = m.shape[1] // n
    sums = [[0.0, 0.0], [0.0, 0.0]]
    for r, at, kind in places:
        j = partner(me, kind, plane)
        lanes = refs[r].shape[1]
        blocks = x.shape[1] // n // lanes
        up = refs[r][at + blocks * ks : at + (blocks + 1) * ks, :ku]
        for who, rows in enumerate(spans(n, x, m, xo, j, 1, 0, ku)):
            sums[who][0] += dot_last(rows, up)
        table = jnp.concatenate([refs[r][at + b * ks : at + (b + 1) * ks, :] for b in range(blocks)], axis=1)
        for who, rows in enumerate(spans(n, x, m, xo, j, 0, 0, blocks * lanes)):
            sums[who][1] += dot_last(rows, table)
    return sums


def products(n, places, x, m, xo, refs):
    me, plane = lax.axis_index("fsdp"), lax.axis_index("dp")
    sums = [[0.0, 0.0], [0.0, 0.0]]
    for ref, row, kind, sketch, first, count in places:
        piece = refs[ref][row : row + count, :]
        for who, rows in enumerate(spans(n, x, m, xo, partner(me, kind, plane), sketch, first, count)):
            sums[who][sketch] += dot(rows, piece)
    return sums


def early_kernel(n, ks, places, tables, x, m, xo, *refs):
    refs, (sums_ref, small_ref) = refs[:-2], refs[-2:]
    sums = products(n, places, x, m, xo, refs)
    small = small_sums(n, ks, tables, x, m, xo, refs)
    for who in range(2):
        for t in range(2):
            sums_ref[who, t] = sums[who][t]
            small_ref[who, t] = small[who][t]


def late_kernel(n, ks, side, places, tables, x, m, xo, sums, early_small, *refs):
    refs, (keep, keep_small, send, wide, narrow) = refs[:-5], refs[-5:]
    core = lax.axis_index("fsdp") % 2
    half = x.shape[0] // 2
    rows = pl.ds(side * half, half)
    views = x.at[rows], m.at[rows], xo.at[rows]
    late = products(n, places, *views, refs)
    late_small = small_sums(n, ks, tables, *views, refs)
    for t in range(2):
        for who in range(2):
            wide[t, who * half : (who + 1) * half, :] = late[who][t] + sums[who, t, rows, :]
        both = [late_small[who][t] + early_small[who, t, rows, :] for who in range(2)]
        narrow[t] = jnp.concatenate(both, axis=0).T
    keep[...] = wide[core]
    keep_small[...] = narrow[core]
    for who in range(2):
        first = (1 - who) * half
        send[who * half : (who + 1) * half, :] = wide[1 - core, first : first + half, :].astype(jnp.bfloat16)
    small = narrow[1 - core]
    high, low = split_two(jnp.concatenate([small[:, half:], small[:, :half]], axis=1))
    send[2 * half : 2 * half + ks, :] = high
    send[2 * half + ks :, :] = low


def gradients(seq, keep, keep_small, got):
    rows, ks = keep.shape[0], keep_small.shape[0]
    small = keep_small[...] + got[rows : rows + ks, :].astype(jnp.float32) + got[rows + ks :, :].astype(jnp.float32)
    count = rows // seq
    tiled = jnp.concatenate([small] * count, axis=0)
    e_row = lax.broadcasted_iota(jnp.int32, tiled.shape, 0) // ks
    e_col = lax.broadcasted_iota(jnp.int32, tiled.shape, 1) // seq
    factor = jnp.where(e_row == e_col, tiled, 0.0).astype(jnp.bfloat16)
    total = keep[...] + got[:rows, :].astype(jnp.float32)
    return dot(factor, total.astype(jnp.bfloat16))


def flatten(grads, ks, out, scratch, base=0):
    cols, lanes = grads.shape[1], scratch.shape[2]
    for b in range(cols // lanes):
        scratch[b] = grads[:, b * lanes : (b + 1) * lanes]
    for k in range(ks):
        for b in range(cols // lanes):
            at = base + k * cols + b * lanes
            rows = pl.ds(k, grads.shape[0] // ks, stride=ks)
            out[:, at : at + lanes] = scratch[b, rows, :].astype(out.dtype)


def probe_kernel(seq, keep, keep_small, got, out, scratch):
    flatten(gradients(seq, keep, keep_small, got), keep_small.shape[0], out, scratch)


def candidate_kernel(seq, keep, keep_small, got, out, own, send, scratch):
    grads = gradients(seq, keep, keep_small, got)
    flatten(grads, keep_small.shape[0], out, scratch)
    half = grads.shape[0] // 2
    own[...] = grads[:half]
    send[...] = grads[half:]


def feature_kernel(ks, own, got, out, scratch):
    core = lax.axis_index("fsdp") % 2
    left = jnp.where(core == 0, own[...], got[...])
    right = jnp.where(core == 0, got[...], own[...])
    rows, cols = left.shape
    square = (left * left + right * right).reshape(rows // ks, ks, cols)
    scale = lax.rsqrt(jnp.sum(square, axis=(1, 2), keepdims=True) / (2 * ks * cols) + eps_mean)
    for t, part in enumerate((left, right)):
        scaled = (part.reshape(rows // ks, ks, cols) * scale).reshape(rows, cols)
        flatten(scaled, ks, out, scratch, t * ks * cols)


def score_kernel(kinds, c_ref, *refs):
    probes, (own_ref, send_ref) = refs[:-2], refs[-2:]
    me = lax.axis_index("fsdp")
    cands = c_ref[...]
    per = cands.shape[0] // 2
    held = jnp.concatenate([ref[...] for ref in probes], axis=0)
    width = held.shape[0]
    mixed = dot_last(jnp.concatenate([cands, held], axis=0), held)
    scores, gram = mixed[: 2 * per], mixed[2 * per :]

    def diagonal(square, axis):
        rows = lax.broadcasted_iota(jnp.int32, square.shape, 0)
        cols = lax.broadcasted_iota(jnp.int32, square.shape, 1)
        return jnp.sum(jnp.where(rows == cols, square, 0.0), axis=axis, keepdims=True)

    rows = jnp.concatenate([scores, jnp.broadcast_to(diagonal(gram, 0), scores.shape)], axis=0)
    group = lax.broadcasted_iota(jnp.int32, rows.shape, 1) // per
    placed = jnp.zeros(rows.shape, jnp.float32)
    for g in range(width // per):
        block = jnp.concatenate([rows[:, g * per : (g + 1) * per]] * (width // per), axis=1)
        placed = jnp.where(group == (me ^ kinds[g // 2] ^ (g % 2)), block, placed)
    squares = jnp.broadcast_to(diagonal(dot_last(cands, cands), 1), (2 * per, width))
    for i, ref in enumerate((own_ref, send_ref)):
        ref[:per, :] = placed[i * per : (i + 1) * per]
        ref[per : 2 * per, :] = placed[2 * per : 3 * per]
        ref[2 * per :, :] = squares[i * per : (i + 1) * per]


def final_kernel(entries, own, got, out):
    total = own[...] + got[...]
    per = out.shape[0]
    scale = lax.rsqrt(total[per:] / entries + eps_mean)
    out[...] = total[:per] * scale[:per] * scale[per:] / entries


def swap(x, k, axis, size):
    return lax.ppermute(x, axis, [(i, i ^ k) for i in range(size)])


def fast_body(n, planes, c_x, c_m, c_len, p_x, p_m, p_len, down, up, sketch_in, sketch_out, rank_down, rank_up):
    examples, seq, model = c_x.shape
    value = c_m.shape[2]
    ks, kp = rank_down.shape[1], sketch_in.shape[1]
    s_rows, o_rows = sketch_in.shape[0], sketch_out.shape[0]
    t_rows = (s_rows // kp + 1) * ks
    sw = functools.partial(swap, axis="fsdp", size=n)

    def along(x, second):
        pairs = []
        for i in range(n):
            for z in range(planes):
                way = first_way(i % 2, z)
                pairs.append((i * planes + z, (i ^ (6 - way if second else way)) * planes + z))
        return lax.ppermute(x, ("fsdp", "dp"), pairs)

    def array(*shape, dtype=jnp.bfloat16):
        return jax.ShapeDtypeStruct(shape, dtype)

    def kernel(f, name, outs, operands, in_specs=None, scratch=(), limit=8):
        return pl.pallas_call(
            f,
            out_shape=outs,
            in_specs=in_specs or [VMEM] * len(operands),
            out_specs=(VMEM,) * len(outs) if isinstance(outs, tuple) else VMEM,
            scratch_shapes=scratch,
            compiler_params=pltpu.CompilerParams(vmem_limit_bytes=limit * MIB),
            cost_estimate=SHORT,
            name=name,
        )(*operands)

    beside = s_rows * 5 // 8 // 128 * 128
    extra, own, tail = kernel(
        pack_kernel,
        "pack_weights",
        (array(o_rows + t_rows, kp), array(s_rows, kp), array(s_rows - beside + o_rows, kp)),
        in_hbm(down, up, rank_down.T, rank_up.T, sketch_in, sketch_out),
        in_specs=[HBM] * 6,
        scratch=[
            pltpu.VMEM(down.shape, down.dtype),
            pltpu.VMEM(up.shape, up.dtype),
            pltpu.VMEM(rank_down.shape[::-1], rank_down.dtype),
            pltpu.VMEM(rank_up.shape[::-1], rank_up.dtype),
            pltpu.SemaphoreType.DMA((8,)),
        ],
    )
    flat = (examples * seq, model)
    flat_m = (examples * seq, value)
    rows = 2 * examples * seq
    x, m, send = kernel(
        functools.partial(load_kernel, n, seq),
        "load_rows",
        (array(rows, model), array(rows, value), array(rows, (model + value) // 2)),
        in_hbm(c_x.reshape(flat), c_m.reshape(flat_m), c_len, p_x.reshape(flat), p_m.reshape(flat_m), p_len),
        in_specs=[HBM] * 6,
        scratch=[
            pltpu.SMEM(c_len.shape, c_len.dtype),
            pltpu.SMEM(p_len.shape, p_len.dtype),
            pltpu.SemaphoreType.DMA((6,)),
        ],
    )

    first, first_extra = along(sketch_in, False), along(extra, False)
    first, first_extra, x, m, send = lax.optimization_barrier((first, first_extra, x, m, send))

    more = along(jnp.concatenate([first, first_extra, tail]), True)
    rest = swap(jnp.concatenate([first[:beside], first_extra[o_rows:]]), 1, "dp", planes)
    xo = sw(send, 1)

    f32 = jnp.float32
    early_places = (
        (0, 0, 0, 0, 0, s_rows), (1, 0, 0, 1, 0, o_rows), (2, 0, 1, 0, 0, s_rows), (3, 0, 1, 1, 0, o_rows),
    )
    sums, small = kernel(
        functools.partial(early_kernel, n, ks, early_places, ((1, o_rows, 0), (3, o_rows, 1))),
        "early_products",
        (array(2, 2, rows, kp, dtype=f32), array(2, 2, rows, ks, dtype=f32)),
        (x, m, xo, own, extra, first, first_extra),
    )
    t_at = s_rows + o_rows
    tail_at = t_at + t_rows
    left_rows = s_rows - beside
    late_places = (
        (0, 0, 3, 0, 0, s_rows), (0, s_rows, 3, 1, 0, o_rows),
        (0, tail_at, 2, 0, beside, left_rows), (0, tail_at + left_rows, 2, 1, 0, o_rows),
        (1, 0, 2, 0, 0, beside),
    )

    def late(side, name):
        keep, keep_small, out = kernel(
            functools.partial(late_kernel, n, ks, side, late_places, ((0, t_at, 3), (1, beside, 2))),
            name,
            (array(rows, kp, dtype=f32), array(ks, rows, dtype=f32), array(rows + 2 * ks, kp)),
            (x, m, xo, sums, small, more, rest),
            scratch=[pltpu.VMEM((2, rows, kp), f32), pltpu.VMEM((2, ks, rows), f32)],
        )
        return keep, keep_small, sw(out, 1)

    total = 2 * examples * ks
    side = array(2 * examples, ks * kp)

    def scratch(count):
        return [pltpu.VMEM((kp // 128, count, 128), f32)]

    p_side = kernel(
        functools.partial(probe_kernel, seq), "probe_sides", side, late(1, "probe_products"), scratch=scratch(total)
    )
    grads = array(total // 2, kp, dtype=f32)
    c_side, c_grads, c_send = kernel(
        functools.partial(candidate_kernel, seq),
        "candidate_sides",
        (side, grads, grads),
        late(0, "candidate_products"),
        scratch=scratch(total),
    )
    c_feat = kernel(
        functools.partial(feature_kernel, ks),
        "candidate_features",
        array(examples, 2 * ks * kp),
        (c_grads, sw(c_send, 1)),
        scratch=scratch(total // 2),
    )

    kinds = (0, 6, 4, 2)
    got = [sw(p_side, k) for k in kinds[1:]]
    c_side, *got = lax.optimization_barrier((c_side, *got))
    part = array(3 * examples, n * examples, dtype=f32)
    scores, to_other = kernel(
        functools.partial(score_kernel, kinds), "score_shares", (part, part), (c_side, p_side, *got)
    )
    scores = kernel(
        functools.partial(final_kernel, 2 * ks * kp),
        "scores",
        array(examples, n * examples, dtype=f32),
        (scores, sw(to_other, 1)),
    )
    return scores, c_feat


def plain_features(x, m, lengths, down, up, sketch_in, sketch_out, rank_down, rank_up):
    examples, seq, model = x.shape
    ks, kp = rank_down.shape[1], sketch_in.shape[1]
    live = (lax.broadcasted_iota(jnp.int32, (examples, seq), 1) < lengths[:, None]).astype(m.dtype)
    masked = (m * live[:, :, None]).reshape(examples * seq, -1)
    rows = x.reshape(examples * seq, model)
    grad_rows = dot(masked, up).astype(jnp.bfloat16)
    outward = dot(masked, sketch_out).astype(jnp.bfloat16)
    down_round = dot(rows, down).astype(jnp.bfloat16)
    inward = dot(rows, sketch_in).astype(jnp.bfloat16)
    left_small = dot(grad_rows, rank_down).astype(jnp.bfloat16)
    right_small = dot(down_round, rank_up).astype(jnp.bfloat16)

    def outer(small, wide):
        return jnp.einsum(
            "esk,esp->ekp",
            small.reshape(examples, seq, ks),
            wide.reshape(examples, seq, kp),
            preferred_element_type=jnp.float32,
        )

    joined = jnp.concatenate([outer(left_small, inward), outer(right_small, outward)], axis=1)
    joined = joined.reshape(examples, 2 * ks * kp)
    scale = lax.rsqrt(jnp.mean(joined * joined, axis=1, keepdims=True) + eps_mean)
    return (joined * scale).astype(jnp.bfloat16)


def plain_body(c_x, c_m, c_len, p_x, p_m, p_len, down, up, sketch_in, sketch_out, rank_down, rank_up):
    weights = [
        lax.all_gather(w, "fsdp", axis=0, tiled=True) for w in (down, up, sketch_in, sketch_out)
    ]
    p_feat = plain_features(p_x, p_m, p_len, *weights, rank_down, rank_up)
    c_feat = plain_features(c_x, c_m, c_len, *weights, rank_down, rank_up)
    every = lax.all_gather(p_feat, "fsdp", axis=0, tiled=True)
    return dot(c_feat, every.T) / c_feat.shape[1], c_feat


def solution(mesh):
    n, planes = mesh.shape["fsdp"], mesh.shape["dp"]
    rows = P(("dp", "fsdp"), None)
    cube = P(("dp", "fsdp"), None, None)
    line = P(("dp", "fsdp"))
    shard = P("fsdp", None)
    in_specs = (cube, cube, line, cube, cube, line, shard, shard, shard, shard, P(), P())

    def body(*args):
        if n == 1 << 3 and planes % 2 == 0:
            return fast_body(n, planes, *args)
        return plain_body(*args)

    return jax.shard_map(body, mesh=mesh, in_specs=in_specs, out_specs=(rows, rows), check_vma=False)
```

```python
import functools

import jax
import jax.numpy as jnp
from jax import lax
from jax.experimental import pallas as pl
from jax.experimental.pallas import tpu as pltpu
from jax.sharding import PartitionSpec as P

eps_mean = 1e-06
LAST = (((1,), (1,)), ((), ()))
VMEM = pl.BlockSpec(memory_space=pltpu.VMEM)
SMEM = pl.BlockSpec(memory_space=pltpu.SMEM)
HBM = pl.BlockSpec(memory_space=pltpu.HBM)
MIB = 1 << 20
SHORT = pl.CostEstimate(flops=1, bytes_accessed=1, transcendentals=0)


def in_hbm(*arrays):
    return tuple(pltpu.with_memory_space_constraint(a, pltpu.HBM) for a in arrays)


def dot(a, b):
    return jnp.dot(a, b, preferred_element_type=jnp.float32)


def dot_last(a, b):
    return lax.dot_general(a, b, LAST, preferred_element_type=jnp.float32)


def split_two(x):
    high = x.astype(jnp.bfloat16)
    return high, (x - high.astype(jnp.float32)).astype(jnp.bfloat16)


def first_way(core, plane):
    return 2 + 2 * ((core + plane) % 2)


def partner(me, kind, plane):
    first = first_way(me % 2, plane)
    return me ^ (0, first, 6 - first, 6)[kind]


def prepare_kernel(
    n, seq, down_hbm, up_hbm, rank_down_hbm, rank_up_hbm, in_hbm, out_hbm,
    c_x_hbm, c_m_hbm, c_len_hbm, p_x_hbm, p_m_hbm, p_len_hbm,
    extra_ref, tail_ref, x_ref, m_ref, live_ref, c_send, p_send,
    down_ref, up_ref, rank_down_ref, rank_up_ref, c_len, p_len, sems,
):
    o_rows, half = out_hbm.shape[0], c_x_hbm.shape[0]
    s_rows, tail = in_hbm.shape[0], tail_ref.shape[0]
    moves = (
        (down_hbm, down_ref),
        (up_hbm, up_ref),
        (rank_down_hbm, rank_down_ref),
        (rank_up_hbm, rank_up_ref),
        (c_len_hbm, c_len),
        (p_len_hbm, p_len),
        (out_hbm, extra_ref.at[pl.ds(0, o_rows)]),
        (in_hbm.at[pl.ds(s_rows - tail, tail)], tail_ref),
    )
    moves += tuple(
        (source.at[pl.ds(e * seq, seq)], to.at[pl.ds(base + e * seq, seq)])
        for source, to, base in ((c_m_hbm, m_ref, 0), (c_x_hbm, x_ref, 0), (p_m_hbm, m_ref, half), (p_x_hbm, x_ref, half))
        for e in range(half // seq)
    )
    copies = [pltpu.make_async_copy(a, b, sems.at[i]) for i, (a, b) in enumerate(moves)]
    for copy in copies:
        copy.start()
    for copy in copies[:6]:
        copy.wait()
    down_table = dot_last(rank_up_ref[...], down_ref[...]).astype(jnp.bfloat16)
    up_table = dot_last(rank_down_ref[...], up_ref[...]).astype(jnp.bfloat16)
    ks, width = up_table.shape
    lanes = extra_ref.shape[1]
    blocks = down_table.shape[1] // lanes
    for b in range(blocks):
        at = o_rows + b * ks
        extra_ref[at : at + ks, :] = down_table[:, b * lanes : (b + 1) * lanes]
    at = o_rows + blocks * ks
    extra_ref[at:, :] = jnp.zeros((ks, lanes), jnp.bfloat16)
    extra_ref[at:, :width] = up_table
    lane = lax.broadcasted_iota(jnp.int32, live_ref.shape[1:], 1)
    for side, lengths in enumerate((c_len, p_len)):
        live = jnp.zeros(live_ref.shape[1:], jnp.bool_)
        for e in range(half // seq):
            live = live | ((lane >= e * seq) & (lane < e * seq + lengths[e]))
        live_ref[side] = live.astype(jnp.float32).astype(live_ref.dtype)
    other = 1 - lax.axis_index("fsdp") % 2
    examples = half // seq
    kd, ku = x_ref.shape[1] // n, m_ref.shape[1] // n
    for copy in copies[6:8]:
        copy.wait()
    for side, send_ref in enumerate((c_send, p_send)):
        for ref, wide, base, turn in ((m_ref, ku, (n // 2) * kd, 0), (x_ref, kd, 0, 1)):
            for e in range(examples):
                copies[8 + (2 * side + turn) * examples + e].wait()
                rows = pl.ds(e * seq, seq)
                for b in range(n // 2):
                    first = pl.multiple_of((2 * b + other) * wide, wide)
                    at = base + b * wide
                    send_ref[rows, at : at + wide] = ref[pl.ds(side * half + e * seq, seq), pl.ds(first, wide)]


def spans(n, x, m, xo, block, sketch, first, count):
    kind, core, whos = block
    j = partner(lax.axis_index("fsdp") ^ core, kind, lax.axis_index("dp"))
    source, wide, base = ((x, x.shape[1] // n, 0), (m, m.shape[1] // n, (n // 2) * (x.shape[1] // n)))[sketch]
    for who in whos:
        if who == 0:
            yield who, source[:, pl.ds(pl.multiple_of(j * wide + first, 128), count)]
        else:
            yield who, xo[:, pl.ds(pl.multiple_of(base + (j // 2) * wide + first, 128), count)]


def small_sums(n, ks, places, x, m, xo, refs):
    ku = m.shape[1] // n
    sums = [[0.0, 0.0], [0.0, 0.0]]
    for r, at, block in places:
        lanes = refs[r].shape[1]
        blocks = x.shape[1] // n // lanes
        up = refs[r][at + blocks * ks : at + (blocks + 1) * ks, :ku]
        for who, rows in spans(n, x, m, xo, block, 1, 0, ku):
            sums[who][0] += dot_last(rows, up)
        table = jnp.concatenate([refs[r][at + b * ks : at + (b + 1) * ks, :] for b in range(blocks)], axis=1)
        for who, rows in spans(n, x, m, xo, block, 0, 0, blocks * lanes):
            sums[who][1] += dot_last(rows, table)
    return sums


def products(n, places, x, m, xo, refs):
    sums = [[0.0, 0.0], [0.0, 0.0]]
    for ref, row, block, sketch, first, count in places:
        piece = refs[ref][row : row + count, :]
        for who, rows in spans(n, x, m, xo, block, sketch, first, count):
            sums[who][sketch] += dot(rows, piece)
    return sums


def own_kernel(n, ks, places, tables, in_hbm, extra, x, m, own, second, sums_ref, small_ref, sems):
    extra_rows = extra.shape[0]
    part = second.shape[0] - extra_rows
    first = in_hbm.shape[0] * 3 // 8 // 128 * 128
    copies = [
        pltpu.make_async_copy(in_hbm, own, sems.at[0]),
        pltpu.make_async_copy(in_hbm.at[pl.ds(first, part)], second.at[pl.ds(0, part)], sems.at[1]),
    ]
    for copy in copies:
        copy.start()
    second[part:, :] = extra[...]
    half = x.shape[0] // 2
    views = [(x.at[pl.ds(side * half, half)], m.at[pl.ds(side * half, half)], None) for side in range(2)]
    for side in range(2):
        small = small_sums(n, ks, tables, *views[side], (extra,))
        for t in range(2):
            small_ref[side, t] = small[0][t]
    for copy in copies:
        copy.wait()
    for side in range(2):
        sums = products(n, places, *views[side], (extra, own))
        for t in range(2):
            sums_ref[side, t] = sums[0][t]


def early_kernel(n, ks, places, tables, x, m, c_xo, p_xo, own_sums, own_small, *refs):
    refs, (sums_ref, small_ref) = refs[:-2], refs[-2:]
    half = c_xo.shape[0]
    for side, xo in enumerate((c_xo, p_xo)):
        rows = pl.ds(side * half, half)
        views = x.at[rows], m.at[rows], xo
        small = small_sums(n, ks, tables, *views, refs)
        sums = products(n, places, *views, refs)
        for t in range(2):
            small_ref[side, 0, t] = small[0][t] + own_small[side, t]
            small_ref[side, 1, t] = small[1][t]
            sums_ref[side, 0, t] = sums[0][t] + own_sums[side, t]
            sums_ref[side, 1, t] = sums[1][t]


def late_kernel(n, ks, side, places, tables, x, m, xo, live, sums, early_small, *refs):
    refs, (keep, keep_small, send, wide, narrow) = refs[:-5], refs[-5:]
    core = lax.axis_index("fsdp") % 2
    half = x.shape[0] // 2
    rows = pl.ds(side * half, half)
    views = x.at[rows], m.at[rows], xo
    late = products(n, places, *views, refs)
    late_small = small_sums(n, ks, tables, *views, refs)
    for t in range(2):
        for who in range(2):
            wide[t, who * half : (who + 1) * half, :] = late[who][t] + sums[side, who, t]
        both = [late_small[who][t] + early_small[side, who, t] for who in range(2)]
        narrow[t] = jnp.concatenate(both, axis=0).T
    keep[...] = wide[core]
    keep_small[...] = narrow[core]
    for who in range(2):
        first = (1 - who) * half
        send[who * half : (who + 1) * half, :] = wide[1 - core, first : first + half, :].astype(jnp.bfloat16)
    small = narrow[1 - core]
    high, low = split_two(jnp.concatenate([small[:, half:], small[:, :half]], axis=1))
    send[2 * half : 2 * half + ks, :] = high
    send[2 * half + ks : 2 * half + 2 * ks, :] = low
    send[2 * half + 2 * ks :, :half] = live[side]
    send[2 * half + 2 * ks :, half:] = live[side]


def gradients(seq, side, keep, keep_small, got, live):
    rows, ks = keep.shape[0], keep_small.shape[0]
    high, low = (got[at : at + ks, :].astype(jnp.float32) for at in (rows, rows + ks))
    there = got[rows + 2 * ks : rows + 2 * ks + 1, rows // 2 :]
    lives = jnp.concatenate([live[side, :1, :].astype(jnp.float32), there.astype(jnp.float32)], axis=1)
    small = jnp.where(lives > 0, keep_small[...] + high + low, 0.0)
    count = rows // seq
    tiled = jnp.concatenate([small] * count, axis=0)
    e_row = lax.broadcasted_iota(jnp.int32, tiled.shape, 0) // ks
    e_col = lax.broadcasted_iota(jnp.int32, tiled.shape, 1) // seq
    factor = jnp.where(e_row == e_col, tiled, 0.0).astype(jnp.bfloat16)
    total = keep[...] + got[:rows, :].astype(jnp.float32)
    return dot(factor, total.astype(jnp.bfloat16))


def flatten(grads, ks, out, scratch, base=0):
    cols, lanes = grads.shape[1], scratch.shape[2]
    for b in range(cols // lanes):
        scratch[b] = grads[:, b * lanes : (b + 1) * lanes]
    for k in range(ks):
        for b in range(cols // lanes):
            at = base + k * cols + b * lanes
            rows = pl.ds(k, grads.shape[0] // ks, stride=ks)
            out[:, at : at + lanes] = scratch[b, rows, :].astype(out.dtype)


def probe_kernel(seq, keep, keep_small, got, live, out, scratch):
    flatten(gradients(seq, 1, keep, keep_small, got, live), keep_small.shape[0], out, scratch)


def candidate_kernel(seq, keep, keep_small, got, live, out, own, send, scratch):
    grads = gradients(seq, 0, keep, keep_small, got, live)
    flatten(grads, keep_small.shape[0], out, scratch)
    half = grads.shape[0] // 2
    own[...] = grads[:half]
    send[...] = grads[half:]


def feature_kernel(ks, own, got, out, scratch):
    core = lax.axis_index("fsdp") % 2
    left = jnp.where(core == 0, own[...], got[...])
    right = jnp.where(core == 0, got[...], own[...])
    rows, cols = left.shape
    square = (left * left + right * right).reshape(rows // ks, ks, cols)
    scale = lax.rsqrt(jnp.sum(square, axis=(1, 2), keepdims=True) / (2 * ks * cols) + eps_mean)
    for t, part in enumerate((left, right)):
        scaled = (part.reshape(rows // ks, ks, cols) * scale).reshape(rows, cols)
        flatten(scaled, ks, out, scratch, t * ks * cols)


def score_kernel(kinds, c_ref, *refs):
    probes, (own_ref, send_ref) = refs[:-2], refs[-2:]
    me = lax.axis_index("fsdp")
    cands = c_ref[...]
    per = cands.shape[0] // 2
    held = jnp.concatenate([ref[...] for ref in probes], axis=0)
    width = held.shape[0]
    mixed = dot_last(jnp.concatenate([cands, held], axis=0), held)
    scores, gram = mixed[: 2 * per], mixed[2 * per :]

    def diagonal(square, axis):
        rows = lax.broadcasted_iota(jnp.int32, square.shape, 0)
        cols = lax.broadcasted_iota(jnp.int32, square.shape, 1)
        return jnp.sum(jnp.where(rows == cols, square, 0.0), axis=axis, keepdims=True)

    rows = jnp.concatenate([scores, jnp.broadcast_to(diagonal(gram, 0), scores.shape)], axis=0)
    group = lax.broadcasted_iota(jnp.int32, rows.shape, 1) // per
    placed = jnp.zeros(rows.shape, jnp.float32)
    for g in range(width // per):
        block = jnp.concatenate([rows[:, g * per : (g + 1) * per]] * (width // per), axis=1)
        placed = jnp.where(group == (me ^ kinds[g // 2] ^ (g % 2)), block, placed)
    squares = jnp.broadcast_to(diagonal(dot_last(cands, cands), 1), (2 * per, width))
    for i, ref in enumerate((own_ref, send_ref)):
        ref[:per, :] = placed[i * per : (i + 1) * per]
        ref[per : 2 * per, :] = placed[2 * per : 3 * per]
        ref[2 * per :, :] = squares[i * per : (i + 1) * per]


def final_kernel(entries, own, got, out):
    total = own[...] + got[...]
    per = out.shape[0]
    scale = lax.rsqrt(total[per:] / entries + eps_mean)
    out[...] = total[:per] * scale[:per] * scale[per:] / entries


def swap(x, k, axis, size):
    return lax.ppermute(x, axis, [(i, i ^ k) for i in range(size)])


def fast_body(n, planes, c_x, c_m, c_len, p_x, p_m, p_len, down, up, sketch_in, sketch_out, rank_down, rank_up):
    examples, seq, model = c_x.shape
    value = c_m.shape[2]
    ks, kp = rank_down.shape[1], sketch_in.shape[1]
    s_rows, o_rows = sketch_in.shape[0], sketch_out.shape[0]
    t_rows = (s_rows // kp + 1) * ks
    sw = functools.partial(swap, axis="fsdp", size=n)

    def along(x, second):
        pairs = []
        for i in range(n):
            for z in range(planes):
                way = first_way(i % 2, z)
                pairs.append((i * planes + z, (i ^ (6 - way if second else way)) * planes + z))
        return lax.ppermute(x, ("fsdp", "dp"), pairs)

    def array(*shape, dtype=jnp.bfloat16):
        return jax.ShapeDtypeStruct(shape, dtype)

    def kernel(f, name, outs, operands, in_specs=None, scratch=(), limit=8):
        return pl.pallas_call(
            f,
            out_shape=outs,
            in_specs=in_specs or [VMEM] * len(operands),
            out_specs=(VMEM,) * len(outs) if isinstance(outs, tuple) else VMEM,
            scratch_shapes=scratch,
            compiler_params=pltpu.CompilerParams(vmem_limit_bytes=limit * MIB),
            cost_estimate=SHORT,
            name=name,
        )(*operands)

    flat = (examples * seq, model)
    flat_m = (examples * seq, value)
    rows = 2 * examples * seq
    beside, part = s_rows * 3 // 8 // 128 * 128, s_rows // 2
    tail = s_rows - beside - part
    extra, last, x, m, live, c_cols, p_cols = kernel(
        functools.partial(prepare_kernel, n, seq),
        "prepare",
        (
            array(o_rows + t_rows, kp),
            array(tail, kp),
            array(rows, model),
            array(rows, value),
            array(2, 16, rows // 2),
            array(rows // 2, (model + value) // 2),
            array(rows // 2, (model + value) // 2),
        ),
        in_hbm(
            down, up, rank_down.T, rank_up.T, sketch_in, sketch_out,
            c_x.reshape(flat), c_m.reshape(flat_m), c_len, p_x.reshape(flat), p_m.reshape(flat_m), p_len,
        ),
        in_specs=[HBM] * 12,
        scratch=[
            pltpu.VMEM(down.shape, down.dtype),
            pltpu.VMEM(up.shape, up.dtype),
            pltpu.VMEM(rank_down.shape[::-1], rank_down.dtype),
            pltpu.VMEM(rank_up.shape[::-1], rank_up.dtype),
            pltpu.SMEM(c_len.shape, c_len.dtype),
            pltpu.SMEM(p_len.shape, p_len.dtype),
            pltpu.SemaphoreType.DMA((8 + 4 * examples,)),
        ],
    )

    f32 = jnp.float32
    here, there, both = (0,), (1,), (0, 1)
    own, second, own_sums, own_small = kernel(
        functools.partial(
            own_kernel, n, ks,
            ((0, 0, (0, 0, here), 1, 0, o_rows), (1, 0, (0, 0, here), 0, 0, s_rows)),
            ((0, o_rows, (0, 0, here)),),
        ),
        "own_products",
        (
            array(s_rows, kp),
            array(part + o_rows + t_rows, kp),
            array(2, 2, rows // 2, kp, dtype=f32),
            array(2, 2, rows // 2, ks, dtype=f32),
        ),
        (*in_hbm(sketch_in), extra, x, m),
        in_specs=[HBM] + [VMEM] * 3,
        scratch=[pltpu.SemaphoreType.DMA((2,))],
    )

    first, first_extra = along(sketch_in, False), along(extra, False)
    second = along(second, True)
    c_xo, p_xo = sw(c_cols, 1), sw(p_cols, 1)

    more = along(jnp.concatenate([first, first_extra, last]), True)
    rest = swap(first[:beside], 1, "dp", planes)
    second_other = sw(second, 1)

    t_at = part + o_rows
    early_places = (
        (0, 0, (0, 0, there), 1, 0, o_rows), (1, 0, (1, 0, both), 0, 0, s_rows), (2, 0, (1, 0, both), 1, 0, o_rows),
        (3, 0, (2, 0, here), 0, beside, part), (3, part, (2, 0, here), 1, 0, o_rows),
        (4, 0, (2, 1, here), 0, beside, part), (4, part, (2, 1, here), 1, 0, o_rows),
        (5, 0, (0, 0, there), 0, 0, s_rows),
    )
    early_tables = (
        (0, o_rows, (0, 0, there)), (2, o_rows, (1, 0, both)), (3, t_at, (2, 0, here)), (4, t_at, (2, 1, here)),
    )
    sums, small = kernel(
        functools.partial(early_kernel, n, ks, early_places, early_tables),
        "early_products",
        (array(2, 2, 2, rows // 2, kp, dtype=f32), array(2, 2, 2, rows // 2, ks, dtype=f32)),
        (x, m, c_xo, p_xo, own_sums, own_small, extra, first, first_extra, second, second_other, own),
    )
    late_places = (
        (0, 0, (3, 0, both), 0, 0, s_rows), (0, s_rows, (3, 0, both), 1, 0, o_rows),
        (0, s_rows + o_rows + t_rows, (2, 0, both), 0, beside + part, tail),
        (1, 0, (2, 0, both), 0, 0, beside),
    )

    def late(side, name):
        keep, keep_small, out = kernel(
            functools.partial(late_kernel, n, ks, side, late_places, ((0, s_rows + o_rows, (3, 0, both)),)),
            name,
            (array(rows, kp, dtype=f32), array(ks, rows, dtype=f32), array(rows + 2 * ks + 16, kp)),
            (x, m, (c_xo, p_xo)[side], live, sums, small, more, rest),
            scratch=[pltpu.VMEM((2, rows, kp), f32), pltpu.VMEM((2, ks, rows), f32)],
        )
        return keep, keep_small, sw(out, 1)

    total = 2 * examples * ks
    side = array(2 * examples, ks * kp)

    def scratch(count):
        return [pltpu.VMEM((kp // 128, count, 128), f32)]

    p_side = kernel(
        functools.partial(probe_kernel, seq), "probe_sides", side, (*late(1, "probe_products"), live), scratch=scratch(total)
    )
    grads = array(total // 2, kp, dtype=f32)
    c_side, c_grads, c_send = kernel(
        functools.partial(candidate_kernel, seq),
        "candidate_sides",
        (side, grads, grads),
        (*late(0, "candidate_products"), live),
        scratch=scratch(total),
    )
    c_feat = kernel(
        functools.partial(feature_kernel, ks),
        "candidate_features",
        array(examples, 2 * ks * kp),
        (c_grads, sw(c_send, 1)),
        scratch=scratch(total // 2),
    )

    kinds = (0, 6, 4, 2)
    got = [sw(p_side, k) for k in kinds[1:]]
    c_side, *got = lax.optimization_barrier((c_side, *got))
    part = array(3 * examples, n * examples, dtype=f32)
    scores, to_other = kernel(
        functools.partial(score_kernel, kinds), "score_shares", (part, part), (c_side, p_side, *got)
    )
    scores = kernel(
        functools.partial(final_kernel, 2 * ks * kp),
        "scores",
        array(examples, n * examples, dtype=f32),
        (scores, sw(to_other, 1)),
    )
    return scores, c_feat


def plain_features(x, m, lengths, down, up, sketch_in, sketch_out, rank_down, rank_up):
    examples, seq, model = x.shape
    ks, kp = rank_down.shape[1], sketch_in.shape[1]
    live = (lax.broadcasted_iota(jnp.int32, (examples, seq), 1) < lengths[:, None]).astype(m.dtype)
    masked = (m * live[:, :, None]).reshape(examples * seq, -1)
    rows = x.reshape(examples * seq, model)
    grad_rows = dot(masked, up).astype(jnp.bfloat16)
    outward = dot(masked, sketch_out).astype(jnp.bfloat16)
    down_round = dot(rows, down).astype(jnp.bfloat16)
    inward = dot(rows, sketch_in).astype(jnp.bfloat16)
    left_small = dot(grad_rows, rank_down).astype(jnp.bfloat16)
    right_small = dot(down_round, rank_up).astype(jnp.bfloat16)

    def outer(small, wide):
        return jnp.einsum(
            "esk,esp->ekp",
            small.reshape(examples, seq, ks),
            wide.reshape(examples, seq, kp),
            preferred_element_type=jnp.float32,
        )

    joined = jnp.concatenate([outer(left_small, inward), outer(right_small, outward)], axis=1)
    joined = joined.reshape(examples, 2 * ks * kp)
    scale = lax.rsqrt(jnp.mean(joined * joined, axis=1, keepdims=True) + eps_mean)
    return (joined * scale).astype(jnp.bfloat16)


def plain_body(c_x, c_m, c_len, p_x, p_m, p_len, down, up, sketch_in, sketch_out, rank_down, rank_up):
    weights = [
        lax.all_gather(w, "fsdp", axis=0, tiled=True) for w in (down, up, sketch_in, sketch_out)
    ]
    p_feat = plain_features(p_x, p_m, p_len, *weights, rank_down, rank_up)
    c_feat = plain_features(c_x, c_m, c_len, *weights, rank_down, rank_up)
    every = lax.all_gather(p_feat, "fsdp", axis=0, tiled=True)
    return dot(c_feat, every.T) / c_feat.shape[1], c_feat


def solution(mesh):
    n, planes = mesh.shape["fsdp"], mesh.shape["dp"]
    rows = P(("dp", "fsdp"), None)
    cube = P(("dp", "fsdp"), None, None)
    line = P(("dp", "fsdp"))
    shard = P("fsdp", None)
    in_specs = (cube, cube, line, cube, cube, line, shard, shard, shard, shard, P(), P())

    def body(*args):
        if n == 1 << 3 and planes % 2 == 0:
            return fast_body(n, planes, *args)
        return plain_body(*args)

    return jax.shard_map(body, mesh=mesh, in_specs=in_specs, out_specs=(rows, rows), check_vma=False)
```

```python
import functools

import jax
import jax.numpy as jnp
from jax import lax
from jax.experimental import pallas as pl
from jax.experimental.pallas import tpu as pltpu
from jax.sharding import PartitionSpec as P

eps_mean = 1e-06
LAST = (((1,), (1,)), ((), ()))
VMEM = pl.BlockSpec(memory_space=pltpu.VMEM)
SMEM = pl.BlockSpec(memory_space=pltpu.SMEM)
HBM = pl.BlockSpec(memory_space=pltpu.HBM)
MIB = 1 << 20
SHORT = pl.CostEstimate(flops=1, bytes_accessed=1, transcendentals=0)


def in_hbm(*arrays):
    return tuple(pltpu.with_memory_space_constraint(a, pltpu.HBM) for a in arrays)


def dot(a, b):
    return jnp.dot(a, b, preferred_element_type=jnp.float32)


def dot_last(a, b):
    return lax.dot_general(a, b, LAST, preferred_element_type=jnp.float32)


def split_two(x):
    high = x.astype(jnp.bfloat16)
    return high, (x - high.astype(jnp.float32)).astype(jnp.bfloat16)


def first_way(core, plane):
    return 2 + 2 * ((core + plane) % 2)


def partner(me, kind, plane):
    first = first_way(me % 2, plane)
    return me ^ (0, first, 6 - first, 6)[kind]


def there_at(kd, ku):
    return (0, kd, None, 2 * kd), tuple(3 * kd + kind * ku for kind in range(4))


def prepare_kernel(
    n, seq, down_hbm, up_hbm, rank_down_hbm, rank_up_hbm, out_hbm,
    c_x_hbm, c_m_hbm, c_len_hbm, p_x_hbm, p_m_hbm, p_len_hbm,
    extra_ref, x_ref, m_ref, live_ref, c_send, p_send,
    down_ref, up_ref, rank_down_ref, rank_up_ref, c_len, p_len, sems,
):
    o_rows, half = out_hbm.shape[0], c_x_hbm.shape[0]
    moves = (
        (down_hbm, down_ref),
        (up_hbm, up_ref),
        (rank_down_hbm, rank_down_ref),
        (rank_up_hbm, rank_up_ref),
        (c_len_hbm, c_len),
        (p_len_hbm, p_len),
        (out_hbm, extra_ref.at[pl.ds(0, o_rows)]),
    )
    moves += tuple(
        (source.at[pl.ds(e * seq, seq)], to.at[pl.ds(base + e * seq, seq)])
        for source, to, base in ((c_m_hbm, m_ref, 0), (c_x_hbm, x_ref, 0), (p_m_hbm, m_ref, half), (p_x_hbm, x_ref, half))
        for e in range(half // seq)
    )
    copies = [pltpu.make_async_copy(a, b, sems.at[i]) for i, (a, b) in enumerate(moves)]
    for copy in copies:
        copy.start()
    for copy in copies[:6]:
        copy.wait()
    down_table = dot_last(rank_up_ref[...], down_ref[...]).astype(jnp.bfloat16)
    up_table = dot_last(rank_down_ref[...], up_ref[...]).astype(jnp.bfloat16)
    ks, width = up_table.shape
    lanes = extra_ref.shape[1]
    blocks = down_table.shape[1] // lanes
    for b in range(blocks):
        at = o_rows + b * ks
        extra_ref[at : at + ks, :] = down_table[:, b * lanes : (b + 1) * lanes]
    at = o_rows + blocks * ks
    extra_ref[at:, :] = jnp.zeros((ks, lanes), jnp.bfloat16)
    extra_ref[at:, :width] = up_table
    lane = lax.broadcasted_iota(jnp.int32, live_ref.shape[1:], 1)
    for side, lengths in enumerate((c_len, p_len)):
        live = jnp.zeros(live_ref.shape[1:], jnp.bool_)
        for e in range(half // seq):
            live = live | ((lane >= e * seq) & (lane < e * seq + lengths[e]))
        live_ref[side] = live.astype(jnp.float32).astype(live_ref.dtype)
    other, plane = lax.axis_index("fsdp") ^ 1, lax.axis_index("dp")
    examples = half // seq
    kd, ku = x_ref.shape[1] // n, m_ref.shape[1] // n
    copies[6].wait()
    for side, send_ref in enumerate((c_send, p_send)):
        for sketch, ref, wide in ((1, m_ref, ku), (0, x_ref, kd)):
            for e in range(examples):
                copies[7 + (2 * side + 1 - sketch) * examples + e].wait()
                rows = pl.ds(e * seq, seq)
                for kind, at in enumerate(there_at(kd, ku)[sketch]):
                    if at is not None:
                        first = pl.multiple_of(partner(other, kind, plane) * wide, wide)
                        send_ref[rows, at : at + wide] = ref[pl.ds(side * half + e * seq, seq), pl.ds(first, wide)]


def spans(n, x, m, xo, block, sketch, first, count):
    kind, core, whos = block
    j = partner(lax.axis_index("fsdp") ^ core, kind, lax.axis_index("dp"))
    kd, ku = x.shape[1] // n, m.shape[1] // n
    source, wide = ((x, kd), (m, ku))[sketch]
    for who in whos:
        if who == 0:
            yield who, source[:, pl.ds(pl.multiple_of(j * wide + first, 128), count)]
        else:
            at = there_at(kd, ku)[sketch][kind] + first
            yield who, xo[:, at : at + count]


def small_sums(n, ks, places, x, m, xo, refs):
    ku = m.shape[1] // n
    sums = [[0.0, 0.0], [0.0, 0.0]]
    for r, at, block in places:
        lanes = refs[r].shape[1]
        blocks = x.shape[1] // n // lanes
        up = refs[r][at + blocks * ks : at + (blocks + 1) * ks, :ku]
        for who, rows in spans(n, x, m, xo, block, 1, 0, ku):
            sums[who][0] += dot_last(rows, up)
        table = jnp.concatenate([refs[r][at + b * ks : at + (b + 1) * ks, :] for b in range(blocks)], axis=1)
        for who, rows in spans(n, x, m, xo, block, 0, 0, blocks * lanes):
            sums[who][1] += dot_last(rows, table)
    return sums


def products(n, places, x, m, xo, refs):
    sums = [[0.0, 0.0], [0.0, 0.0]]
    for ref, row, block, sketch, first, count in places:
        piece = refs[ref][row : row + count, :]
        for who, rows in spans(n, x, m, xo, block, sketch, first, count):
            sums[who][sketch] += dot(rows, piece)
    return sums


def own_kernel(n, ks, places, tables, in_hbm, extra, x, m, own, second, sums_ref, small_ref, sems):
    part = first = in_hbm.shape[0] // 2
    o_rows = m.shape[1] // n
    copies = [
        pltpu.make_async_copy(in_hbm, own, sems.at[0]),
        pltpu.make_async_copy(in_hbm.at[pl.ds(first, part)], second.at[pl.ds(0, part)], sems.at[1]),
    ]
    for copy in copies:
        copy.start()
    second[part : second.shape[0] - o_rows, :] = extra[o_rows:, :]
    second[second.shape[0] - o_rows :, :] = extra[:o_rows, :]
    half = x.shape[0] // 2
    views = [(x.at[pl.ds(side * half, half)], m.at[pl.ds(side * half, half)], None) for side in range(2)]
    for side in range(2):
        small = small_sums(n, ks, tables, *views[side], (extra,))
        for t in range(2):
            small_ref[side, t] = small[0][t]
    for copy in copies:
        copy.wait()
    for side in range(2):
        sums = products(n, places, *views[side], (extra, own))
        for t in range(2):
            sums_ref[side, t] = sums[0][t]


def early_kernel(n, ks, places, tables, x, m, c_xo, p_xo, own_sums, own_small, *refs):
    refs, (sums_ref, small_ref) = refs[:-2], refs[-2:]
    half = c_xo.shape[0]
    for side, xo in enumerate((c_xo, p_xo)):
        rows = pl.ds(side * half, half)
        views = x.at[rows], m.at[rows], xo
        small = small_sums(n, ks, tables, *views, refs)
        sums = products(n, places, *views, refs)
        for t in range(2):
            small_ref[side, 0, t] = small[0][t] + own_small[side, t]
            small_ref[side, 1, t] = small[1][t]
            sums_ref[side, 0, t] = sums[0][t] + own_sums[side, t]
            sums_ref[side, 1, t] = sums[1][t]


def late_kernel(n, ks, side, places, tables, x, m, xo, live, sums, early_small, *refs):
    refs, (keep, keep_small, send, wide, narrow) = refs[:-5], refs[-5:]
    core = lax.axis_index("fsdp") % 2
    half = x.shape[0] // 2
    rows = pl.ds(side * half, half)
    views = x.at[rows], m.at[rows], xo
    late = products(n, places, *views, refs)
    late_small = small_sums(n, ks, tables, *views, refs)
    for t in range(2):
        for who in range(2):
            wide[t, who * half : (who + 1) * half, :] = late[who][t] + sums[side, who, t]
        both = [late_small[who][t] + early_small[side, who, t] for who in range(2)]
        narrow[t] = jnp.concatenate(both, axis=0).T
    keep[...] = wide[core]
    keep_small[...] = narrow[core]
    for who in range(2):
        first = (1 - who) * half
        send[who * half : (who + 1) * half, :] = wide[1 - core, first : first + half, :].astype(jnp.bfloat16)
    small = narrow[1 - core]
    high, low = split_two(jnp.concatenate([small[:, half:], small[:, :half]], axis=1))
    send[2 * half : 2 * half + ks, :] = high
    send[2 * half + ks : 2 * half + 2 * ks, :] = low
    send[2 * half + 2 * ks :, :half] = live[side]
    send[2 * half + 2 * ks :, half:] = live[side]


def gradients(seq, side, keep, keep_small, got, live):
    rows, ks = keep.shape[0], keep_small.shape[0]
    high, low = (got[at : at + ks, :].astype(jnp.float32) for at in (rows, rows + ks))
    there = got[rows + 2 * ks : rows + 2 * ks + 1, rows // 2 :]
    lives = jnp.concatenate([live[side, :1, :].astype(jnp.float32), there.astype(jnp.float32)], axis=1)
    small = jnp.where(lives > 0, keep_small[...] + high + low, 0.0)
    count = rows // seq
    tiled = jnp.concatenate([small] * count, axis=0)
    e_row = lax.broadcasted_iota(jnp.int32, tiled.shape, 0) // ks
    e_col = lax.broadcasted_iota(jnp.int32, tiled.shape, 1) // seq
    factor = jnp.where(e_row == e_col, tiled, 0.0).astype(jnp.bfloat16)
    total = keep[...] + got[:rows, :].astype(jnp.float32)
    return dot(factor, total.astype(jnp.bfloat16))


def flatten(grads, ks, out, scratch, base=0):
    cols, lanes = grads.shape[1], scratch.shape[2]
    for b in range(cols // lanes):
        scratch[b] = grads[:, b * lanes : (b + 1) * lanes]
    for k in range(ks):
        for b in range(cols // lanes):
            at = base + k * cols + b * lanes
            rows = pl.ds(k, grads.shape[0] // ks, stride=ks)
            out[:, at : at + lanes] = scratch[b, rows, :].astype(out.dtype)


def probe_kernel(seq, keep, keep_small, got, live, out, scratch):
    flatten(gradients(seq, 1, keep, keep_small, got, live), keep_small.shape[0], out, scratch)


def candidate_kernel(seq, keep, keep_small, got, live, out, own, send, scratch):
    grads = gradients(seq, 0, keep, keep_small, got, live)
    flatten(grads, keep_small.shape[0], out, scratch)
    half = grads.shape[0] // 2
    own[...] = grads[:half]
    send[...] = grads[half:]


def feature_kernel(ks, own, got, out, scratch):
    core = lax.axis_index("fsdp") % 2
    left = jnp.where(core == 0, own[...], got[...])
    right = jnp.where(core == 0, got[...], own[...])
    rows, cols = left.shape
    square = (left * left + right * right).reshape(rows // ks, ks, cols)
    scale = lax.rsqrt(jnp.sum(square, axis=(1, 2), keepdims=True) / (2 * ks * cols) + eps_mean)
    for t, part in enumerate((left, right)):
        scaled = (part.reshape(rows // ks, ks, cols) * scale).reshape(rows, cols)
        flatten(scaled, ks, out, scratch, t * ks * cols)


def score_kernel(kinds, c_ref, *refs):
    probes, (own_ref, send_ref) = refs[:-2], refs[-2:]
    me = lax.axis_index("fsdp")
    cands = c_ref[...]
    per = cands.shape[0] // 2
    held = jnp.concatenate([ref[...] for ref in probes], axis=0)
    width = held.shape[0]
    mixed = dot_last(jnp.concatenate([cands, held], axis=0), held)
    scores, gram = mixed[: 2 * per], mixed[2 * per :]

    def diagonal(square, axis):
        rows = lax.broadcasted_iota(jnp.int32, square.shape, 0)
        cols = lax.broadcasted_iota(jnp.int32, square.shape, 1)
        return jnp.sum(jnp.where(rows == cols, square, 0.0), axis=axis, keepdims=True)

    rows = jnp.concatenate([scores, jnp.broadcast_to(diagonal(gram, 0), scores.shape)], axis=0)
    group = lax.broadcasted_iota(jnp.int32, rows.shape, 1) // per
    placed = jnp.zeros(rows.shape, jnp.float32)
    for g in range(width // per):
        block = jnp.concatenate([rows[:, g * per : (g + 1) * per]] * (width // per), axis=1)
        placed = jnp.where(group == (me ^ kinds[g // 2] ^ (g % 2)), block, placed)
    squares = jnp.broadcast_to(diagonal(dot_last(cands, cands), 1), (2 * per, width))
    for i, ref in enumerate((own_ref, send_ref)):
        ref[:per, :] = placed[i * per : (i + 1) * per]
        ref[per : 2 * per, :] = placed[2 * per : 3 * per]
        ref[2 * per :, :] = squares[i * per : (i + 1) * per]


def final_kernel(entries, own, got, out):
    total = own[...] + got[...]
    per = out.shape[0]
    scale = lax.rsqrt(total[per:] / entries + eps_mean)
    out[...] = total[:per] * scale[:per] * scale[per:] / entries


def swap(x, k, axis, size):
    return lax.ppermute(x, axis, [(i, i ^ k) for i in range(size)])


def fast_body(n, planes, c_x, c_m, c_len, p_x, p_m, p_len, down, up, sketch_in, sketch_out, rank_down, rank_up):
    examples, seq, model = c_x.shape
    value = c_m.shape[2]
    ks, kp = rank_down.shape[1], sketch_in.shape[1]
    s_rows, o_rows = sketch_in.shape[0], sketch_out.shape[0]
    t_rows = (s_rows // kp + 1) * ks
    sw = functools.partial(swap, axis="fsdp", size=n)

    def along(x, second):
        pairs = []
        for i in range(n):
            for z in range(planes):
                way = first_way(i % 2, z)
                pairs.append((i * planes + z, (i ^ (6 - way if second else way)) * planes + z))
        return lax.ppermute(x, ("fsdp", "dp"), pairs)

    def array(*shape, dtype=jnp.bfloat16):
        return jax.ShapeDtypeStruct(shape, dtype)

    def kernel(f, name, outs, operands, in_specs=None, scratch=(), limit=8):
        return pl.pallas_call(
            f,
            out_shape=outs,
            in_specs=in_specs or [VMEM] * len(operands),
            out_specs=(VMEM,) * len(outs) if isinstance(outs, tuple) else VMEM,
            scratch_shapes=scratch,
            compiler_params=pltpu.CompilerParams(vmem_limit_bytes=limit * MIB),
            cost_estimate=SHORT,
            name=name,
        )(*operands)

    flat = (examples * seq, model)
    flat_m = (examples * seq, value)
    rows = 2 * examples * seq
    beside = part = s_rows // 2
    extra, x, m, live, c_cols, p_cols = kernel(
        functools.partial(prepare_kernel, n, seq),
        "prepare",
        (
            array(o_rows + t_rows, kp),
            array(rows, model),
            array(rows, value),
            array(2, 16, rows // 2),
            array(rows // 2, 3 * s_rows + 4 * o_rows),
            array(rows // 2, 3 * s_rows + 4 * o_rows),
        ),
        in_hbm(
            down, up, rank_down.T, rank_up.T, sketch_out,
            c_x.reshape(flat), c_m.reshape(flat_m), c_len, p_x.reshape(flat), p_m.reshape(flat_m), p_len,
        ),
        in_specs=[HBM] * 11,
        scratch=[
            pltpu.VMEM(down.shape, down.dtype),
            pltpu.VMEM(up.shape, up.dtype),
            pltpu.VMEM(rank_down.shape[::-1], rank_down.dtype),
            pltpu.VMEM(rank_up.shape[::-1], rank_up.dtype),
            pltpu.SMEM(c_len.shape, c_len.dtype),
            pltpu.SMEM(p_len.shape, p_len.dtype),
            pltpu.SemaphoreType.DMA((7 + 4 * examples,)),
        ],
    )

    f32 = jnp.float32
    here, there, both = (0,), (1,), (0, 1)
    own, second, own_sums, own_small = kernel(
        functools.partial(
            own_kernel, n, ks,
            ((0, 0, (0, 0, here), 1, 0, o_rows), (1, 0, (0, 0, here), 0, 0, s_rows)),
            ((0, o_rows, (0, 0, here)),),
        ),
        "own_products",
        (
            array(s_rows, kp),
            array(part + o_rows + t_rows, kp),
            array(2, 2, rows // 2, kp, dtype=f32),
            array(2, 2, rows // 2, ks, dtype=f32),
        ),
        (*in_hbm(sketch_in), extra, x, m),
        in_specs=[HBM] + [VMEM] * 3,
        scratch=[pltpu.SemaphoreType.DMA((2,))],
    )

    first, first_extra = along(sketch_in, False), along(extra, False)
    second = along(second, True)
    c_xo, p_xo = sw(c_cols, 1), sw(p_cols, 1)

    more = along(jnp.concatenate([first, first_extra]), True)
    rest = swap(first[:beside], 1, "dp", planes)
    second_other, rest_other = sw(second[: part + t_rows], 1), sw(rest, 1)

    o_at = part + t_rows
    early_places = (
        (0, 0, (0, 0, there), 1, 0, o_rows), (1, 0, (1, 0, both), 0, 0, s_rows), (2, 0, (1, 0, both), 1, 0, o_rows),
        (3, 0, (2, 0, here), 0, beside, part), (4, 0, (2, 1, here), 0, beside, part),
        (3, o_at, (2, 0, both), 1, 0, o_rows), (5, 0, (0, 0, there), 0, 0, s_rows),
    )
    early_tables = (
        (0, o_rows, (0, 0, there)), (2, o_rows, (1, 0, both)), (3, part, (2, 0, here)), (4, part, (2, 1, here)),
    )
    sums, small = kernel(
        functools.partial(early_kernel, n, ks, early_places, early_tables),
        "early_products",
        (array(2, 2, 2, rows // 2, kp, dtype=f32), array(2, 2, 2, rows // 2, ks, dtype=f32)),
        (x, m, c_xo, p_xo, own_sums, own_small, extra, first, first_extra, second, second_other, own),
    )
    late_places = (
        (0, 0, (3, 0, both), 0, 0, s_rows), (0, s_rows, (3, 0, both), 1, 0, o_rows),
        (1, 0, (2, 0, here), 0, 0, beside), (2, 0, (2, 1, here), 0, 0, beside),
    )

    def late(side, name):
        keep, keep_small, out = kernel(
            functools.partial(late_kernel, n, ks, side, late_places, ((0, s_rows + o_rows, (3, 0, both)),)),
            name,
            (array(rows, kp, dtype=f32), array(ks, rows, dtype=f32), array(rows + 2 * ks + 16, kp)),
            (x, m, (c_xo, p_xo)[side], live, sums, small, more, rest, rest_other),
            scratch=[pltpu.VMEM((2, rows, kp), f32), pltpu.VMEM((2, ks, rows), f32)],
        )
        return keep, keep_small, sw(out, 1)

    total = 2 * examples * ks
    side = array(2 * examples, ks * kp)

    def scratch(count):
        return [pltpu.VMEM((kp // 128, count, 128), f32)]

    p_side = kernel(
        functools.partial(probe_kernel, seq), "probe_sides", side, (*late(1, "probe_products"), live), scratch=scratch(total)
    )
    grads = array(total // 2, kp, dtype=f32)
    c_side, c_grads, c_send = kernel(
        functools.partial(candidate_kernel, seq),
        "candidate_sides",
        (side, grads, grads),
        (*late(0, "candidate_products"), live),
        scratch=scratch(total),
    )
    c_feat = kernel(
        functools.partial(feature_kernel, ks),
        "candidate_features",
        array(examples, 2 * ks * kp),
        (c_grads, sw(c_send, 1)),
        scratch=scratch(total // 2),
    )

    kinds = (0, 6, 4, 2)
    got = [sw(p_side, k) for k in kinds[1:]]
    c_side, *got = lax.optimization_barrier((c_side, *got))
    part = array(3 * examples, n * examples, dtype=f32)
    scores, to_other = kernel(
        functools.partial(score_kernel, kinds), "score_shares", (part, part), (c_side, p_side, *got)
    )
    scores = kernel(
        functools.partial(final_kernel, 2 * ks * kp),
        "scores",
        array(examples, n * examples, dtype=f32),
        (scores, sw(to_other, 1)),
    )
    return scores, c_feat


def plain_features(x, m, lengths, down, up, sketch_in, sketch_out, rank_down, rank_up):
    examples, seq, model = x.shape
    ks, kp = rank_down.shape[1], sketch_in.shape[1]
    live = (lax.broadcasted_iota(jnp.int32, (examples, seq), 1) < lengths[:, None]).astype(m.dtype)
    masked = (m * live[:, :, None]).reshape(examples * seq, -1)
    rows = x.reshape(examples * seq, model)
    grad_rows = dot(masked, up).astype(jnp.bfloat16)
    outward = dot(masked, sketch_out).astype(jnp.bfloat16)
    down_round = dot(rows, down).astype(jnp.bfloat16)
    inward = dot(rows, sketch_in).astype(jnp.bfloat16)
    left_small = dot(grad_rows, rank_down).astype(jnp.bfloat16)
    right_small = dot(down_round, rank_up).astype(jnp.bfloat16)

    def outer(small, wide):
        return jnp.einsum(
            "esk,esp->ekp",
            small.reshape(examples, seq, ks),
            wide.reshape(examples, seq, kp),
            preferred_element_type=jnp.float32,
        )

    joined = jnp.concatenate([outer(left_small, inward), outer(right_small, outward)], axis=1)
    joined = joined.reshape(examples, 2 * ks * kp)
    scale = lax.rsqrt(jnp.mean(joined * joined, axis=1, keepdims=True) + eps_mean)
    return (joined * scale).astype(jnp.bfloat16)


def plain_body(c_x, c_m, c_len, p_x, p_m, p_len, down, up, sketch_in, sketch_out, rank_down, rank_up):
    weights = [
        lax.all_gather(w, "fsdp", axis=0, tiled=True) for w in (down, up, sketch_in, sketch_out)
    ]
    p_feat = plain_features(p_x, p_m, p_len, *weights, rank_down, rank_up)
    c_feat = plain_features(c_x, c_m, c_len, *weights, rank_down, rank_up)
    every = lax.all_gather(p_feat, "fsdp", axis=0, tiled=True)
    return dot(c_feat, every.T) / c_feat.shape[1], c_feat


def solution(mesh):
    n, planes = mesh.shape["fsdp"], mesh.shape["dp"]
    rows = P(("dp", "fsdp"), None)
    cube = P(("dp", "fsdp"), None, None)
    line = P(("dp", "fsdp"))
    shard = P("fsdp", None)
    in_specs = (cube, cube, line, cube, cube, line, shard, shard, shard, shard, P(), P())

    def body(*args):
        if n == 1 << 3 and planes % 2 == 0:
            return fast_body(n, planes, *args)
        return plain_body(*args)

    return jax.shard_map(body, mesh=mesh, in_specs=in_specs, out_specs=(rows, rows), check_vma=False)
```

```python
import functools

import jax
import jax.numpy as jnp
from jax import lax
from jax.experimental import pallas as pl
from jax.experimental.pallas import tpu as pltpu
from jax.sharding import PartitionSpec as P

eps_mean = 1e-06
LAST = (((1,), (1,)), ((), ()))
VMEM = pl.BlockSpec(memory_space=pltpu.VMEM)
SMEM = pl.BlockSpec(memory_space=pltpu.SMEM)
HBM = pl.BlockSpec(memory_space=pltpu.HBM)
MIB = 1 << 20
SHORT = pl.CostEstimate(flops=1, bytes_accessed=1, transcendentals=0)


def in_hbm(*arrays):
    return tuple(pltpu.with_memory_space_constraint(a, pltpu.HBM) for a in arrays)


def dot(a, b):
    return jnp.dot(a, b, preferred_element_type=jnp.float32)


def dot_last(a, b):
    return lax.dot_general(a, b, LAST, preferred_element_type=jnp.float32)


def split_two(x):
    high = x.astype(jnp.bfloat16)
    return high, (x - high.astype(jnp.float32)).astype(jnp.bfloat16)


def first_way(core, plane):
    return 2 + 2 * ((core + plane) % 2)


def partner(me, kind, plane):
    first = first_way(me % 2, plane)
    return me ^ (0, first, 6 - first, 6)[kind]


def there_at(kd, ku):
    return (0, kd, None, 2 * kd), tuple(3 * kd + kind * ku for kind in range(4))


def prepare_kernel(
    n, seq, down_hbm, up_hbm, rank_down_hbm, rank_up_hbm, out_hbm,
    c_x_hbm, c_m_hbm, c_len_hbm, p_x_hbm, p_m_hbm, p_len_hbm,
    extra_ref, x_ref, m_ref, live_ref, c_send, p_send,
    down_ref, up_ref, rank_down_ref, rank_up_ref, c_len, p_len, sems,
):
    o_rows, half = out_hbm.shape[0], c_x_hbm.shape[0]
    moves = (
        (down_hbm, down_ref),
        (up_hbm, up_ref),
        (rank_down_hbm, rank_down_ref),
        (rank_up_hbm, rank_up_ref),
        (c_len_hbm, c_len),
        (p_len_hbm, p_len),
        (out_hbm, extra_ref.at[pl.ds(0, o_rows)]),
    )
    moves += tuple(
        (source.at[pl.ds(e * seq, seq)], to.at[pl.ds(base + e * seq, seq)])
        for source, to, base in ((c_m_hbm, m_ref, 0), (c_x_hbm, x_ref, 0), (p_m_hbm, m_ref, half), (p_x_hbm, x_ref, half))
        for e in range(half // seq)
    )
    copies = [pltpu.make_async_copy(a, b, sems.at[i]) for i, (a, b) in enumerate(moves)]
    for copy in copies:
        copy.start()
    for copy in copies[:6]:
        copy.wait()
    down_table = dot_last(rank_up_ref[...], down_ref[...]).astype(jnp.bfloat16)
    up_table = dot_last(rank_down_ref[...], up_ref[...]).astype(jnp.bfloat16)
    ks, width = up_table.shape
    lanes = extra_ref.shape[1]
    blocks = down_table.shape[1] // lanes
    for b in range(blocks):
        at = o_rows + b * ks
        extra_ref[at : at + ks, :] = down_table[:, b * lanes : (b + 1) * lanes]
    at = o_rows + blocks * ks
    extra_ref[at:, :] = jnp.zeros((ks, lanes), jnp.bfloat16)
    extra_ref[at:, :width] = up_table
    lane = lax.broadcasted_iota(jnp.int32, live_ref.shape[1:], 1)
    for side, lengths in enumerate((c_len, p_len)):
        live = jnp.zeros(live_ref.shape[1:], jnp.bool_)
        for e in range(half // seq):
            live = live | ((lane >= e * seq) & (lane < e * seq + lengths[e]))
        live_ref[side] = live.astype(jnp.float32).astype(live_ref.dtype)
    other, plane = lax.axis_index("fsdp") ^ 1, lax.axis_index("dp")
    examples = half // seq
    kd, ku = x_ref.shape[1] // n, m_ref.shape[1] // n
    copies[6].wait()
    for side, send_ref in enumerate((c_send, p_send)):
        for sketch, ref, wide in ((1, m_ref, ku), (0, x_ref, kd)):
            for e in range(examples):
                copies[7 + (2 * side + 1 - sketch) * examples + e].wait()
                rows = pl.ds(e * seq, seq)
                for kind, at in enumerate(there_at(kd, ku)[sketch]):
                    if at is not None:
                        first = pl.multiple_of(partner(other, kind, plane) * wide, wide)
                        send_ref[rows, at : at + wide] = ref[pl.ds(side * half + e * seq, seq), pl.ds(first, wide)]


def spans(n, x, m, xo, block, sketch, first, count):
    kind, core, whos = block
    j = partner(lax.axis_index("fsdp") ^ core, kind, lax.axis_index("dp"))
    kd, ku = x.shape[1] // n, m.shape[1] // n
    source, wide = ((x, kd), (m, ku))[sketch]
    for who in whos:
        if who == 0:
            yield who, source[:, pl.ds(pl.multiple_of(j * wide + first, 128), count)]
        else:
            at = there_at(kd, ku)[sketch][kind] + first
            yield who, xo[:, at : at + count]


def small_sums(n, ks, places, x, m, xo, refs):
    ku = m.shape[1] // n
    sums = [[0.0, 0.0], [0.0, 0.0]]
    for r, at, block in places:
        lanes = refs[r].shape[1]
        blocks = x.shape[1] // n // lanes
        up = refs[r][at + blocks * ks : at + (blocks + 1) * ks, :ku]
        for who, rows in spans(n, x, m, xo, block, 1, 0, ku):
            sums[who][0] += dot_last(rows, up)
        table = jnp.concatenate([refs[r][at + b * ks : at + (b + 1) * ks, :] for b in range(blocks)], axis=1)
        for who, rows in spans(n, x, m, xo, block, 0, 0, blocks * lanes):
            sums[who][1] += dot_last(rows, table)
    return sums


def products(n, places, x, m, xo, refs):
    sums = [[0.0, 0.0], [0.0, 0.0]]
    for ref, row, block, sketch, first, count in places:
        piece = refs[ref][row : row + count, :]
        for who, rows in spans(n, x, m, xo, block, sketch, first, count):
            sums[who][sketch] += dot(rows, piece)
    return sums


def own_kernel(n, ks, places, tables, in_hbm, extra, x, m, own, second, sums_ref, small_ref, sems):
    part = first = in_hbm.shape[0] // 2
    o_rows = m.shape[1] // n
    load = pltpu.make_async_copy(in_hbm, own, sems.at[0])
    load.start()
    half = x.shape[0] // 2
    views = [(x.at[pl.ds(side * half, half)], m.at[pl.ds(side * half, half)], None) for side in range(2)]
    for side in range(2):
        small = small_sums(n, ks, tables, *views[side], (extra,))
        for t in range(2):
            small_ref[side, t] = small[0][t]
    load.wait()
    for side in range(2):
        sums = products(n, places, *views[side], (extra, own))
        for t in range(2):
            sums_ref[side, t] = sums[0][t]
    fill = pltpu.make_async_copy(in_hbm.at[pl.ds(first, part)], second.at[pl.ds(0, part)], sems.at[1])
    fill.start()
    second[part : second.shape[0] - o_rows, :] = extra[o_rows:, :]
    second[second.shape[0] - o_rows :, :] = extra[:o_rows, :]
    fill.wait()


def early_kernel(n, ks, places, tables, x, m, c_xo, p_xo, own_sums, own_small, *refs):
    refs, (sums_ref, small_ref) = refs[:-2], refs[-2:]
    half = c_xo.shape[0]
    for side, xo in enumerate((c_xo, p_xo)):
        rows = pl.ds(side * half, half)
        views = x.at[rows], m.at[rows], xo
        small = small_sums(n, ks, tables, *views, refs)
        sums = products(n, places, *views, refs)
        for t in range(2):
            small_ref[side, 0, t] = small[0][t] + own_small[side, t]
            small_ref[side, 1, t] = small[1][t]
            sums_ref[side, 0, t] = sums[0][t] + own_sums[side, t]
            sums_ref[side, 1, t] = sums[1][t]


def late_kernel(n, ks, side, places, tables, x, m, xo, live, sums, early_small, *refs):
    refs, (keep, keep_small, send, wide, narrow) = refs[:-5], refs[-5:]
    core = lax.axis_index("fsdp") % 2
    half = x.shape[0] // 2
    rows = pl.ds(side * half, half)
    views = x.at[rows], m.at[rows], xo
    late = products(n, places, *views, refs)
    late_small = small_sums(n, ks, tables, *views, refs)
    for t in range(2):
        for who in range(2):
            wide[t, who * half : (who + 1) * half, :] = late[who][t] + sums[side, who, t]
        both = [late_small[who][t] + early_small[side, who, t] for who in range(2)]
        narrow[t] = jnp.concatenate(both, axis=0).T
    keep[...] = wide[core]
    keep_small[...] = narrow[core]
    for who in range(2):
        first = (1 - who) * half
        send[who * half : (who + 1) * half, :] = wide[1 - core, first : first + half, :].astype(jnp.bfloat16)
    small = narrow[1 - core]
    high, low = split_two(jnp.concatenate([small[:, half:], small[:, :half]], axis=1))
    send[2 * half : 2 * half + ks, :] = high
    send[2 * half + ks : 2 * half + 2 * ks, :] = low
    send[2 * half + 2 * ks :, :half] = live[side]
    send[2 * half + 2 * ks :, half:] = live[side]


def gradients(seq, side, keep, keep_small, got, live):
    rows, ks = keep.shape[0], keep_small.shape[0]
    high, low = (got[at : at + ks, :].astype(jnp.float32) for at in (rows, rows + ks))
    there = got[rows + 2 * ks : rows + 2 * ks + 1, rows // 2 :]
    lives = jnp.concatenate([live[side, :1, :].astype(jnp.float32), there.astype(jnp.float32)], axis=1)
    small = jnp.where(lives > 0, keep_small[...] + high + low, 0.0)
    count = rows // seq
    tiled = jnp.concatenate([small] * count, axis=0)
    e_row = lax.broadcasted_iota(jnp.int32, tiled.shape, 0) // ks
    e_col = lax.broadcasted_iota(jnp.int32, tiled.shape, 1) // seq
    factor = jnp.where(e_row == e_col, tiled, 0.0).astype(jnp.bfloat16)
    total = keep[...] + got[:rows, :].astype(jnp.float32)
    return dot(factor, total.astype(jnp.bfloat16))


def flatten(grads, ks, out, scratch, base=0):
    cols, lanes = grads.shape[1], scratch.shape[2]
    for b in range(cols // lanes):
        scratch[b, : grads.shape[0], :] = grads[:, b * lanes : (b + 1) * lanes]
    for k in range(ks):
        for b in range(cols // lanes):
            at = base + k * cols + b * lanes
            rows = pl.ds(k, grads.shape[0] // ks, stride=ks)
            out[:, at : at + lanes] = scratch[b, rows, :].astype(out.dtype)


def probe_kernel(seq, keep, keep_small, got, live, out, scratch):
    flatten(gradients(seq, 1, keep, keep_small, got, live), keep_small.shape[0], out, scratch)


def candidate_kernel(seq, keep, keep_small, got, live, out, own, send, scratch):
    grads = gradients(seq, 0, keep, keep_small, got, live)
    flatten(grads, keep_small.shape[0], out, scratch)
    half = grads.shape[0] // 2
    own[...] = grads[:half]
    send[...] = grads[half:]


def feature_kernel(ks, own, got, out, scratch):
    core = lax.axis_index("fsdp") % 2
    left = jnp.where(core == 0, own[...], got[...])
    right = jnp.where(core == 0, got[...], own[...])
    rows, cols = left.shape
    square = (left * left + right * right).reshape(rows // ks, ks, cols)
    scale = lax.rsqrt(jnp.sum(square, axis=(1, 2), keepdims=True) / (2 * ks * cols) + eps_mean)
    for t, part in enumerate((left, right)):
        scaled = (part.reshape(rows // ks, ks, cols) * scale).reshape(rows, cols)
        flatten(scaled, ks, out, scratch, t * ks * cols)


def score_kernel(kinds, c_ref, *refs):
    probes, (own_ref, send_ref) = refs[:-2], refs[-2:]
    me, plane = lax.axis_index("fsdp"), lax.axis_index("dp")
    cands = c_ref[...]
    per = cands.shape[0] // 2
    held = jnp.concatenate([ref[...] for ref in probes], axis=0)
    width = held.shape[0]
    mixed = dot_last(jnp.concatenate([cands, held], axis=0), held)
    scores, gram = mixed[: 2 * per], mixed[2 * per :]

    def diagonal(square, axis):
        rows = lax.broadcasted_iota(jnp.int32, square.shape, 0)
        cols = lax.broadcasted_iota(jnp.int32, square.shape, 1)
        return jnp.sum(jnp.where(rows == cols, square, 0.0), axis=axis, keepdims=True)

    rows = jnp.concatenate([scores, jnp.broadcast_to(diagonal(gram, 0), scores.shape)], axis=0)
    group = lax.broadcasted_iota(jnp.int32, rows.shape, 1) // per
    placed = jnp.zeros(rows.shape, jnp.float32)
    for g in range(width // per):
        block = jnp.concatenate([rows[:, g * per : (g + 1) * per]] * (width // per), axis=1)
        placed = jnp.where(group == (partner(me, kinds[g // 2], plane) ^ (g % 2)), block, placed)
    squares = jnp.broadcast_to(diagonal(dot_last(cands, cands), 1), (2 * per, width))
    for i, ref in enumerate((own_ref, send_ref)):
        ref[:per, :] = placed[i * per : (i + 1) * per]
        ref[per : 2 * per, :] = placed[2 * per : 3 * per]
        ref[2 * per :, :] = squares[i * per : (i + 1) * per]


def final_kernel(entries, own, got, out):
    total = own[...] + got[...]
    per = out.shape[0]
    scale = lax.rsqrt(total[per:] / entries + eps_mean)
    out[...] = total[:per] * scale[:per] * scale[per:] / entries


def swap(x, k, axis, size):
    return lax.ppermute(x, axis, [(i, i ^ k) for i in range(size)])


def fast_body(n, planes, c_x, c_m, c_len, p_x, p_m, p_len, down, up, sketch_in, sketch_out, rank_down, rank_up):
    examples, seq, model = c_x.shape
    value = c_m.shape[2]
    ks, kp = rank_down.shape[1], sketch_in.shape[1]
    s_rows, o_rows = sketch_in.shape[0], sketch_out.shape[0]
    t_rows = (s_rows // kp + 1) * ks
    sw = functools.partial(swap, axis="fsdp", size=n)

    def along(x, second):
        pairs = []
        for i in range(n):
            for z in range(planes):
                way = first_way(i % 2, z)
                pairs.append((i * planes + z, (i ^ (6 - way if second else way)) * planes + z))
        return lax.ppermute(x, ("fsdp", "dp"), pairs)

    def array(*shape, dtype=jnp.bfloat16):
        return jax.ShapeDtypeStruct(shape, dtype)

    def kernel(f, name, outs, operands, in_specs=None, scratch=(), limit=8):
        return pl.pallas_call(
            f,
            out_shape=outs,
            in_specs=in_specs or [VMEM] * len(operands),
            out_specs=(VMEM,) * len(outs) if isinstance(outs, tuple) else VMEM,
            scratch_shapes=scratch,
            compiler_params=pltpu.CompilerParams(vmem_limit_bytes=limit * MIB),
            cost_estimate=SHORT,
            name=name,
        )(*operands)

    flat = (examples * seq, model)
    flat_m = (examples * seq, value)
    rows = 2 * examples * seq
    beside = part = s_rows // 2
    extra, x, m, live, c_cols, p_cols = kernel(
        functools.partial(prepare_kernel, n, seq),
        "prepare",
        (
            array(o_rows + t_rows, kp),
            array(rows, model),
            array(rows, value),
            array(2, 16, rows // 2),
            array(rows // 2, 3 * s_rows + 4 * o_rows),
            array(rows // 2, 3 * s_rows + 4 * o_rows),
        ),
        in_hbm(
            down, up, rank_down.T, rank_up.T, sketch_out,
            c_x.reshape(flat), c_m.reshape(flat_m), c_len, p_x.reshape(flat), p_m.reshape(flat_m), p_len,
        ),
        in_specs=[HBM] * 11,
        scratch=[
            pltpu.VMEM(down.shape, down.dtype),
            pltpu.VMEM(up.shape, up.dtype),
            pltpu.VMEM(rank_down.shape[::-1], rank_down.dtype),
            pltpu.VMEM(rank_up.shape[::-1], rank_up.dtype),
            pltpu.SMEM(c_len.shape, c_len.dtype),
            pltpu.SMEM(p_len.shape, p_len.dtype),
            pltpu.SemaphoreType.DMA((7 + 4 * examples,)),
        ],
    )

    f32 = jnp.float32
    here, there, both = (0,), (1,), (0, 1)
    own, second, own_sums, own_small = kernel(
        functools.partial(
            own_kernel, n, ks,
            ((0, 0, (0, 0, here), 1, 0, o_rows), (1, 0, (0, 0, here), 0, 0, s_rows)),
            ((0, o_rows, (0, 0, here)),),
        ),
        "own_products",
        (
            array(s_rows, kp),
            array(part + o_rows + t_rows, kp),
            array(2, 2, rows // 2, kp, dtype=f32),
            array(2, 2, rows // 2, ks, dtype=f32),
        ),
        (*in_hbm(sketch_in), extra, x, m),
        in_specs=[HBM] + [VMEM] * 3,
        scratch=[pltpu.SemaphoreType.DMA((2,))],
    )

    first, first_extra = along(sketch_in, False), along(extra, False)
    second = along(second, True)
    c_xo, p_xo = sw(c_cols, 1), sw(p_cols, 1)

    more = along(jnp.concatenate([first, first_extra]), True)
    rest = swap(first[:beside], 1, "dp", planes)
    second_other, rest_other = sw(second[: part + t_rows], 1), sw(rest, 1)

    o_at = part + t_rows
    early_places = (
        (0, 0, (0, 0, there), 1, 0, o_rows), (1, 0, (1, 0, both), 0, 0, s_rows), (2, 0, (1, 0, both), 1, 0, o_rows),
        (3, 0, (2, 0, here), 0, beside, part), (4, 0, (2, 1, here), 0, beside, part),
        (3, o_at, (2, 0, both), 1, 0, o_rows), (5, 0, (0, 0, there), 0, 0, s_rows),
    )
    early_tables = (
        (0, o_rows, (0, 0, there)), (2, o_rows, (1, 0, both)), (3, part, (2, 0, here)), (4, part, (2, 1, here)),
    )
    sums, small = kernel(
        functools.partial(early_kernel, n, ks, early_places, early_tables),
        "early_products",
        (array(2, 2, 2, rows // 2, kp, dtype=f32), array(2, 2, 2, rows // 2, ks, dtype=f32)),
        (x, m, c_xo, p_xo, own_sums, own_small, extra, first, first_extra, second, second_other, own),
    )
    late_places = (
        (0, 0, (3, 0, both), 0, 0, s_rows), (0, s_rows, (3, 0, both), 1, 0, o_rows),
        (1, 0, (2, 0, here), 0, 0, beside), (2, 0, (2, 1, here), 0, 0, beside),
    )

    def late(side, name):
        keep, keep_small, out = kernel(
            functools.partial(late_kernel, n, ks, side, late_places, ((0, s_rows + o_rows, (3, 0, both)),)),
            name,
            (array(rows, kp, dtype=f32), array(ks, rows, dtype=f32), array(rows + 2 * ks + 16, kp)),
            (x, m, (c_xo, p_xo)[side], live, sums, small, more, rest, rest_other),
            scratch=[pltpu.VMEM((2, rows, kp), f32), pltpu.VMEM((2, ks, rows), f32)],
        )
        return keep, keep_small, sw(out, 1)

    total = 2 * examples * ks
    side = array(2 * examples, ks * kp)

    def scratch(count):
        return [pltpu.VMEM((kp // 128, count + ks, 128), f32)]

    p_side = kernel(
        functools.partial(probe_kernel, seq), "probe_sides", side, (*late(1, "probe_products"), live), scratch=scratch(total)
    )
    grads = array(total // 2, kp, dtype=f32)
    c_side, c_grads, c_send = kernel(
        functools.partial(candidate_kernel, seq),
        "candidate_sides",
        (side, grads, grads),
        (*late(0, "candidate_products"), live),
        scratch=scratch(total),
    )
    c_feat = kernel(
        functools.partial(feature_kernel, ks),
        "candidate_features",
        array(examples, 2 * ks * kp),
        (c_grads, sw(c_send, 1)),
        scratch=scratch(total // 2),
    )

    kinds = (0, 3, 2, 1)
    got = [sw(p_side, 6), along(p_side, True), along(p_side, False)]
    c_side, *got = lax.optimization_barrier((c_side, *got))
    part = array(3 * examples, n * examples, dtype=f32)
    scores, to_other = kernel(
        functools.partial(score_kernel, kinds), "score_shares", (part, part), (c_side, p_side, *got)
    )
    scores = kernel(
        functools.partial(final_kernel, 2 * ks * kp),
        "scores",
        array(examples, n * examples, dtype=f32),
        (scores, sw(to_other, 1)),
    )
    return scores, c_feat


def plain_features(x, m, lengths, down, up, sketch_in, sketch_out, rank_down, rank_up):
    examples, seq, model = x.shape
    ks, kp = rank_down.shape[1], sketch_in.shape[1]
    live = (lax.broadcasted_iota(jnp.int32, (examples, seq), 1) < lengths[:, None]).astype(m.dtype)
    masked = (m * live[:, :, None]).reshape(examples * seq, -1)
    rows = x.reshape(examples * seq, model)
    grad_rows = dot(masked, up).astype(jnp.bfloat16)
    outward = dot(masked, sketch_out).astype(jnp.bfloat16)
    down_round = dot(rows, down).astype(jnp.bfloat16)
    inward = dot(rows, sketch_in).astype(jnp.bfloat16)
    left_small = dot(grad_rows, rank_down).astype(jnp.bfloat16)
    right_small = dot(down_round, rank_up).astype(jnp.bfloat16)

    def outer(small, wide):
        return jnp.einsum(
            "esk,esp->ekp",
            small.reshape(examples, seq, ks),
            wide.reshape(examples, seq, kp),
            preferred_element_type=jnp.float32,
        )

    joined = jnp.concatenate([outer(left_small, inward), outer(right_small, outward)], axis=1)
    joined = joined.reshape(examples, 2 * ks * kp)
    scale = lax.rsqrt(jnp.mean(joined * joined, axis=1, keepdims=True) + eps_mean)
    return (joined * scale).astype(jnp.bfloat16)


def plain_body(c_x, c_m, c_len, p_x, p_m, p_len, down, up, sketch_in, sketch_out, rank_down, rank_up):
    weights = [
        lax.all_gather(w, "fsdp", axis=0, tiled=True) for w in (down, up, sketch_in, sketch_out)
    ]
    p_feat = plain_features(p_x, p_m, p_len, *weights, rank_down, rank_up)
    c_feat = plain_features(c_x, c_m, c_len, *weights, rank_down, rank_up)
    every = lax.all_gather(p_feat, "fsdp", axis=0, tiled=True)
    return dot(c_feat, every.T) / c_feat.shape[1], c_feat


def solution(mesh):
    n, planes = mesh.shape["fsdp"], mesh.shape["dp"]
    rows = P(("dp", "fsdp"), None)
    cube = P(("dp", "fsdp"), None, None)
    line = P(("dp", "fsdp"))
    shard = P("fsdp", None)
    in_specs = (cube, cube, line, cube, cube, line, shard, shard, shard, shard, P(), P())

    def body(*args):
        sketch_in, sketch_out = args[8:10]
        s_rows, (o_rows, kp) = sketch_in.shape[0], sketch_out.shape
        whole = s_rows % 256 == 0 and s_rows % kp == 0 and o_rows % 128 == 0 and o_rows <= kp and kp % 128 == 0
        if n == 1 << 3 and planes % 2 == 0 and whole:
            return fast_body(n, planes, *args)
        return plain_body(*args)

    return jax.shard_map(body, mesh=mesh, in_specs=in_specs, out_specs=(rows, rows), check_vma=False)
```

```python
import functools

import jax
import jax.numpy as jnp
from jax import lax
from jax.experimental import pallas as pl
from jax.experimental.pallas import tpu as pltpu
from jax.sharding import PartitionSpec as P

eps_mean = 1e-06
LAST = (((1,), (1,)), ((), ()))
VMEM = pl.BlockSpec(memory_space=pltpu.VMEM)
SMEM = pl.BlockSpec(memory_space=pltpu.SMEM)
HBM = pl.BlockSpec(memory_space=pltpu.HBM)
MIB = 1 << 20
SHORT = pl.CostEstimate(flops=1, bytes_accessed=1, transcendentals=0)


def in_hbm(*arrays):
    return tuple(pltpu.with_memory_space_constraint(a, pltpu.HBM) for a in arrays)


def dot(a, b):
    return jnp.dot(a, b, preferred_element_type=jnp.float32)


def dot_last(a, b):
    return lax.dot_general(a, b, LAST, preferred_element_type=jnp.float32)


def split_two(x):
    high = x.astype(jnp.bfloat16)
    return high, (x - high.astype(jnp.float32)).astype(jnp.bfloat16)


def first_way(core, plane):
    return 2 + 2 * ((core + plane) % 2)


def partner(me, kind, plane):
    first = first_way(me % 2, plane)
    return me ^ (0, first, 6 - first, 6)[kind]


def there_at(kd, ku):
    return (0, kd, None, 2 * kd), tuple(3 * kd + kind * ku for kind in range(4))


def prepare_kernel(
    n, seq, down_hbm, up_hbm, rank_down_hbm, rank_up_hbm, out_hbm,
    c_x_hbm, c_m_hbm, c_len_hbm, p_x_hbm, p_m_hbm, p_len_hbm,
    extra_ref, x_ref, m_ref, live_ref, c_send, p_send,
    down_ref, up_ref, rank_down_ref, rank_up_ref, c_len, p_len, sems,
):
    o_rows, half = out_hbm.shape[0], c_x_hbm.shape[0]
    moves = (
        (down_hbm, down_ref),
        (up_hbm, up_ref),
        (rank_down_hbm, rank_down_ref),
        (rank_up_hbm, rank_up_ref),
        (c_len_hbm, c_len),
        (p_len_hbm, p_len),
        (out_hbm, extra_ref.at[pl.ds(0, o_rows)]),
    )
    moves += tuple(
        (source.at[pl.ds(e * seq, seq)], to.at[pl.ds(base + e * seq, seq)])
        for source, to, base in ((c_m_hbm, m_ref, 0), (c_x_hbm, x_ref, 0), (p_m_hbm, m_ref, half), (p_x_hbm, x_ref, half))
        for e in range(half // seq)
    )
    copies = [pltpu.make_async_copy(a, b, sems.at[i]) for i, (a, b) in enumerate(moves)]
    for copy in copies:
        copy.start()
    for copy in copies[:6]:
        copy.wait()
    down_table = dot_last(rank_up_ref[...], down_ref[...]).astype(jnp.bfloat16)
    up_table = dot_last(rank_down_ref[...], up_ref[...]).astype(jnp.bfloat16)
    ks, width = up_table.shape
    lanes = extra_ref.shape[1]
    blocks = down_table.shape[1] // lanes
    for b in range(blocks):
        at = o_rows + b * ks
        extra_ref[at : at + ks, :] = down_table[:, b * lanes : (b + 1) * lanes]
    at = o_rows + blocks * ks
    extra_ref[at:, :] = jnp.zeros((ks, lanes), jnp.bfloat16)
    extra_ref[at:, :width] = up_table
    lane = lax.broadcasted_iota(jnp.int32, live_ref.shape[1:], 1)
    for side, lengths in enumerate((c_len, p_len)):
        live = jnp.zeros(live_ref.shape[1:], jnp.bool_)
        for e in range(half // seq):
            live = live | ((lane >= e * seq) & (lane < e * seq + lengths[e]))
        live_ref[side] = live.astype(jnp.float32).astype(live_ref.dtype)
    other, plane = lax.axis_index("fsdp") ^ 1, lax.axis_index("dp")
    examples = half // seq
    kd, ku = x_ref.shape[1] // n, m_ref.shape[1] // n
    copies[6].wait()
    for side, send_ref in enumerate((c_send, p_send)):
        for sketch, ref, wide in ((1, m_ref, ku), (0, x_ref, kd)):
            for e in range(examples):
                copies[7 + (2 * side + 1 - sketch) * examples + e].wait()
                rows = pl.ds(e * seq, seq)
                for kind, at in enumerate(there_at(kd, ku)[sketch]):
                    if at is not None:
                        first = pl.multiple_of(partner(other, kind, plane) * wide, wide)
                        send_ref[rows, at : at + wide] = ref[pl.ds(side * half + e * seq, seq), pl.ds(first, wide)]


def spans(n, x, m, xo, block, sketch, first, count):
    kind, core, whos = block
    j = partner(lax.axis_index("fsdp") ^ core, kind, lax.axis_index("dp"))
    kd, ku = x.shape[1] // n, m.shape[1] // n
    source, wide = ((x, kd), (m, ku))[sketch]
    for who in whos:
        if who == 0:
            yield who, source[:, pl.ds(pl.multiple_of(j * wide + first, 128), count)]
        else:
            at = there_at(kd, ku)[sketch][kind] + first
            yield who, jnp.concatenate([ref[:, at : at + count] for ref in xo], axis=0)


def small_sums(n, ks, places, x, m, xo, refs):
    ku = m.shape[1] // n
    sums = [[0.0, 0.0], [0.0, 0.0]]
    for r, at, block in places:
        lanes = refs[r].shape[1]
        blocks = x.shape[1] // n // lanes
        up = refs[r][at + blocks * ks : at + (blocks + 1) * ks, :ku]
        for who, rows in spans(n, x, m, xo, block, 1, 0, ku):
            sums[who][0] += dot_last(rows, up)
        table = jnp.concatenate([refs[r][at + b * ks : at + (b + 1) * ks, :] for b in range(blocks)], axis=1)
        for who, rows in spans(n, x, m, xo, block, 0, 0, blocks * lanes):
            sums[who][1] += dot_last(rows, table)
    return sums


def products(n, places, x, m, xo, refs):
    sums = [[0.0, 0.0], [0.0, 0.0]]
    height = x.shape[0]
    for ref, row, block, sketch, first, count in places:
        piece = refs[ref][row : row + count, :]
        whos, rows = zip(*spans(n, x, m, xo, block, sketch, first, count))
        total = dot(jnp.concatenate(rows, axis=0), piece)
        for i, who in enumerate(whos):
            sums[who][sketch] += total[i * height : (i + 1) * height]
    return sums


def own_kernel(n, ks, places, tables, in_hbm, extra, x, m, own, second, sums_ref, small_ref, sems):
    part = first = in_hbm.shape[0] // 2
    o_rows = m.shape[1] // n
    load = pltpu.make_async_copy(in_hbm, own, sems.at[0])
    load.start()
    half = x.shape[0] // 2
    views = [(x.at[pl.ds(side * half, half)], m.at[pl.ds(side * half, half)], None) for side in range(2)]
    for side in range(2):
        small = small_sums(n, ks, tables, *views[side], (extra,))
        for t in range(2):
            small_ref[side, t] = small[0][t]
    load.wait()
    for side in range(2):
        sums = products(n, places, *views[side], (extra, own))
        for t in range(2):
            sums_ref[side, t] = sums[0][t]
    fill = pltpu.make_async_copy(in_hbm.at[pl.ds(first, part)], second.at[pl.ds(0, part)], sems.at[1])
    fill.start()
    second[part : second.shape[0] - o_rows, :] = extra[o_rows:, :]
    second[second.shape[0] - o_rows :, :] = extra[:o_rows, :]
    fill.wait()


def early_kernel(n, ks, places, tables, x, m, c_xo, p_xo, own_sums, own_small, *refs):
    refs, (sums_ref, small_ref) = refs[:-2], refs[-2:]
    half = c_xo.shape[0]
    views = x, m, (c_xo, p_xo)
    small = small_sums(n, ks, tables, *views, refs)
    sums = products(n, places, *views, refs)
    for side in range(2):
        rows = slice(side * half, (side + 1) * half)
        for t in range(2):
            small_ref[side, 0, t] = small[0][t][rows] + own_small[side, t]
            small_ref[side, 1, t] = small[1][t][rows]
            sums_ref[side, 0, t] = sums[0][t][rows] + own_sums[side, t]
            sums_ref[side, 1, t] = sums[1][t][rows]


def late_kernel(n, ks, side, places, tables, x, m, xo, live, sums, early_small, *refs):
    refs, (keep, keep_small, send, wide, narrow) = refs[:-5], refs[-5:]
    core = lax.axis_index("fsdp") % 2
    half = x.shape[0] // 2
    rows = pl.ds(side * half, half)
    views = x.at[rows], m.at[rows], (xo,)
    late = products(n, places, *views, refs)
    late_small = small_sums(n, ks, tables, *views, refs)
    for t in range(2):
        for who in range(2):
            wide[t, who * half : (who + 1) * half, :] = late[who][t] + sums[side, who, t]
        both = [late_small[who][t] + early_small[side, who, t] for who in range(2)]
        narrow[t] = jnp.concatenate(both, axis=0).T
    keep[...] = wide[core]
    keep_small[...] = narrow[core]
    for who in range(2):
        first = (1 - who) * half
        send[who * half : (who + 1) * half, :] = wide[1 - core, first : first + half, :].astype(jnp.bfloat16)
    small = narrow[1 - core]
    high, low = split_two(jnp.concatenate([small[:, half:], small[:, :half]], axis=1))
    send[2 * half : 2 * half + ks, :] = high
    send[2 * half + ks : 2 * half + 2 * ks, :] = low
    send[2 * half + 2 * ks :, :half] = live[side]
    send[2 * half + 2 * ks :, half:] = live[side]


def gradients(seq, side, keep, keep_small, got, live):
    rows, ks = keep.shape[0], keep_small.shape[0]
    high, low = (got[at : at + ks, :].astype(jnp.float32) for at in (rows, rows + ks))
    there = got[rows + 2 * ks : rows + 2 * ks + 1, rows // 2 :]
    lives = jnp.concatenate([live[side, :1, :].astype(jnp.float32), there.astype(jnp.float32)], axis=1)
    small = jnp.where(lives > 0, keep_small[...] + high + low, 0.0)
    count = rows // seq
    tiled = jnp.concatenate([small] * count, axis=0)
    e_row = lax.broadcasted_iota(jnp.int32, tiled.shape, 0) // ks
    e_col = lax.broadcasted_iota(jnp.int32, tiled.shape, 1) // seq
    factor = jnp.where(e_row == e_col, tiled, 0.0).astype(jnp.bfloat16)
    total = keep[...] + got[:rows, :].astype(jnp.float32)
    return dot(factor, total.astype(jnp.bfloat16))


def flatten(grads, ks, out, scratch, base=0):
    cols, lanes = grads.shape[1], scratch.shape[2]
    for b in range(cols // lanes):
        scratch[b, : grads.shape[0], :] = grads[:, b * lanes : (b + 1) * lanes]
    for k in range(ks):
        for b in range(cols // lanes):
            at = base + k * cols + b * lanes
            rows = pl.ds(k, grads.shape[0] // ks, stride=ks)
            out[:, at : at + lanes] = scratch[b, rows, :].astype(out.dtype)


def probe_kernel(seq, keep, keep_small, got, live, out, scratch):
    flatten(gradients(seq, 1, keep, keep_small, got, live), keep_small.shape[0], out, scratch)


def candidate_kernel(seq, keep, keep_small, got, live, out, own, send, scratch):
    grads = gradients(seq, 0, keep, keep_small, got, live)
    flatten(grads, keep_small.shape[0], out, scratch)
    half = grads.shape[0] // 2
    own[...] = grads[:half]
    send[...] = grads[half:]


def feature_kernel(ks, own, got, out, scratch):
    core = lax.axis_index("fsdp") % 2
    left = jnp.where(core == 0, own[...], got[...])
    right = jnp.where(core == 0, got[...], own[...])
    rows, cols = left.shape
    square = (left * left + right * right).reshape(rows // ks, ks, cols)
    scale = lax.rsqrt(jnp.sum(square, axis=(1, 2), keepdims=True) / (2 * ks * cols) + eps_mean)
    for t, part in enumerate((left, right)):
        scaled = (part.reshape(rows // ks, ks, cols) * scale).reshape(rows, cols)
        flatten(scaled, ks, out, scratch, t * ks * cols)


def score_kernel(kinds, c_ref, *refs):
    probes, (own_ref, send_ref) = refs[:-2], refs[-2:]
    me, plane = lax.axis_index("fsdp"), lax.axis_index("dp")
    cands = c_ref[...]
    per = cands.shape[0] // 2
    held = jnp.concatenate([ref[...] for ref in probes], axis=0)
    width = held.shape[0]
    mixed = dot_last(jnp.concatenate([cands, held], axis=0), held)
    scores, gram = mixed[: 2 * per], mixed[2 * per :]

    def diagonal(square, axis):
        rows = lax.broadcasted_iota(jnp.int32, square.shape, 0)
        cols = lax.broadcasted_iota(jnp.int32, square.shape, 1)
        return jnp.sum(jnp.where(rows == cols, square, 0.0), axis=axis, keepdims=True)

    rows = jnp.concatenate([scores, jnp.broadcast_to(diagonal(gram, 0), scores.shape)], axis=0)
    group = lax.broadcasted_iota(jnp.int32, rows.shape, 1) // per
    placed = jnp.zeros(rows.shape, jnp.float32)
    for g in range(width // per):
        block = jnp.concatenate([rows[:, g * per : (g + 1) * per]] * (width // per), axis=1)
        placed = jnp.where(group == (partner(me, kinds[g // 2], plane) ^ (g % 2)), block, placed)
    squares = jnp.broadcast_to(diagonal(dot_last(cands, cands), 1), (2 * per, width))
    for i, ref in enumerate((own_ref, send_ref)):
        ref[:per, :] = placed[i * per : (i + 1) * per]
        ref[per : 2 * per, :] = placed[2 * per : 3 * per]
        ref[2 * per :, :] = squares[i * per : (i + 1) * per]


def final_kernel(entries, own, got, out):
    total = own[...] + got[...]
    per = out.shape[0]
    scale = lax.rsqrt(total[per:] / entries + eps_mean)
    out[...] = total[:per] * scale[:per] * scale[per:] / entries


def swap(x, k, axis, size):
    return lax.ppermute(x, axis, [(i, i ^ k) for i in range(size)])


def fast_body(n, planes, c_x, c_m, c_len, p_x, p_m, p_len, down, up, sketch_in, sketch_out, rank_down, rank_up):
    examples, seq, model = c_x.shape
    value = c_m.shape[2]
    ks, kp = rank_down.shape[1], sketch_in.shape[1]
    s_rows, o_rows = sketch_in.shape[0], sketch_out.shape[0]
    t_rows = (s_rows // kp + 1) * ks
    sw = functools.partial(swap, axis="fsdp", size=n)

    def along(x, second):
        pairs = []
        for i in range(n):
            for z in range(planes):
                way = first_way(i % 2, z)
                pairs.append((i * planes + z, (i ^ (6 - way if second else way)) * planes + z))
        return lax.ppermute(x, ("fsdp", "dp"), pairs)

    def array(*shape, dtype=jnp.bfloat16):
        return jax.ShapeDtypeStruct(shape, dtype)

    def kernel(f, name, outs, operands, in_specs=None, scratch=(), limit=8):
        return pl.pallas_call(
            f,
            out_shape=outs,
            in_specs=in_specs or [VMEM] * len(operands),
            out_specs=(VMEM,) * len(outs) if isinstance(outs, tuple) else VMEM,
            scratch_shapes=scratch,
            compiler_params=pltpu.CompilerParams(vmem_limit_bytes=limit * MIB),
            cost_estimate=SHORT,
            name=name,
        )(*operands)

    flat = (examples * seq, model)
    flat_m = (examples * seq, value)
    rows = 2 * examples * seq
    beside = part = s_rows // 2
    extra, x, m, live, c_cols, p_cols = kernel(
        functools.partial(prepare_kernel, n, seq),
        "prepare",
        (
            array(o_rows + t_rows, kp),
            array(rows, model),
            array(rows, value),
            array(2, 16, rows // 2),
            array(rows // 2, 3 * s_rows + 4 * o_rows),
            array(rows // 2, 3 * s_rows + 4 * o_rows),
        ),
        in_hbm(
            down, up, rank_down.T, rank_up.T, sketch_out,
            c_x.reshape(flat), c_m.reshape(flat_m), c_len, p_x.reshape(flat), p_m.reshape(flat_m), p_len,
        ),
        in_specs=[HBM] * 11,
        scratch=[
            pltpu.VMEM(down.shape, down.dtype),
            pltpu.VMEM(up.shape, up.dtype),
            pltpu.VMEM(rank_down.shape[::-1], rank_down.dtype),
            pltpu.VMEM(rank_up.shape[::-1], rank_up.dtype),
            pltpu.SMEM(c_len.shape, c_len.dtype),
            pltpu.SMEM(p_len.shape, p_len.dtype),
            pltpu.SemaphoreType.DMA((7 + 4 * examples,)),
        ],
    )

    f32 = jnp.float32
    here, there, both = (0,), (1,), (0, 1)
    own, second, own_sums, own_small = kernel(
        functools.partial(
            own_kernel, n, ks,
            ((0, 0, (0, 0, here), 1, 0, o_rows), (1, 0, (0, 0, here), 0, 0, s_rows)),
            ((0, o_rows, (0, 0, here)),),
        ),
        "own_products",
        (
            array(s_rows, kp),
            array(part + o_rows + t_rows, kp),
            array(2, 2, rows // 2, kp, dtype=f32),
            array(2, 2, rows // 2, ks, dtype=f32),
        ),
        (*in_hbm(sketch_in), extra, x, m),
        in_specs=[HBM] + [VMEM] * 3,
        scratch=[pltpu.SemaphoreType.DMA((2,))],
    )

    first, first_extra = along(sketch_in, False), along(extra, False)
    second = along(second, True)
    c_xo, p_xo = sw(c_cols, 1), sw(p_cols, 1)

    more = along(jnp.concatenate([first, first_extra]), True)
    rest = swap(first[:beside], 1, "dp", planes)
    second_other, rest_other = sw(second[: part + t_rows], 1), sw(rest, 1)

    o_at = part + t_rows
    early_places = (
        (0, 0, (0, 0, there), 1, 0, o_rows), (1, 0, (1, 0, both), 0, 0, s_rows), (2, 0, (1, 0, both), 1, 0, o_rows),
        (3, 0, (2, 0, here), 0, beside, part), (4, 0, (2, 1, here), 0, beside, part),
        (3, o_at, (2, 0, both), 1, 0, o_rows), (5, 0, (0, 0, there), 0, 0, s_rows),
    )
    early_tables = (
        (0, o_rows, (0, 0, there)), (2, o_rows, (1, 0, both)), (3, part, (2, 0, here)), (4, part, (2, 1, here)),
    )
    sums, small = kernel(
        functools.partial(early_kernel, n, ks, early_places, early_tables),
        "early_products",
        (array(2, 2, 2, rows // 2, kp, dtype=f32), array(2, 2, 2, rows // 2, ks, dtype=f32)),
        (x, m, c_xo, p_xo, own_sums, own_small, extra, first, first_extra, second, second_other, own),
    )
    late_places = (
        (0, 0, (3, 0, both), 0, 0, s_rows), (0, s_rows, (3, 0, both), 1, 0, o_rows),
        (1, 0, (2, 0, here), 0, 0, beside), (2, 0, (2, 1, here), 0, 0, beside),
    )

    def late(side, name):
        keep, keep_small, out = kernel(
            functools.partial(late_kernel, n, ks, side, late_places, ((0, s_rows + o_rows, (3, 0, both)),)),
            name,
            (array(rows, kp, dtype=f32), array(ks, rows, dtype=f32), array(rows + 2 * ks + 16, kp)),
            (x, m, (c_xo, p_xo)[side], live, sums, small, more, rest, rest_other),
            scratch=[pltpu.VMEM((2, rows, kp), f32), pltpu.VMEM((2, ks, rows), f32)],
        )
        return keep, keep_small, sw(out, 1)

    total = 2 * examples * ks
    side = array(2 * examples, ks * kp)

    def scratch(count):
        return [pltpu.VMEM((kp // 128, count + ks, 128), f32)]

    p_side = kernel(
        functools.partial(probe_kernel, seq), "probe_sides", side, (*late(1, "probe_products"), live), scratch=scratch(total)
    )
    grads = array(total // 2, kp, dtype=f32)
    c_side, c_grads, c_send = kernel(
        functools.partial(candidate_kernel, seq),
        "candidate_sides",
        (side, grads, grads),
        (*late(0, "candidate_products"), live),
        scratch=scratch(total),
    )
    c_feat = kernel(
        functools.partial(feature_kernel, ks),
        "candidate_features",
        array(examples, 2 * ks * kp),
        (c_grads, sw(c_send, 1)),
        scratch=scratch(total // 2),
    )

    kinds = (0, 3, 2, 1)
    got = [sw(p_side, 6), along(p_side, True), along(p_side, False)]
    c_side, *got = lax.optimization_barrier((c_side, *got))
    part = array(3 * examples, n * examples, dtype=f32)
    scores, to_other = kernel(
        functools.partial(score_kernel, kinds), "score_shares", (part, part), (c_side, p_side, *got)
    )
    scores = kernel(
        functools.partial(final_kernel, 2 * ks * kp),
        "scores",
        array(examples, n * examples, dtype=f32),
        (scores, sw(to_other, 1)),
    )
    return scores, c_feat


def plain_features(x, m, lengths, down, up, sketch_in, sketch_out, rank_down, rank_up):
    examples, seq, model = x.shape
    ks, kp = rank_down.shape[1], sketch_in.shape[1]
    live = (lax.broadcasted_iota(jnp.int32, (examples, seq), 1) < lengths[:, None]).astype(m.dtype)
    masked = (m * live[:, :, None]).reshape(examples * seq, -1)
    rows = x.reshape(examples * seq, model)
    grad_rows = dot(masked, up).astype(jnp.bfloat16)
    outward = dot(masked, sketch_out).astype(jnp.bfloat16)
    down_round = dot(rows, down).astype(jnp.bfloat16)
    inward = dot(rows, sketch_in).astype(jnp.bfloat16)
    left_small = dot(grad_rows, rank_down).astype(jnp.bfloat16)
    right_small = dot(down_round, rank_up).astype(jnp.bfloat16)

    def outer(small, wide):
        return jnp.einsum(
            "esk,esp->ekp",
            small.reshape(examples, seq, ks),
            wide.reshape(examples, seq, kp),
            preferred_element_type=jnp.float32,
        )

    joined = jnp.concatenate([outer(left_small, inward), outer(right_small, outward)], axis=1)
    joined = joined.reshape(examples, 2 * ks * kp)
    scale = lax.rsqrt(jnp.mean(joined * joined, axis=1, keepdims=True) + eps_mean)
    return (joined * scale).astype(jnp.bfloat16)


def plain_body(c_x, c_m, c_len, p_x, p_m, p_len, down, up, sketch_in, sketch_out, rank_down, rank_up):
    weights = [
        lax.all_gather(w, "fsdp", axis=0, tiled=True) for w in (down, up, sketch_in, sketch_out)
    ]
    p_feat = plain_features(p_x, p_m, p_len, *weights, rank_down, rank_up)
    c_feat = plain_features(c_x, c_m, c_len, *weights, rank_down, rank_up)
    every = lax.all_gather(p_feat, "fsdp", axis=0, tiled=True)
    return dot(c_feat, every.T) / c_feat.shape[1], c_feat


def solution(mesh):
    n, planes = mesh.shape["fsdp"], mesh.shape["dp"]
    rows = P(("dp", "fsdp"), None)
    cube = P(("dp", "fsdp"), None, None)
    line = P(("dp", "fsdp"))
    shard = P("fsdp", None)
    in_specs = (cube, cube, line, cube, cube, line, shard, shard, shard, shard, P(), P())

    def body(*args):
        sketch_in, sketch_out = args[8:10]
        s_rows, (o_rows, kp) = sketch_in.shape[0], sketch_out.shape
        whole = s_rows % 256 == 0 and s_rows % kp == 0 and o_rows % 128 == 0 and o_rows <= kp and kp % 128 == 0
        if n == 1 << 3 and planes % 2 == 0 and whole:
            return fast_body(n, planes, *args)
        return plain_body(*args)

    return jax.shard_map(body, mesh=mesh, in_specs=in_specs, out_specs=(rows, rows), check_vma=False)
```

```python
import functools

import jax
import jax.numpy as jnp
from jax import lax
from jax.experimental import pallas as pl
from jax.experimental.pallas import tpu as pltpu
from jax.sharding import PartitionSpec as P

eps_mean = 1e-06
LAST = (((1,), (1,)), ((), ()))
VMEM = pl.BlockSpec(memory_space=pltpu.VMEM)
SMEM = pl.BlockSpec(memory_space=pltpu.SMEM)
HBM = pl.BlockSpec(memory_space=pltpu.HBM)
MIB = 1 << 20
SHORT = pl.CostEstimate(flops=1, bytes_accessed=1, transcendentals=0)


def in_hbm(*arrays):
    return tuple(pltpu.with_memory_space_constraint(a, pltpu.HBM) for a in arrays)


def dot(a, b):
    return jnp.dot(a, b, preferred_element_type=jnp.float32)


def dot_last(a, b):
    return lax.dot_general(a, b, LAST, preferred_element_type=jnp.float32)


def split_two(x):
    high = x.astype(jnp.bfloat16)
    return high, (x - high.astype(jnp.float32)).astype(jnp.bfloat16)


def first_way(core, plane):
    return 2 + 2 * ((core + plane) % 2)


def partner(me, kind, plane):
    first = first_way(me % 2, plane)
    return me ^ (0, first, 6 - first, 6)[kind]


def there_at(kd, ku):
    return (0, kd, None, 2 * kd), tuple(3 * kd + kind * ku for kind in range(4))


def prepare_kernel(
    n, seq, down_hbm, up_hbm, rank_down_hbm, rank_up_hbm, out_hbm,
    c_x_hbm, c_m_hbm, c_len_hbm, p_x_hbm, p_m_hbm, p_len_hbm,
    extra_ref, x_ref, m_ref, live_ref, c_send, p_send,
    down_ref, up_ref, rank_down_ref, rank_up_ref, c_len, p_len, sems,
):
    o_rows, half = out_hbm.shape[0], c_x_hbm.shape[0]
    moves = (
        (down_hbm, down_ref),
        (up_hbm, up_ref),
        (rank_down_hbm, rank_down_ref),
        (rank_up_hbm, rank_up_ref),
        (c_len_hbm, c_len),
        (p_len_hbm, p_len),
        (out_hbm, extra_ref.at[pl.ds(0, o_rows)]),
    )
    moves += tuple(
        (source.at[pl.ds(e * seq, seq)], to.at[pl.ds(base + e * seq, seq)])
        for source, to, base in ((c_m_hbm, m_ref, 0), (c_x_hbm, x_ref, 0), (p_m_hbm, m_ref, half), (p_x_hbm, x_ref, half))
        for e in range(half // seq)
    )
    copies = [pltpu.make_async_copy(a, b, sems.at[i]) for i, (a, b) in enumerate(moves)]
    for copy in copies:
        copy.start()
    for copy in copies[:6]:
        copy.wait()
    down_table = dot_last(rank_up_ref[...], down_ref[...]).astype(jnp.bfloat16)
    up_table = dot_last(rank_down_ref[...], up_ref[...]).astype(jnp.bfloat16)
    ks, width = up_table.shape
    lanes = extra_ref.shape[1]
    blocks = down_table.shape[1] // lanes
    for b in range(blocks):
        at = o_rows + b * ks
        extra_ref[at : at + ks, :] = down_table[:, b * lanes : (b + 1) * lanes]
    at = o_rows + blocks * ks
    extra_ref[at:, :] = jnp.zeros((ks, lanes), jnp.bfloat16)
    extra_ref[at:, :width] = up_table
    lane = lax.broadcasted_iota(jnp.int32, live_ref.shape[1:], 1)
    for side, lengths in enumerate((c_len, p_len)):
        live = jnp.zeros(live_ref.shape[1:], jnp.bool_)
        for e in range(half // seq):
            live = live | ((lane >= e * seq) & (lane < e * seq + lengths[e]))
        live_ref[side] = live.astype(jnp.float32).astype(live_ref.dtype)
    other, plane = lax.axis_index("fsdp") ^ 1, lax.axis_index("dp")
    examples = half // seq
    kd, ku = x_ref.shape[1] // n, m_ref.shape[1] // n
    copies[6].wait()
    for side, send_ref in enumerate((c_send, p_send)):
        for sketch, ref, wide in ((1, m_ref, ku), (0, x_ref, kd)):
            for e in range(examples):
                copies[7 + (2 * side + 1 - sketch) * examples + e].wait()
                rows = pl.ds(e * seq, seq)
                for kind, at in enumerate(there_at(kd, ku)[sketch]):
                    if at is not None:
                        first = pl.multiple_of(partner(other, kind, plane) * wide, wide)
                        send_ref[rows, at : at + wide] = ref[pl.ds(side * half + e * seq, seq), pl.ds(first, wide)]


def spans(n, x, m, xo, block, sketch, first, count):
    kind, core, whos = block
    j = partner(lax.axis_index("fsdp") ^ core, kind, lax.axis_index("dp"))
    kd, ku = x.shape[1] // n, m.shape[1] // n
    source, wide = ((x, kd), (m, ku))[sketch]
    for who in whos:
        if who == 0:
            yield who, source[:, pl.ds(pl.multiple_of(j * wide + first, 128), count)]
        else:
            at = there_at(kd, ku)[sketch][kind] + first
            yield who, jnp.concatenate([ref[:, at : at + count] for ref in xo], axis=0)


def small_sums(n, ks, places, x, m, xo, refs):
    ku = m.shape[1] // n
    sums = [[0.0, 0.0], [0.0, 0.0]]
    for r, at, block in places:
        lanes = refs[r].shape[1]
        blocks = x.shape[1] // n // lanes
        up = refs[r][at + blocks * ks : at + (blocks + 1) * ks, :ku]
        for who, rows in spans(n, x, m, xo, block, 1, 0, ku):
            sums[who][0] += dot_last(rows, up)
        table = jnp.concatenate([refs[r][at + b * ks : at + (b + 1) * ks, :] for b in range(blocks)], axis=1)
        for who, rows in spans(n, x, m, xo, block, 0, 0, blocks * lanes):
            sums[who][1] += dot_last(rows, table)
    return sums


def products(n, places, x, m, xo, refs):
    sums = [[0.0, 0.0], [0.0, 0.0]]
    height = x.shape[0]
    for ref, row, block, sketch, first, count in places:
        piece = refs[ref][row : row + count, :]
        whos, rows = zip(*spans(n, x, m, xo, block, sketch, first, count))
        total = dot(jnp.concatenate(rows, axis=0), piece)
        for i, who in enumerate(whos):
            sums[who][sketch] += total[i * height : (i + 1) * height]
    return sums


def own_kernel(n, ks, places, tables, in_hbm, extra, x, m, own, second, sums_ref, small_ref, sems):
    part = first = in_hbm.shape[0] // 2
    o_rows = m.shape[1] // n
    load = pltpu.make_async_copy(in_hbm, own, sems.at[0])
    load.start()
    half = x.shape[0] // 2
    views = [(x.at[pl.ds(side * half, half)], m.at[pl.ds(side * half, half)], None) for side in range(2)]
    for side in range(2):
        small = small_sums(n, ks, tables, *views[side], (extra,))
        for t in range(2):
            small_ref[side, t] = small[0][t]
    load.wait()
    for side in range(2):
        sums = products(n, places, *views[side], (extra, own))
        for t in range(2):
            sums_ref[side, t] = sums[0][t]
    fill = pltpu.make_async_copy(in_hbm.at[pl.ds(first, part)], second.at[pl.ds(0, part)], sems.at[1])
    fill.start()
    second[part : second.shape[0] - o_rows, :] = extra[o_rows:, :]
    second[second.shape[0] - o_rows :, :] = extra[:o_rows, :]
    fill.wait()


def early_kernel(n, ks, places, tables, x, m, c_xo, p_xo, own_sums, own_small, *refs):
    refs, (sums_ref, small_ref) = refs[:-2], refs[-2:]
    half = c_xo.shape[0]
    views = x, m, (c_xo, p_xo)
    small = small_sums(n, ks, tables, *views, refs)
    sums = products(n, places, *views, refs)
    for side in range(2):
        rows = slice(side * half, (side + 1) * half)
        for t in range(2):
            small_ref[side, 0, t] = small[0][t][rows] + own_small[side, t]
            small_ref[side, 1, t] = small[1][t][rows]
            sums_ref[side, 0, t] = sums[0][t][rows] + own_sums[side, t]
            sums_ref[side, 1, t] = sums[1][t][rows]


def late_kernel(n, ks, side, places, tables, x, m, xo, live, sums, early_small, *refs):
    refs, (keep, keep_small, send, wide, narrow) = refs[:-5], refs[-5:]
    core = lax.axis_index("fsdp") % 2
    half = x.shape[0] // 2
    rows = pl.ds(side * half, half)
    views = x.at[rows], m.at[rows], (xo,)
    late = products(n, places, *views, refs)
    late_small = small_sums(n, ks, tables, *views, refs)
    for t in range(2):
        for who in range(2):
            wide[t, who * half : (who + 1) * half, :] = late[who][t] + sums[side, who, t]
        both = [late_small[who][t] + early_small[side, who, t] for who in range(2)]
        narrow[t] = jnp.concatenate(both, axis=0).T
    keep[...] = wide[core]
    keep_small[...] = narrow[core]
    for who in range(2):
        first = (1 - who) * half
        send[who * half : (who + 1) * half, :] = wide[1 - core, first : first + half, :].astype(jnp.bfloat16)
    small = narrow[1 - core]
    high, low = split_two(jnp.concatenate([small[:, half:], small[:, :half]], axis=1))
    send[2 * half : 2 * half + ks, :] = high
    send[2 * half + ks : 2 * half + 2 * ks, :] = low
    send[2 * half + 2 * ks :, :half] = live[side]
    send[2 * half + 2 * ks :, half:] = live[side]


def gradients(seq, side, keep, keep_small, got, live):
    rows, ks = keep.shape[0], keep_small.shape[0]
    high, low = (got[at : at + ks, :].astype(jnp.float32) for at in (rows, rows + ks))
    there = got[rows + 2 * ks : rows + 2 * ks + 1, rows // 2 :]
    lives = jnp.concatenate([live[side, :1, :].astype(jnp.float32), there.astype(jnp.float32)], axis=1)
    small = jnp.where(lives > 0, keep_small[...] + high + low, 0.0)
    count = rows // seq
    tiled = jnp.concatenate([small] * count, axis=0)
    e_row = lax.broadcasted_iota(jnp.int32, tiled.shape, 0) // ks
    e_col = lax.broadcasted_iota(jnp.int32, tiled.shape, 1) // seq
    factor = jnp.where(e_row == e_col, tiled, 0.0).astype(jnp.bfloat16)
    total = keep[...] + got[:rows, :].astype(jnp.float32)
    return dot(factor, total.astype(jnp.bfloat16))


def flatten(grads, ks, out, scratch, base=0):
    cols, lanes = grads.shape[1], scratch.shape[2]
    for b in range(cols // lanes):
        scratch[b, : grads.shape[0], :] = grads[:, b * lanes : (b + 1) * lanes]
    for k in range(ks):
        for b in range(cols // lanes):
            at = base + k * cols + b * lanes
            rows = pl.ds(k, grads.shape[0] // ks, stride=ks)
            out[:, at : at + lanes] = scratch[b, rows, :].astype(out.dtype)


def probe_kernel(seq, keep, keep_small, got, live, out, scratch):
    flatten(gradients(seq, 1, keep, keep_small, got, live), keep_small.shape[0], out, scratch)


def candidate_kernel(seq, keep, keep_small, got, live, out, own, send, scratch):
    grads = gradients(seq, 0, keep, keep_small, got, live)
    flatten(grads, keep_small.shape[0], out, scratch)
    half = grads.shape[0] // 2
    own[...] = grads[:half]
    send[...] = grads[half:]


def feature_kernel(ks, own, got, out, scratch):
    core = lax.axis_index("fsdp") % 2
    left = jnp.where(core == 0, own[...], got[...])
    right = jnp.where(core == 0, got[...], own[...])
    rows, cols = left.shape
    square = (left * left + right * right).reshape(rows // ks, ks, cols)
    scale = lax.rsqrt(jnp.sum(square, axis=(1, 2), keepdims=True) / (2 * ks * cols) + eps_mean)
    for t, part in enumerate((left, right)):
        scaled = (part.reshape(rows // ks, ks, cols) * scale).reshape(rows, cols)
        flatten(scaled, ks, out, scratch, t * ks * cols)


def score_kernel(kinds, c_ref, *refs):
    probes, before, (own_ref, send_ref) = refs[: len(kinds)], refs[len(kinds) : -2], refs[-2:]
    me, plane = lax.axis_index("fsdp"), lax.axis_index("dp")
    cands = c_ref[...]
    per, total = cands.shape[0] // 2, own_ref.shape[1]
    held = jnp.concatenate([ref[...] for ref in probes], axis=0)
    width = held.shape[0]
    mixed = dot_last(jnp.concatenate([cands, held], axis=0), held)
    scores, gram = mixed[: 2 * per], mixed[2 * per :]

    def diagonal(square, axis):
        rows = lax.broadcasted_iota(jnp.int32, square.shape, 0)
        cols = lax.broadcasted_iota(jnp.int32, square.shape, 1)
        return jnp.sum(jnp.where(rows == cols, square, 0.0), axis=axis, keepdims=True)

    rows = jnp.concatenate([scores, jnp.broadcast_to(diagonal(gram, 0), scores.shape)], axis=0)
    group = lax.broadcasted_iota(jnp.int32, (rows.shape[0], total), 1) // per
    placed = jnp.zeros(group.shape, jnp.float32)
    for g in range(width // per):
        block = jnp.concatenate([rows[:, g * per : (g + 1) * per]] * (total // per), axis=1)
        placed = jnp.where(group == (partner(me, kinds[g // 2], plane) ^ (g % 2)), block, placed)
    if before:
        for i, (ref, held_ref) in enumerate(zip((own_ref, send_ref), before)):
            ref[:per, :] = held_ref[:per, :] + placed[i * per : (i + 1) * per]
            ref[per : 2 * per, :] = held_ref[per : 2 * per, :] + placed[2 * per : 3 * per]
            ref[2 * per :, :] = held_ref[2 * per :, :]
        return
    squares = jnp.broadcast_to(diagonal(dot_last(cands, cands), 1), (2 * per, total))
    for i, ref in enumerate((own_ref, send_ref)):
        ref[:per, :] = placed[i * per : (i + 1) * per]
        ref[per : 2 * per, :] = placed[2 * per : 3 * per]
        ref[2 * per :, :] = squares[i * per : (i + 1) * per]


def final_kernel(entries, own, got, out):
    total = own[...] + got[...]
    per = out.shape[0]
    scale = lax.rsqrt(total[per:] / entries + eps_mean)
    out[...] = total[:per] * scale[:per] * scale[per:] / entries


def swap(x, k, axis, size):
    return lax.ppermute(x, axis, [(i, i ^ k) for i in range(size)])


def fast_body(n, planes, c_x, c_m, c_len, p_x, p_m, p_len, down, up, sketch_in, sketch_out, rank_down, rank_up):
    examples, seq, model = c_x.shape
    value = c_m.shape[2]
    ks, kp = rank_down.shape[1], sketch_in.shape[1]
    s_rows, o_rows = sketch_in.shape[0], sketch_out.shape[0]
    t_rows = (s_rows // kp + 1) * ks
    sw = functools.partial(swap, axis="fsdp", size=n)

    def along(x, second):
        pairs = []
        for i in range(n):
            for z in range(planes):
                way = first_way(i % 2, z)
                pairs.append((i * planes + z, (i ^ (6 - way if second else way)) * planes + z))
        return lax.ppermute(x, ("fsdp", "dp"), pairs)

    def array(*shape, dtype=jnp.bfloat16):
        return jax.ShapeDtypeStruct(shape, dtype)

    def kernel(f, name, outs, operands, in_specs=None, scratch=(), limit=8):
        return pl.pallas_call(
            f,
            out_shape=outs,
            in_specs=in_specs or [VMEM] * len(operands),
            out_specs=(VMEM,) * len(outs) if isinstance(outs, tuple) else VMEM,
            scratch_shapes=scratch,
            compiler_params=pltpu.CompilerParams(vmem_limit_bytes=limit * MIB),
            cost_estimate=SHORT,
            name=name,
        )(*operands)

    flat = (examples * seq, model)
    flat_m = (examples * seq, value)
    rows = 2 * examples * seq
    beside = part = s_rows // 2
    extra, x, m, live, c_cols, p_cols = kernel(
        functools.partial(prepare_kernel, n, seq),
        "prepare",
        (
            array(o_rows + t_rows, kp),
            array(rows, model),
            array(rows, value),
            array(2, 16, rows // 2),
            array(rows // 2, 3 * s_rows + 4 * o_rows),
            array(rows // 2, 3 * s_rows + 4 * o_rows),
        ),
        in_hbm(
            down, up, rank_down.T, rank_up.T, sketch_out,
            c_x.reshape(flat), c_m.reshape(flat_m), c_len, p_x.reshape(flat), p_m.reshape(flat_m), p_len,
        ),
        in_specs=[HBM] * 11,
        scratch=[
            pltpu.VMEM(down.shape, down.dtype),
            pltpu.VMEM(up.shape, up.dtype),
            pltpu.VMEM(rank_down.shape[::-1], rank_down.dtype),
            pltpu.VMEM(rank_up.shape[::-1], rank_up.dtype),
            pltpu.SMEM(c_len.shape, c_len.dtype),
            pltpu.SMEM(p_len.shape, p_len.dtype),
            pltpu.SemaphoreType.DMA((7 + 4 * examples,)),
        ],
    )

    f32 = jnp.float32
    here, there, both = (0,), (1,), (0, 1)
    own, second, own_sums, own_small = kernel(
        functools.partial(
            own_kernel, n, ks,
            ((0, 0, (0, 0, here), 1, 0, o_rows), (1, 0, (0, 0, here), 0, 0, s_rows)),
            ((0, o_rows, (0, 0, here)),),
        ),
        "own_products",
        (
            array(s_rows, kp),
            array(part + o_rows + t_rows, kp),
            array(2, 2, rows // 2, kp, dtype=f32),
            array(2, 2, rows // 2, ks, dtype=f32),
        ),
        (*in_hbm(sketch_in), extra, x, m),
        in_specs=[HBM] + [VMEM] * 3,
        scratch=[pltpu.SemaphoreType.DMA((2,))],
    )

    first, first_extra = along(sketch_in, False), along(extra, False)
    second = along(second, True)
    c_xo, p_xo = sw(c_cols, 1), sw(p_cols, 1)

    more = along(jnp.concatenate([first, first_extra]), True)
    rest = swap(first[:beside], 1, "dp", planes)
    second_other, rest_other = sw(second[: part + t_rows], 1), sw(rest, 1)

    o_at = part + t_rows
    early_places = (
        (0, 0, (0, 0, there), 1, 0, o_rows), (1, 0, (1, 0, both), 0, 0, s_rows), (2, 0, (1, 0, both), 1, 0, o_rows),
        (3, 0, (2, 0, here), 0, beside, part), (4, 0, (2, 1, here), 0, beside, part),
        (3, o_at, (2, 0, both), 1, 0, o_rows), (5, 0, (0, 0, there), 0, 0, s_rows),
    )
    early_tables = (
        (0, o_rows, (0, 0, there)), (2, o_rows, (1, 0, both)), (3, part, (2, 0, here)), (4, part, (2, 1, here)),
    )
    sums, small = kernel(
        functools.partial(early_kernel, n, ks, early_places, early_tables),
        "early_products",
        (array(2, 2, 2, rows // 2, kp, dtype=f32), array(2, 2, 2, rows // 2, ks, dtype=f32)),
        (x, m, c_xo, p_xo, own_sums, own_small, extra, first, first_extra, second, second_other, own),
    )
    late_places = (
        (0, 0, (3, 0, both), 0, 0, s_rows), (0, s_rows, (3, 0, both), 1, 0, o_rows),
        (1, 0, (2, 0, here), 0, 0, beside), (2, 0, (2, 1, here), 0, 0, beside),
    )

    def late(side, name):
        keep, keep_small, out = kernel(
            functools.partial(late_kernel, n, ks, side, late_places, ((0, s_rows + o_rows, (3, 0, both)),)),
            name,
            (array(rows, kp, dtype=f32), array(ks, rows, dtype=f32), array(rows + 2 * ks + 16, kp)),
            (x, m, (c_xo, p_xo)[side], live, sums, small, more, rest, rest_other),
            scratch=[pltpu.VMEM((2, rows, kp), f32), pltpu.VMEM((2, ks, rows), f32)],
        )
        return keep, keep_small, sw(out, 1)

    total = 2 * examples * ks
    side = array(2 * examples, ks * kp)

    def scratch(count):
        return [pltpu.VMEM((kp // 128, count + ks, 128), f32)]

    p_side = kernel(
        functools.partial(probe_kernel, seq), "probe_sides", side, (*late(1, "probe_products"), live), scratch=scratch(total)
    )
    grads = array(total // 2, kp, dtype=f32)
    c_side, c_grads, c_send = kernel(
        functools.partial(candidate_kernel, seq),
        "candidate_sides",
        (side, grads, grads),
        (*late(0, "candidate_products"), live),
        scratch=scratch(total),
    )
    c_feat = kernel(
        functools.partial(feature_kernel, ks),
        "candidate_features",
        array(examples, 2 * ks * kp),
        (c_grads, sw(c_send, 1)),
        scratch=scratch(total // 2),
    )

    across, second_side, first_side = sw(p_side, 6), along(p_side, True), along(p_side, False)
    part = array(3 * examples, n * examples, dtype=f32)
    shares = kernel(
        functools.partial(score_kernel, (0, 3)), "first_shares", (part, part), (c_side, p_side, across)
    )
    *shares, second_side, first_side = lax.optimization_barrier((*shares, second_side, first_side))
    scores, to_other = kernel(
        functools.partial(score_kernel, (2, 1)),
        "score_shares",
        (part, part),
        (c_side, second_side, first_side, *shares),
    )
    scores = kernel(
        functools.partial(final_kernel, 2 * ks * kp),
        "scores",
        array(examples, n * examples, dtype=f32),
        (scores, sw(to_other, 1)),
    )
    return scores, c_feat


def plain_features(x, m, lengths, down, up, sketch_in, sketch_out, rank_down, rank_up):
    examples, seq, model = x.shape
    ks, kp = rank_down.shape[1], sketch_in.shape[1]
    live = (lax.broadcasted_iota(jnp.int32, (examples, seq), 1) < lengths[:, None]).astype(m.dtype)
    masked = (m * live[:, :, None]).reshape(examples * seq, -1)
    rows = x.reshape(examples * seq, model)
    grad_rows = dot(masked, up).astype(jnp.bfloat16)
    outward = dot(masked, sketch_out).astype(jnp.bfloat16)
    down_round = dot(rows, down).astype(jnp.bfloat16)
    inward = dot(rows, sketch_in).astype(jnp.bfloat16)
    left_small = dot(grad_rows, rank_down).astype(jnp.bfloat16)
    right_small = dot(down_round, rank_up).astype(jnp.bfloat16)

    def outer(small, wide):
        return jnp.einsum(
            "esk,esp->ekp",
            small.reshape(examples, seq, ks),
            wide.reshape(examples, seq, kp),
            preferred_element_type=jnp.float32,
        )

    joined = jnp.concatenate([outer(left_small, inward), outer(right_small, outward)], axis=1)
    joined = joined.reshape(examples, 2 * ks * kp)
    scale = lax.rsqrt(jnp.mean(joined * joined, axis=1, keepdims=True) + eps_mean)
    return (joined * scale).astype(jnp.bfloat16)


def plain_body(c_x, c_m, c_len, p_x, p_m, p_len, down, up, sketch_in, sketch_out, rank_down, rank_up):
    weights = [
        lax.all_gather(w, "fsdp", axis=0, tiled=True) for w in (down, up, sketch_in, sketch_out)
    ]
    p_feat = plain_features(p_x, p_m, p_len, *weights, rank_down, rank_up)
    c_feat = plain_features(c_x, c_m, c_len, *weights, rank_down, rank_up)
    every = lax.all_gather(p_feat, "fsdp", axis=0, tiled=True)
    return dot(c_feat, every.T) / c_feat.shape[1], c_feat


def solution(mesh):
    n, planes = mesh.shape["fsdp"], mesh.shape["dp"]
    rows = P(("dp", "fsdp"), None)
    cube = P(("dp", "fsdp"), None, None)
    line = P(("dp", "fsdp"))
    shard = P("fsdp", None)
    in_specs = (cube, cube, line, cube, cube, line, shard, shard, shard, shard, P(), P())

    def body(*args):
        sketch_in, sketch_out = args[8:10]
        s_rows, (o_rows, kp) = sketch_in.shape[0], sketch_out.shape
        whole = s_rows % 256 == 0 and s_rows % kp == 0 and o_rows % 128 == 0 and o_rows <= kp and kp % 128 == 0
        if n == 1 << 3 and planes % 2 == 0 and whole:
            return fast_body(n, planes, *args)
        return plain_body(*args)

    return jax.shard_map(body, mesh=mesh, in_specs=in_specs, out_specs=(rows, rows), check_vma=False)
```

```python
import functools

import jax
import jax.numpy as jnp
from jax import lax
from jax.experimental import pallas as pl
from jax.experimental.pallas import tpu as pltpu
from jax.sharding import PartitionSpec as P

eps_mean = 1e-06
LAST = (((1,), (1,)), ((), ()))
VMEM = pl.BlockSpec(memory_space=pltpu.VMEM)
SMEM = pl.BlockSpec(memory_space=pltpu.SMEM)
HBM = pl.BlockSpec(memory_space=pltpu.HBM)
MIB = 1 << 20
SHORT = pl.CostEstimate(flops=1, bytes_accessed=1, transcendentals=0)


def in_hbm(*arrays):
    return tuple(pltpu.with_memory_space_constraint(a, pltpu.HBM) for a in arrays)


def dot(a, b):
    return jnp.dot(a, b, preferred_element_type=jnp.float32)


def dot_last(a, b):
    return lax.dot_general(a, b, LAST, preferred_element_type=jnp.float32)


def split_two(x):
    high = x.astype(jnp.bfloat16)
    return high, (x - high.astype(jnp.float32)).astype(jnp.bfloat16)


def first_way(core, plane):
    return 2 + 2 * ((core + plane) % 2)


def partner(me, kind, plane):
    first = first_way(me % 2, plane)
    return me ^ (0, first, 6 - first, 6)[kind]


def there_at(kd, ku):
    return (0, kd, None, 2 * kd), tuple(3 * kd + kind * ku for kind in range(4))


def prepare_kernel(
    n, seq, down_hbm, up_hbm, rank_down_hbm, rank_up_hbm, out_hbm,
    c_x_hbm, c_m_hbm, c_len_hbm, p_x_hbm, p_m_hbm, p_len_hbm,
    extra_ref, x_ref, m_ref, live_ref, c_send, p_send,
    down_ref, up_ref, rank_down_ref, rank_up_ref, c_len, p_len, sems,
):
    o_rows, half = out_hbm.shape[0], c_x_hbm.shape[0]
    moves = (
        (down_hbm, down_ref),
        (up_hbm, up_ref),
        (rank_down_hbm, rank_down_ref),
        (rank_up_hbm, rank_up_ref),
        (c_len_hbm, c_len),
        (p_len_hbm, p_len),
        (out_hbm, extra_ref.at[pl.ds(0, o_rows)]),
    )
    moves += tuple(
        (source.at[pl.ds(e * seq, seq)], to.at[pl.ds(base + e * seq, seq)])
        for source, to, base in ((c_m_hbm, m_ref, 0), (c_x_hbm, x_ref, 0), (p_m_hbm, m_ref, half), (p_x_hbm, x_ref, half))
        for e in range(half // seq)
    )
    copies = [pltpu.make_async_copy(a, b, sems.at[i]) for i, (a, b) in enumerate(moves)]
    for copy in copies:
        copy.start()
    for copy in copies[:6]:
        copy.wait()
    down_table = dot_last(rank_up_ref[...], down_ref[...]).astype(jnp.bfloat16)
    up_table = dot_last(rank_down_ref[...], up_ref[...]).astype(jnp.bfloat16)
    ks, width = up_table.shape
    lanes = extra_ref.shape[1]
    blocks = down_table.shape[1] // lanes
    for b in range(blocks):
        at = o_rows + b * ks
        extra_ref[at : at + ks, :] = down_table[:, b * lanes : (b + 1) * lanes]
    at = o_rows + blocks * ks
    extra_ref[at:, :] = jnp.zeros((ks, lanes), jnp.bfloat16)
    extra_ref[at:, :width] = up_table
    lane = lax.broadcasted_iota(jnp.int32, live_ref.shape[1:], 1)
    for side, lengths in enumerate((c_len, p_len)):
        live = jnp.zeros(live_ref.shape[1:], jnp.bool_)
        for e in range(half // seq):
            live = live | ((lane >= e * seq) & (lane < e * seq + lengths[e]))
        live_ref[side] = live.astype(jnp.float32).astype(live_ref.dtype)
    other, plane = lax.axis_index("fsdp") ^ 1, lax.axis_index("dp")
    examples = half // seq
    kd, ku = x_ref.shape[1] // n, m_ref.shape[1] // n
    copies[6].wait()
    for side, send_ref in enumerate((c_send, p_send)):
        for sketch, ref, wide in ((1, m_ref, ku), (0, x_ref, kd)):
            for e in range(examples):
                copies[7 + (2 * side + 1 - sketch) * examples + e].wait()
                rows = pl.ds(e * seq, seq)
                for kind, at in enumerate(there_at(kd, ku)[sketch]):
                    if at is not None:
                        first = pl.multiple_of(partner(other, kind, plane) * wide, wide)
                        send_ref[rows, at : at + wide] = ref[pl.ds(side * half + e * seq, seq), pl.ds(first, wide)]


def spans(n, x, m, xo, block, sketch, first, count):
    kind, core, whos = block
    j = partner(lax.axis_index("fsdp") ^ core, kind, lax.axis_index("dp"))
    kd, ku = x.shape[1] // n, m.shape[1] // n
    source, wide = ((x, kd), (m, ku))[sketch]
    for who in whos:
        if who == 0:
            yield who, source[:, pl.ds(pl.multiple_of(j * wide + first, 128), count)]
        else:
            at = there_at(kd, ku)[sketch][kind] + first
            yield who, jnp.concatenate([ref[:, at : at + count] for ref in xo], axis=0)


def small_sums(n, ks, places, x, m, xo, refs):
    ku = m.shape[1] // n
    sums = [[0.0, 0.0], [0.0, 0.0]]
    for r, at, block in places:
        lanes = refs[r].shape[1]
        blocks = x.shape[1] // n // lanes
        up = refs[r][at + blocks * ks : at + (blocks + 1) * ks, :ku]
        for who, rows in spans(n, x, m, xo, block, 1, 0, ku):
            sums[who][0] += dot_last(rows, up)
        table = jnp.concatenate([refs[r][at + b * ks : at + (b + 1) * ks, :] for b in range(blocks)], axis=1)
        for who, rows in spans(n, x, m, xo, block, 0, 0, blocks * lanes):
            sums[who][1] += dot_last(rows, table)
    return sums


def products(n, places, x, m, xo, refs):
    sums = [[0.0, 0.0], [0.0, 0.0]]
    height = x.shape[0]
    for ref, row, block, sketch, first, count in places:
        piece = refs[ref][row : row + count, :]
        whos, rows = zip(*spans(n, x, m, xo, block, sketch, first, count))
        total = dot(jnp.concatenate(rows, axis=0), piece)
        for i, who in enumerate(whos):
            sums[who][sketch] += total[i * height : (i + 1) * height]
    return sums


def own_kernel(n, ks, places, tables, in_hbm, extra, x, m, own, second, sums_ref, small_ref, sems):
    part = first = in_hbm.shape[0] // 2
    o_rows = m.shape[1] // n
    load = pltpu.make_async_copy(in_hbm, own, sems.at[0])
    load.start()
    half = x.shape[0] // 2
    views = [(x.at[pl.ds(side * half, half)], m.at[pl.ds(side * half, half)], None) for side in range(2)]
    for side in range(2):
        small = small_sums(n, ks, tables, *views[side], (extra,))
        for t in range(2):
            small_ref[side, t] = small[0][t]
    load.wait()
    for side in range(2):
        sums = products(n, places, *views[side], (extra, own))
        for t in range(2):
            sums_ref[side, t] = sums[0][t]
    fill = pltpu.make_async_copy(in_hbm.at[pl.ds(first, part)], second.at[pl.ds(0, part)], sems.at[1])
    fill.start()
    second[part : second.shape[0] - o_rows, :] = extra[o_rows:, :]
    second[second.shape[0] - o_rows :, :] = extra[:o_rows, :]
    fill.wait()


def early_kernel(n, ks, places, tables, x, m, c_xo, p_xo, own_sums, own_small, *refs):
    refs, (sums_ref, small_ref) = refs[:-2], refs[-2:]
    half = c_xo.shape[0]
    views = x, m, (c_xo, p_xo)
    small = small_sums(n, ks, tables, *views, refs)
    sums = products(n, places, *views, refs)
    for side in range(2):
        rows = slice(side * half, (side + 1) * half)
        for t in range(2):
            small_ref[side, 0, t] = small[0][t][rows] + own_small[side, t]
            small_ref[side, 1, t] = small[1][t][rows]
            sums_ref[side, 0, t] = sums[0][t][rows] + own_sums[side, t]
            sums_ref[side, 1, t] = sums[1][t][rows]


def late_kernel(n, ks, side, places, tables, x, m, xo, live, sums, early_small, *refs):
    refs, (keep, keep_small, send, wide, narrow) = refs[:-5], refs[-5:]
    core = lax.axis_index("fsdp") % 2
    half = x.shape[0] // 2
    rows = pl.ds(side * half, half)
    views = x.at[rows], m.at[rows], (xo,)
    late = products(n, places, *views, refs)
    late_small = small_sums(n, ks, tables, *views, refs)
    for t in range(2):
        for who in range(2):
            wide[t, who * half : (who + 1) * half, :] = late[who][t] + sums[side, who, t]
        both = [late_small[who][t] + early_small[side, who, t] for who in range(2)]
        narrow[t] = jnp.concatenate(both, axis=0).T
    keep[...] = wide[core]
    keep_small[...] = narrow[core]
    for who in range(2):
        first = (1 - who) * half
        send[who * half : (who + 1) * half, :] = wide[1 - core, first : first + half, :].astype(jnp.bfloat16)
    small = narrow[1 - core]
    high, low = split_two(jnp.concatenate([small[:, half:], small[:, :half]], axis=1))
    send[2 * half : 2 * half + ks, :] = high
    send[2 * half + ks : 2 * half + 2 * ks, :] = low
    send[2 * half + 2 * ks :, :half] = live[side]
    send[2 * half + 2 * ks :, half:] = live[side]


def gradients(seq, side, keep, keep_small, got, live):
    rows, ks = keep.shape[0], keep_small.shape[0]
    high, low = (got[at : at + ks, :].astype(jnp.float32) for at in (rows, rows + ks))
    there = got[rows + 2 * ks : rows + 2 * ks + 1, rows // 2 :]
    lives = jnp.concatenate([live[side, :1, :].astype(jnp.float32), there.astype(jnp.float32)], axis=1)
    small = jnp.where(lives > 0, keep_small[...] + high + low, 0.0)
    count = rows // seq
    tiled = jnp.concatenate([small] * count, axis=0)
    e_row = lax.broadcasted_iota(jnp.int32, tiled.shape, 0) // ks
    e_col = lax.broadcasted_iota(jnp.int32, tiled.shape, 1) // seq
    factor = jnp.where(e_row == e_col, tiled, 0.0).astype(jnp.bfloat16)
    total = keep[...] + got[:rows, :].astype(jnp.float32)
    return dot(factor, total.astype(jnp.bfloat16))


def flatten(grads, ks, out, scratch, base=0):
    cols, lanes = grads.shape[1], scratch.shape[2]
    for b in range(cols // lanes):
        scratch[b, : grads.shape[0], :] = grads[:, b * lanes : (b + 1) * lanes]
    for k in range(ks):
        for b in range(cols // lanes):
            at = base + k * cols + b * lanes
            rows = pl.ds(k, grads.shape[0] // ks, stride=ks)
            out[:, at : at + lanes] = scratch[b, rows, :].astype(out.dtype)


def probe_kernel(seq, keep, keep_small, got, live, out, scratch):
    flatten(gradients(seq, 1, keep, keep_small, got, live), keep_small.shape[0], out, scratch)


def candidate_kernel(seq, keep, keep_small, got, live, out, own, send, scratch):
    grads = gradients(seq, 0, keep, keep_small, got, live)
    flatten(grads, keep_small.shape[0], out, scratch)
    half = grads.shape[0] // 2
    own[...] = grads[:half]
    send[...] = grads[half:]


def feature_kernel(ks, own, got, out, scratch):
    core = lax.axis_index("fsdp") % 2
    left = jnp.where(core == 0, own[...], got[...])
    right = jnp.where(core == 0, got[...], own[...])
    rows, cols = left.shape
    square = (left * left + right * right).reshape(rows // ks, ks, cols)
    scale = lax.rsqrt(jnp.sum(square, axis=(1, 2), keepdims=True) / (2 * ks * cols) + eps_mean)
    for t, part in enumerate((left, right)):
        scaled = (part.reshape(rows // ks, ks, cols) * scale).reshape(rows, cols)
        flatten(scaled, ks, out, scratch, t * ks * cols)


def score_kernel(kinds, c_ref, *refs):
    probes, before, (own_ref, send_ref) = refs[: len(kinds)], refs[len(kinds) : -2], refs[-2:]
    me, plane = lax.axis_index("fsdp"), lax.axis_index("dp")
    cands = c_ref[...]
    per, total = cands.shape[0] // 2, own_ref.shape[1]
    held = jnp.concatenate([ref[...] for ref in probes], axis=0)
    width = held.shape[0]
    mixed = dot_last(jnp.concatenate([cands, held], axis=0), held)
    scores, gram = mixed[: 2 * per], mixed[2 * per :]

    def diagonal(square, axis):
        rows = lax.broadcasted_iota(jnp.int32, square.shape, 0)
        cols = lax.broadcasted_iota(jnp.int32, square.shape, 1)
        return jnp.sum(jnp.where(rows == cols, square, 0.0), axis=axis, keepdims=True)

    rows = jnp.concatenate([scores, jnp.broadcast_to(diagonal(gram, 0), scores.shape)], axis=0)
    group = lax.broadcasted_iota(jnp.int32, (rows.shape[0], total), 1) // per
    placed = jnp.zeros(group.shape, jnp.float32)
    for g in range(width // per):
        block = jnp.concatenate([rows[:, g * per : (g + 1) * per]] * (total // per), axis=1)
        placed = jnp.where(group == (partner(me, kinds[g // 2], plane) ^ (g % 2)), block, placed)
    if before:
        for i, (ref, held_ref) in enumerate(zip((own_ref, send_ref), before)):
            ref[:per, :] = held_ref[:per, :] + placed[i * per : (i + 1) * per]
            ref[per : 2 * per, :] = held_ref[per : 2 * per, :] + placed[2 * per : 3 * per]
            ref[2 * per :, :] = held_ref[2 * per :, :]
        return
    squares = jnp.broadcast_to(diagonal(dot_last(cands, cands), 1), (2 * per, total))
    for i, ref in enumerate((own_ref, send_ref)):
        ref[:per, :] = placed[i * per : (i + 1) * per]
        ref[per : 2 * per, :] = placed[2 * per : 3 * per]
        ref[2 * per :, :] = squares[i * per : (i + 1) * per]


def final_kernel(entries, own, got, out):
    total = own[...] + got[...]
    per = out.shape[0]
    scale = lax.rsqrt(total[per:] / entries + eps_mean)
    out[...] = total[:per] * scale[:per] * scale[per:] / entries


def swap(x, k, axis, size):
    return lax.ppermute(x, axis, [(i, i ^ k) for i in range(size)])


def fast_body(n, planes, c_x, c_m, c_len, p_x, p_m, p_len, down, up, sketch_in, sketch_out, rank_down, rank_up):
    examples, seq, model = c_x.shape
    value = c_m.shape[2]
    ks, kp = rank_down.shape[1], sketch_in.shape[1]
    s_rows, o_rows = sketch_in.shape[0], sketch_out.shape[0]
    t_rows = (s_rows // kp + 1) * ks
    sw = functools.partial(swap, axis="fsdp", size=n)

    def along(x, second):
        pairs = []
        for i in range(n):
            for z in range(planes):
                way = first_way(i % 2, z)
                pairs.append((i * planes + z, (i ^ (6 - way if second else way)) * planes + z))
        return lax.ppermute(x, ("fsdp", "dp"), pairs)

    def array(*shape, dtype=jnp.bfloat16):
        return jax.ShapeDtypeStruct(shape, dtype)

    def kernel(f, name, outs, operands, in_specs=None, scratch=(), limit=8):
        return pl.pallas_call(
            f,
            out_shape=outs,
            in_specs=in_specs or [VMEM] * len(operands),
            out_specs=(VMEM,) * len(outs) if isinstance(outs, tuple) else VMEM,
            scratch_shapes=scratch,
            compiler_params=pltpu.CompilerParams(vmem_limit_bytes=limit * MIB),
            cost_estimate=SHORT,
            name=name,
        )(*operands)

    flat = (examples * seq, model)
    flat_m = (examples * seq, value)
    rows = 2 * examples * seq
    beside = part = s_rows // 2
    extra, x, m, live, c_cols, p_cols = kernel(
        functools.partial(prepare_kernel, n, seq),
        "prepare",
        (
            array(o_rows + t_rows, kp),
            array(rows, model),
            array(rows, value),
            array(2, 16, rows // 2),
            array(rows // 2, 3 * s_rows + 4 * o_rows),
            array(rows // 2, 3 * s_rows + 4 * o_rows),
        ),
        in_hbm(
            down, up, rank_down.T, rank_up.T, sketch_out,
            c_x.reshape(flat), c_m.reshape(flat_m), c_len, p_x.reshape(flat), p_m.reshape(flat_m), p_len,
        ),
        in_specs=[HBM] * 11,
        scratch=[
            pltpu.VMEM(down.shape, down.dtype),
            pltpu.VMEM(up.shape, up.dtype),
            pltpu.VMEM(rank_down.shape[::-1], rank_down.dtype),
            pltpu.VMEM(rank_up.shape[::-1], rank_up.dtype),
            pltpu.SMEM(c_len.shape, c_len.dtype),
            pltpu.SMEM(p_len.shape, p_len.dtype),
            pltpu.SemaphoreType.DMA((7 + 4 * examples,)),
        ],
    )

    f32 = jnp.float32
    here, there, both = (0,), (1,), (0, 1)
    own, second, own_sums, own_small = kernel(
        functools.partial(
            own_kernel, n, ks,
            ((0, 0, (0, 0, here), 1, 0, o_rows), (1, 0, (0, 0, here), 0, 0, s_rows)),
            ((0, o_rows, (0, 0, here)),),
        ),
        "own_products",
        (
            array(s_rows, kp),
            array(part + o_rows + t_rows, kp),
            array(2, 2, rows // 2, kp, dtype=f32),
            array(2, 2, rows // 2, ks, dtype=f32),
        ),
        (*in_hbm(sketch_in), extra, x, m),
        in_specs=[HBM] + [VMEM] * 3,
        scratch=[pltpu.SemaphoreType.DMA((2,))],
    )

    first, first_extra = along(sketch_in, False), along(extra, False)
    second = along(second, True)
    p_xo, c_xo = sw(p_cols, 1), sw(c_cols, 1)

    more = along(jnp.concatenate([first, first_extra]), True)
    rest = swap(first[:beside], 1, "dp", planes)
    second_other, rest_other = sw(second[: part + t_rows], 1), sw(rest, 1)

    o_at = part + t_rows
    early_places = (
        (0, 0, (0, 0, there), 1, 0, o_rows), (1, 0, (1, 0, both), 0, 0, s_rows), (2, 0, (1, 0, both), 1, 0, o_rows),
        (3, 0, (2, 0, here), 0, beside, part), (4, 0, (2, 1, here), 0, beside, part),
        (3, o_at, (2, 0, both), 1, 0, o_rows), (5, 0, (0, 0, there), 0, 0, s_rows),
    )
    early_tables = (
        (0, o_rows, (0, 0, there)), (2, o_rows, (1, 0, both)), (3, part, (2, 0, here)), (4, part, (2, 1, here)),
    )
    sums, small = kernel(
        functools.partial(early_kernel, n, ks, early_places, early_tables),
        "early_products",
        (array(2, 2, 2, rows // 2, kp, dtype=f32), array(2, 2, 2, rows // 2, ks, dtype=f32)),
        (x, m, c_xo, p_xo, own_sums, own_small, extra, first, first_extra, second, second_other, own),
    )
    late_places = (
        (0, 0, (3, 0, both), 0, 0, s_rows), (0, s_rows, (3, 0, both), 1, 0, o_rows),
        (1, 0, (2, 0, here), 0, 0, beside), (2, 0, (2, 1, here), 0, 0, beside),
    )

    def late(side, name):
        keep, keep_small, out = kernel(
            functools.partial(late_kernel, n, ks, side, late_places, ((0, s_rows + o_rows, (3, 0, both)),)),
            name,
            (array(rows, kp, dtype=f32), array(ks, rows, dtype=f32), array(rows + 2 * ks + 16, kp)),
            (x, m, (c_xo, p_xo)[side], live, sums, small, more, rest, rest_other),
            scratch=[pltpu.VMEM((2, rows, kp), f32), pltpu.VMEM((2, ks, rows), f32)],
        )
        return keep, keep_small, sw(out, 1)

    total = 2 * examples * ks
    side = array(2 * examples, ks * kp)

    def scratch(count):
        return [pltpu.VMEM((kp // 128, count + ks, 128), f32)]

    p_side = kernel(
        functools.partial(probe_kernel, seq), "probe_sides", side, (*late(1, "probe_products"), live), scratch=scratch(total)
    )
    grads = array(total // 2, kp, dtype=f32)
    c_side, c_grads, c_send = kernel(
        functools.partial(candidate_kernel, seq),
        "candidate_sides",
        (side, grads, grads),
        (*late(0, "candidate_products"), live),
        scratch=scratch(total),
    )
    c_feat = kernel(
        functools.partial(feature_kernel, ks),
        "candidate_features",
        array(examples, 2 * ks * kp),
        (c_grads, sw(c_send, 1)),
        scratch=scratch(total // 2),
    )

    across, second_side, first_side = sw(p_side, 6), along(p_side, True), along(p_side, False)
    part = array(3 * examples, n * examples, dtype=f32)
    shares = kernel(
        functools.partial(score_kernel, (0, 3)), "first_shares", (part, part), (c_side, p_side, across)
    )
    *shares, second_side, first_side = lax.optimization_barrier((*shares, second_side, first_side))
    scores, to_other = kernel(
        functools.partial(score_kernel, (2, 1)),
        "score_shares",
        (part, part),
        (c_side, second_side, first_side, *shares),
    )
    scores = kernel(
        functools.partial(final_kernel, 2 * ks * kp),
        "scores",
        array(examples, n * examples, dtype=f32),
        (scores, sw(to_other, 1)),
    )
    return scores, c_feat


def plain_features(x, m, lengths, down, up, sketch_in, sketch_out, rank_down, rank_up):
    examples, seq, model = x.shape
    ks, kp = rank_down.shape[1], sketch_in.shape[1]
    live = (lax.broadcasted_iota(jnp.int32, (examples, seq), 1) < lengths[:, None]).astype(m.dtype)
    masked = (m * live[:, :, None]).reshape(examples * seq, -1)
    rows = x.reshape(examples * seq, model)
    grad_rows = dot(masked, up).astype(jnp.bfloat16)
    outward = dot(masked, sketch_out).astype(jnp.bfloat16)
    down_round = dot(rows, down).astype(jnp.bfloat16)
    inward = dot(rows, sketch_in).astype(jnp.bfloat16)
    left_small = dot(grad_rows, rank_down).astype(jnp.bfloat16)
    right_small = dot(down_round, rank_up).astype(jnp.bfloat16)

    def outer(small, wide):
        return jnp.einsum(
            "esk,esp->ekp",
            small.reshape(examples, seq, ks),
            wide.reshape(examples, seq, kp),
            preferred_element_type=jnp.float32,
        )

    joined = jnp.concatenate([outer(left_small, inward), outer(right_small, outward)], axis=1)
    joined = joined.reshape(examples, 2 * ks * kp)
    scale = lax.rsqrt(jnp.mean(joined * joined, axis=1, keepdims=True) + eps_mean)
    return (joined * scale).astype(jnp.bfloat16)


def plain_body(c_x, c_m, c_len, p_x, p_m, p_len, down, up, sketch_in, sketch_out, rank_down, rank_up):
    weights = [
        lax.all_gather(w, "fsdp", axis=0, tiled=True) for w in (down, up, sketch_in, sketch_out)
    ]
    p_feat = plain_features(p_x, p_m, p_len, *weights, rank_down, rank_up)
    c_feat = plain_features(c_x, c_m, c_len, *weights, rank_down, rank_up)
    every = lax.all_gather(p_feat, "fsdp", axis=0, tiled=True)
    return dot(c_feat, every.T) / c_feat.shape[1], c_feat


def solution(mesh):
    n, planes = mesh.shape["fsdp"], mesh.shape["dp"]
    rows = P(("dp", "fsdp"), None)
    cube = P(("dp", "fsdp"), None, None)
    line = P(("dp", "fsdp"))
    shard = P("fsdp", None)
    in_specs = (cube, cube, line, cube, cube, line, shard, shard, shard, shard, P(), P())

    def body(*args):
        sketch_in, sketch_out = args[8:10]
        s_rows, (o_rows, kp) = sketch_in.shape[0], sketch_out.shape
        whole = s_rows % 256 == 0 and s_rows % kp == 0 and o_rows % 128 == 0 and o_rows <= kp and kp % 128 == 0
        if n == 1 << 3 and planes % 2 == 0 and whole:
            return fast_body(n, planes, *args)
        return plain_body(*args)

    return jax.shard_map(body, mesh=mesh, in_specs=in_specs, out_specs=(rows, rows), check_vma=False)
```
